32 devices in a mesh: species: 4 (over z), mode: 4 (over y, x), space: 2 (over core).
Axes of the slice: x: 2, y: 2, z: 4, core: 2. Of those that a mesh axis runs over, the one named last changes fastest.
Arguments:
- distribution: float32 [8, 1024, 2, 512], P('species', 'mode', 'space'), may hold values from -6 to 6
- kernel: bfloat16 [2, 120, 120, 120], P(None, 'mode'), may hold values from -0.046875 to 0.046875
- pair_kind: int32 [8, 8], replicated, may hold values from 0 to 1
- low_map: int32 [120], replicated, may hold values from 0 to 448, as said below
- thermal_speed: float32 [8], P('species'), may hold values from 0.5 to 1
- relax_rate: float32 [8], P('species'), may hold values from 2 to 8
Outputs:
- updated: float32 [8, 1024, 2, 512], P('species', 'mode', 'space')
The draws below stay inside these ranges and needn't reach their ends.
Inputs may be any that keep to these rules, and one draw needn't show every extreme that they name: low_map lists each of the 120 modes whose degrees a, b, c sum to at most 7 exactly once, in some order; a mode's index is a * 8 * 8 + b * 8 + c.
All inputs are finite; a program needn't handle non-finite values.
Results may differ from the reference program's by a relative error of at most 0.0025.
Values may be sent and summed in bfloat16 or wider, within the bound.
A program may use at most 128 MiB of HBM per device.

```python
import math
import jax
import jax.numpy as jnp
import numpy as np
from jax import lax

SPECIES = 8
NVX = 16
NVY = 8
NVZ = 8
MODES = 1024
DEG = 7
K = 120
NKIND = 2
NX = 2
NY = 256
NZ = 2
PLANE = 512


def draw_low_map(key, part):
    mode_table = np.array([degree_a * NVY * NVZ + degree_b * NVZ + degree_c for degree_a in range(DEG + 1) for degree_b in range(DEG + 1) for degree_c in range(DEG + 1) if degree_a + degree_b + degree_c <= DEG], dtype=np.int32)
    shuffled = jax.random.permutation(key, mode_table.shape[0])
    return jnp.asarray(mode_table)[shuffled].astype(jnp.int32)


def plant(drawn, stream_key, least, top_value):
    spot = [jax.random.randint(jax.random.fold_in(stream_key, axis), (), 0, length) for axis, length in enumerate(drawn.shape)]
    main_axis = drawn.shape.index(max(drawn.shape))
    beside = spot[:main_axis] + [(spot[main_axis] + 1) % drawn.shape[main_axis]] + spot[main_axis + 1:]
    return drawn.at[tuple(spot)].set(least).at[tuple(beside)].set(top_value)


def block_scale(own_key, dims, pieces, low, high):
    level, own = 1.0, jax.random.fold_in(own_key, 6)
    for position, blocks in pieces:
        draws = jnp.exp(jax.random.uniform(jax.random.fold_in(own, position), (blocks,), jnp.float32, low / len(pieces), high / len(pieces)))
        level = level * jnp.repeat(draws, dims[position] // blocks).reshape([-1 if axis == position else 1 for axis in range(len(dims))])
    return level


def centred(stream_key, extent, scale, reach, shards=(), kind=jnp.bfloat16):
    level = block_scale(stream_key, extent, shards, -0.22, 0.18) if shards else 1.0
    values = jax.random.normal(stream_key, extent, jnp.float32) * scale * level
    return jnp.minimum(jnp.maximum(values, -reach), reach).astype(kind)


def setup_inputs(seed: int = 0) -> dict:
    key_list = jax.random.split(jax.random.key(seed), 7)
    distribution = centred(key_list[0], (SPECIES, MODES, NX, PLANE), 1.0, 6.0, ((0, 4), (1, 4), (2, 2)), jnp.float32)
    kernel = centred(key_list[1], (NKIND, K, K, K), (K * K) ** -0.5, 0.046875, ((1, 4),))
    pair_kind = plant(jax.random.randint(key_list[2], (SPECIES, SPECIES), 0, NKIND), jax.random.fold_in(key_list[2], 1), 0, NKIND - 1).astype(jnp.int32)
    low_map = draw_low_map(jax.random.fold_in(key_list[6], 71), 0)
    thermal_speed = jnp.clip(jnp.exp(math.log(1.0) - 0.6931472 * jax.random.uniform(key_list[4], (SPECIES,), jnp.float32) ** block_scale(key_list[4], (SPECIES,), ((0, 4),), -0.2, 0.2)), 0.5, 1.0)
    relax_rate = jnp.clip(jnp.exp(math.log(8.0) - 1.3862944 * jax.random.uniform(key_list[5], (SPECIES,), jnp.float32) ** block_scale(key_list[5], (SPECIES,), ((0, 4),), -0.2, 0.2)), 2.0, 8.0)
    return {"distribution": distribution, "kernel": kernel, "pair_kind": pair_kind, "low_map": low_map, "thermal_speed": thermal_speed, "relax_rate": relax_rate}


nu_step = 0.0625
dt_step = 0.05
bound_x = 6.7
bound_y = 4.2
bound_z = 4.2

def flux_from_padded(padded, axis_dim, first_degree):
    axis_count = padded.shape[axis_dim] - 2
    dims_shape = [1] * padded.ndim
    dims_shape[axis_dim] = axis_count
    degree = (first_degree + jnp.arange(axis_count)).astype(jnp.float32).reshape(dims_shape)
    below_part = lax.slice_in_dim(padded, 0, axis_count, axis=axis_dim)
    above_part = lax.slice_in_dim(padded, 2, axis_count + 2, axis=axis_dim)
    return jnp.sqrt(degree + 1.0) * above_part + jnp.sqrt(degree) * below_part

def degree_flux(phase_field, axis_dim):
    widths = [(0, 0)] * phase_field.ndim
    widths[axis_dim] = (1, 1)
    return flux_from_padded(jnp.pad(phase_field, widths), axis_dim, 0)

def rusanov(phase_field, up_field, down_field, up_flux, down_flux, speed_bound):
    return 0.5 * (up_flux - down_flux) - 0.5 * speed_bound * (up_field - 2.0 * phase_field + down_field)

def periodic_term(phase_field, axis_deg, axis_cell, speed_bound):
    flux_dir = degree_flux(phase_field, axis_deg)
    return rusanov(phase_field, jnp.roll(phase_field, -1, axis_cell), jnp.roll(phase_field, 1, axis_cell), jnp.roll(flux_dir, -1, axis_cell), jnp.roll(flux_dir, 1, axis_cell), speed_bound)

def reference(distribution, kernel, pair_kind, low_map, thermal_speed, relax_rate):
    phase_field = distribution.reshape(SPECIES, NVX, NVY, NVZ, NX, NZ, NY)
    widths = [(0, 0)] * 7
    widths[4] = (1, 1)
    flux_x = degree_flux(phase_field, 1)
    wide_field = jnp.pad(phase_field, widths)
    wide_flux = jnp.pad(flux_x, widths)
    x_term = rusanov(phase_field, lax.slice_in_dim(wide_field, 2, NX + 2, axis=4), lax.slice_in_dim(wide_field, 0, NX, axis=4), lax.slice_in_dim(wide_flux, 2, NX + 2, axis=4), lax.slice_in_dim(wide_flux, 0, NX, axis=4), bound_x)
    y_term = periodic_term(phase_field, 2, 6, bound_y)
    z_term = periodic_term(phase_field, 3, 5, bound_z)
    stream = x_term + y_term + z_term
    advected = phase_field - nu_step * thermal_speed.reshape(SPECIES, 1, 1, 1, 1, 1, 1) * stream
    flat_dist = distribution.reshape(SPECIES, MODES, NX, PLANE)
    low_block = flat_dist[:, low_map].astype(jnp.bfloat16)
    kernel_f32 = kernel.astype(jnp.float32)
    chooser = jnp.stack([(pair_kind == kind_index).astype(jnp.float32) for kind_index in range(NKIND)])

    def row_collide(piece):
        values = piece.astype(jnp.float32)
        summed = jnp.zeros((SPECIES, K, PLANE), jnp.float32)
        for kind_index in range(NKIND):
            partner_sum = jnp.einsum('sr,rlc->slc', chooser[kind_index], values, precision=lax.Precision.HIGHEST)
            mixed_terms = jnp.einsum('nkl,skc->snlc', kernel_f32[kind_index], values, precision=lax.Precision.HIGHEST)
            summed = summed + jnp.einsum('snlc,slc->snc', mixed_terms, partner_sum, precision=lax.Precision.HIGHEST)
        return summed
    row_results = lax.map(row_collide, jnp.moveaxis(low_block, 2, 0))
    gained = jnp.moveaxis(row_results, 0, 2)
    collide = jnp.zeros((SPECIES, MODES, NX, PLANE), jnp.float32).at[:, low_map].set(gained)
    degree_total = (jnp.arange(NVX)[:, None, None] + jnp.arange(NVY)[None, :, None] + jnp.arange(NVZ)[None, None, :]).reshape(MODES)
    high_mask = (degree_total > DEG).astype(jnp.float32).reshape(1, MODES, 1, 1)
    collide = collide - high_mask * relax_rate.reshape(SPECIES, 1, 1, 1) * flat_dist
    return advected.reshape(SPECIES, MODES, NX, PLANE) + dt_step * collide
```

```python
import functools

import jax
import jax.numpy as jnp
import numpy as np
from jax import lax
from jax.experimental import pallas as pl
from jax.experimental.pallas import tpu as pltpu
from jax.sharding import PartitionSpec as P

MESH = pl.DeviceIdType.MESH
F32 = jnp.float32
BF16 = jnp.bfloat16

NVY = 8
NVZ = 8
DEG = 7
NKIND = 2
NY = 256

nu_step = 0.0625
dt_step = 0.05
bound_x = 6.7
bound_y = 4.2
bound_z = 4.2

SPLIT = 4
OWN = 2
ROWS = 256
PER_VX = 4
LANES = 128
HEAD = 208
PACK = 256
PIECE = 64
PAD_J = 128
PAD_N = 32


def packed_table():
    low = [
        (a * NVY + b) * NVZ + c
        for a in range(DEG + 1)
        for b in range(NVY)
        for c in range(NVZ)
        if a + b + c <= DEG
    ]
    table = np.full((PACK, 8), -1, np.int32)
    for start, first in ((0, 0), (HEAD, ROWS)):
        held = [mode for mode in low if first <= mode < first + ROWS]
        row = start
        for slot in range(OWN):
            for mode in held:
                table[row, 0] = slot * ROWS + mode - first
                table[row, 1 + slot] = mode
                row += 1
        assert row <= (HEAD if start == 0 else PACK)
    return table


def dot(left, right):
    return jnp.dot(left, right, preferred_element_type=F32)


def kernel(
    space_count,
    f_in,
    k_in,
    tab_ref,
    lm_ref,
    kind_ref,
    th_ref,
    rx_ref,
    out_ref,
    f_ref,
    kraw,
    k2,
    low_send,
    full,
    low,
    pmat,
    gsum,
    gsend,
    grecv,
    pick,
    spread,
    halo_send,
    halo_recv,
    ab_send,
    ab_recv,
    copy_sem,
    s1,
    r1,
    s2,
    r2,
    s3,
    r3,
    hs,
    hr,
    xs,
    xr,
):
    q = lax.axis_index("species")
    m = lax.axis_index("mode")
    sx = lax.axis_index("space")

    copy_f = pltpu.make_async_copy(f_in, f_ref, copy_sem.at[0])
    copy_k = pltpu.make_async_copy(k_in, kraw, copy_sem.at[1])
    copy_f.start()
    copy_k.start()

    barrier = pltpu.get_barrier_semaphore()
    for step in range(1, SPLIT * SPLIT):
        other = lax.rem(q * SPLIT + m + step, SPLIT * SPLIT)
        pl.semaphore_signal(
            barrier,
            inc=1,
            device_id={"species": other // SPLIT, "mode": lax.rem(other, SPLIT)},
            device_id_type=MESH,
        )

    @pl.when(sx > 0)
    def _():
        pl.semaphore_signal(barrier, inc=1, device_id={"space": sx - 1}, device_id_type=MESH)

    @pl.when(sx < space_count - 1)
    def _():
        pl.semaphore_signal(barrier, inc=1, device_id={"space": sx + 1}, device_id_type=MESH)

    copy_f.wait()

    def extract(first, count):
        rows = lax.broadcasted_iota(jnp.int32, (count, OWN * ROWS), 1)
        chosen = jnp.where(tab_ref[first : first + count, 0:1] == rows, 1.0, 0.0).astype(BF16)
        field = f_ref[...].reshape(OWN * ROWS, SPLIT * LANES).astype(BF16)
        packed = dot(chosen, field).astype(BF16)
        for part in range(SPLIT):
            low_send[part, first : first + count, :] = packed[:, part * LANES : (part + 1) * LANES]

    @pl.when(m == 0)
    def _():
        extract(0, HEAD)

    @pl.when(m == 1)
    def _():
        extract(HEAD, PACK - HEAD)

    for slot in range(OWN):
        halo_send[0, slot] = f_ref[slot, 0:64, :].astype(BF16)
        halo_send[1, slot] = f_ref[slot, ROWS - 64 : ROWS, :].astype(BF16)

    inner = (sx > 0) & (sx < space_count - 1)
    peers = SPLIT * SPLIT - 1

    @pl.when(inner)
    def _():
        pl.semaphore_wait(barrier, peers + 2)

    @pl.when(jnp.logical_not(inner))
    def _():
        pl.semaphore_wait(barrier, peers + min(1, space_count - 1))

    def scatter(part, piece, first, count, source):
        return pltpu.make_async_remote_copy(
            src_ref=low_send.at[part, pl.ds(first, count)],
            dst_ref=full.at[q, pl.ds(first, count)],
            send_sem=s1.at[part, piece],
            recv_sem=r1.at[q, source],
            device_id={"species": part, "mode": piece},
            device_id_type=MESH,
        )

    head_last = HEAD - 3 * PIECE

    def head_copies(step):
        part = lax.rem(q + step, SPLIT)
        found = []
        for piece in (3, 1, 2, 0):
            if step == 0 and piece == 0:
                continue
            count = PIECE if piece < 3 else head_last
            found.append(scatter(part, piece, piece * PIECE, count, 0))
        return found

    def tail_copies(step):
        return scatter(lax.rem(q + step, SPLIT), 3, HEAD, PACK - HEAD, 1)

    @pl.when(m == 0)
    def _():
        for step in (1, 2, 3, 0):
            for item in head_copies(step):
                item.start()
        full[q, 0:PIECE, :] = low_send[q, 0:PIECE, :]

    @pl.when(m == 1)
    def _():
        for step in (1, 2, 3, 0):
            tail_copies(step).start()

    def halo(way):
        return pltpu.make_async_remote_copy(
            src_ref=halo_send.at[way],
            dst_ref=halo_recv.at[1 - way],
            send_sem=hs.at[way],
            recv_sem=hr.at[1 - way],
            device_id={"mode": m - 1 if way == 0 else m + 1},
            device_id_type=MESH,
        )

    @pl.when(m >= 2)
    def _():
        halo(0).start()

    @pl.when(m == 2)
    def _():
        halo(1).start()

    copy_k.wait()

    def lay(n, carry):
        k2[n] = jnp.zeros((PAD_J, NKIND * PAD_J), BF16)

        @pl.when(n < kraw.shape[1])
        def _():
            spot = jnp.minimum(n, kraw.shape[1] - 1)
            for kind in range(NKIND):
                k2[n, 0 : kraw.shape[2], kind * PAD_J : kind * PAD_J + kraw.shape[3]] = kraw[
                    kind, spot
                ]

        return carry

    lax.fori_loop(0, PAD_N, lay, 0)

    for slot in range(OWN):
        same = tab_ref[:, 1 + slot : 2 + slot] == lm_ref[0:1, :]
        pick[slot] = jnp.where(same, 1.0, 0.0).T.astype(BF16)
    mode_of = lax.broadcasted_iota(jnp.int32, (ROWS, PAD_J), 0) + m * ROWS
    spread[...] = jnp.where(mode_of == lm_ref[1:2, :], 1.0, 0.0).astype(BF16)

    def piece_wait(source, count, sender):
        pltpu.make_async_remote_copy(
            src_ref=low_send.at[0, pl.ds(0, count)],
            dst_ref=full.at[source, pl.ds(0, count)],
            send_sem=s1.at[0, 0],
            recv_sem=r1.at[source, sender],
            device_id={"mode": lax.rem(m + 1, SPLIT)},
            device_id_type=MESH,
        ).wait_recv()

    def forward(source, step):
        rows = pl.ds(pl.multiple_of(m * PIECE, PIECE), PIECE)
        return pltpu.make_async_remote_copy(
            src_ref=full.at[source, rows],
            dst_ref=full.at[source, rows],
            send_sem=s2.at[source, step],
            recv_sem=r2.at[source, m],
            device_id={"mode": lax.rem(m + step, SPLIT)},
            device_id_type=MESH,
        )

    for back in range(SPLIT):
        source = lax.rem(q + SPLIT - back, SPLIT)

        if back > 0:

            @pl.when(m == 0)
            def _():
                piece_wait(source, PIECE, 0)

        @pl.when((m == 1) | (m == 2))
        def _():
            piece_wait(source, PIECE, 0)

        @pl.when(m == 3)
        def _():
            piece_wait(source, head_last, 0)
            piece_wait(source, PACK - HEAD, 1)

        for step in range(1, SPLIT):
            forward(source, step).start()

    @pl.when(m < 2)
    def _():
        halo(1).start()

    @pl.when(m == 1)
    def _():
        halo(0).start()

    degree_c = lax.broadcasted_iota(jnp.int32, (NVZ, 1), 0)
    sqrt_c = jnp.sqrt(degree_c.astype(F32))
    sqrt_c_up = jnp.where(degree_c == NVZ - 1, 0.0, jnp.sqrt(degree_c.astype(F32) + 1.0))
    planes = SPLIT * LANES // NY

    def own_terms(i, carry):
        slot = i // PER_VX
        a = lax.rem(i, PER_VX)
        scale = nu_step * th_ref[slot]
        relax = dt_step * rx_ref[slot]
        blocks = [
            f_ref[slot, pl.ds(pl.multiple_of(a * 64 + b * NVZ, NVZ), NVZ), :] for b in range(NVY)
        ]
        for b in range(NVY):
            here = blocks[b]
            flux_y = jnp.zeros_like(here)
            if b < NVY - 1:
                flux_y = flux_y + float(np.sqrt(np.float32(b + 1))) * blocks[b + 1]
            if b > 0:
                flux_y = flux_y + float(np.sqrt(np.float32(b))) * blocks[b - 1]
            up_y = 0.5 * flux_y - 0.5 * bound_y * here
            down_y = -0.5 * flux_y - 0.5 * bound_y * here
            turned = []
            for plane in range(planes):
                cut = slice(plane * NY, (plane + 1) * NY)
                turned.append(
                    pltpu.roll(up_y[:, cut], NY - 1, 1) + pltpu.roll(down_y[:, cut], 1, 1)
                )
            y_term = jnp.concatenate(turned, axis=1) + bound_y * here
            flux_z = sqrt_c_up * pltpu.roll(here, NVZ - 1, 0) + sqrt_c * pltpu.roll(here, 1, 0)
            wide = planes * NY
            up_z = 0.5 * flux_z - 0.5 * bound_z * here
            down_z = -0.5 * flux_z - 0.5 * bound_z * here
            z_term = (
                pltpu.roll(up_z, wide - NY, 1) + pltpu.roll(down_z, NY, 1) + bound_z * here
            )
            total = degree_c + (b + a + m * PER_VX)
            lost = jnp.where(total > DEG, relax, 0.0)
            out_ref[slot, pl.ds(pl.multiple_of(a * 64 + b * NVZ, NVZ), NVZ), :] = (
                here - scale * (y_term + z_term + bound_x * here) - lost * here
            )
        return carry

    lax.fori_loop(0, OWN * PER_VX, own_terms, 0)

    def x_parts(a):
        degree = (m * PER_VX + a).astype(F32)
        root = jnp.sqrt(jnp.full((8, 128), degree, F32))[0:1, 0:1]
        root_up = jnp.sqrt(jnp.full((8, 128), degree + 1.0, F32))[0:1, 0:1]

        def part(i, carry):
            slot = i // 4
            r = lax.rem(i, 4) * 16
            here = f_ref[slot, pl.ds(pl.multiple_of(a * 64 + r, 16), 16), :]
            if a < PER_VX - 1:
                above = f_ref[slot, pl.ds(pl.multiple_of((a + 1) * 64 + r, 16), 16), :]
            else:
                above = halo_recv[1, slot, pl.ds(pl.multiple_of(r, 16), 16), :].astype(F32)
            if a > 0:
                below = f_ref[slot, pl.ds(pl.multiple_of((a - 1) * 64 + r, 16), 16), :]
            else:
                below = halo_recv[0, slot, pl.ds(pl.multiple_of(r, 16), 16), :].astype(F32)
            flux = root_up * above + root * below
            rows = pl.ds(pl.multiple_of(slot * 64 + r, 16), 16)
            ab_send[0, a, rows, :] = (0.5 * flux - 0.5 * bound_x * here).astype(ab_send.dtype)
            ab_send[1, a, rows, :] = (-0.5 * flux - 0.5 * bound_x * here).astype(ab_send.dtype)
            return carry

        lax.fori_loop(0, OWN * 4, part, 0)

    def layer(way, a):
        return pltpu.make_async_remote_copy(
            src_ref=ab_send.at[way, a],
            dst_ref=ab_recv.at[way, a],
            send_sem=xs.at[way, a],
            recv_sem=xr.at[way, a],
            device_id={"space": sx - 1 if way == 0 else sx + 1},
            device_id_type=MESH,
        )

    def send_layers(a):
        @pl.when(sx > 0)
        def _():
            layer(0, a).start()

        @pl.when(sx < space_count - 1)
        def _():
            layer(1, a).start()

    @pl.when(sx == space_count - 1)
    def _():
        ab_recv[0] = jnp.zeros(ab_recv.shape[1:], ab_recv.dtype)

    @pl.when(sx == 0)
    def _():
        ab_recv[1] = jnp.zeros(ab_recv.shape[1:], ab_recv.dtype)

    for a in (1, 2):
        x_parts(a)
        send_layers(a)

    def forward_wait(source, step):
        sender = lax.rem(m + step, SPLIT)
        pltpu.make_async_remote_copy(
            src_ref=full.at[source, pl.ds(0, PIECE)],
            dst_ref=full.at[source, pl.ds(0, PIECE)],
            send_sem=s2.at[source, step],
            recv_sem=r2.at[source, sender],
            device_id={"mode": sender},
            device_id_type=MESH,
        ).wait_recv()

    for back in range(SPLIT):
        source = lax.rem(q + SPLIT - back, SPLIT)
        for step in range(1, SPLIT):
            forward_wait(source, step)
        packed = full[source]
        for slot in range(OWN):
            low[source, :, slot * LANES : (slot + 1) * LANES] = dot(pick[slot], packed)

    def partners(pair, carry):
        for slot in range(OWN):
            sums = [jnp.zeros((PAD_J, LANES), F32) for _ in range(NKIND)]
            for r in range(SPLIT * OWN):
                values = low[r // OWN, :, (r % OWN) * LANES : (r % OWN + 1) * LANES]
                kind_here = kind_ref[pair * OWN + slot, r]
                for kind in range(NKIND):
                    sums[kind] = sums[kind] + jnp.where(kind_here == kind, 1.0, 0.0) * values
            for kind in range(NKIND):
                pmat[
                    pair,
                    kind * PAD_J : (kind + 1) * PAD_J,
                    slot * LANES : (slot + 1) * LANES,
                ] = sums[kind].astype(BF16)
        return carry

    lax.fori_loop(0, SPLIT, partners, 0)

    def give(pair, target):
        return pltpu.make_async_remote_copy(
            src_ref=gsend.at[pair],
            dst_ref=grecv.at[q, pl.ds(pl.multiple_of(m * PAD_N, PAD_N), PAD_N)],
            send_sem=s3.at[pair, target],
            recv_sem=r3.at[q, m],
            device_id={"species": pair, "mode": target},
            device_id_type=MESH,
        )

    group = 8

    def collide(pair):
        def some(i, carry):
            left = k2[pl.ds(pl.multiple_of(i * group, group), group)]
            product = dot(left.reshape(group * PAD_J, NKIND * PAD_J), pmat[pair])
            own = low[pair]
            gsum[pl.ds(pl.multiple_of(i * group, group), group), :] = jnp.sum(
                product.reshape(group, PAD_J, OWN * LANES) * own[None], axis=1
            )
            return carry

        lax.fori_loop(0, PAD_N // group, some, 0)
        gsend[pair] = gsum[...].astype(BF16)

    for step in (1, 2, 3, 0):
        pair = lax.rem(q + step, SPLIT)
        collide(pair)
        for target in range(2):
            if step > 0:
                give(pair, target).start()
            else:

                @pl.when(m != target)
                def _():
                    give(pair, target).start()

                @pl.when(m == target)
                def _():
                    grecv[q, target * PAD_N : (target + 1) * PAD_N, :] = gsend[pair]

    @pl.when(m > 0)
    def _():
        halo(1).wait_recv()

    @pl.when(m == 0)
    def _():
        halo_recv[0] = jnp.zeros(halo_recv.shape[1:], BF16)

    @pl.when(m < SPLIT - 1)
    def _():
        halo(0).wait_recv()

    @pl.when(m == SPLIT - 1)
    def _():
        halo_recv[1] = jnp.zeros(halo_recv.shape[1:], BF16)

    for a in (0, 3):
        x_parts(a)
        send_layers(a)

    for a in (1, 2, 0, 3):

        @pl.when(sx < space_count - 1)
        def _():
            layer(0, a).wait_recv()

        @pl.when(sx > 0)
        def _():
            layer(1, a).wait_recv()

        def add_x(i, carry):
            slot = i // 4
            r = lax.rem(i, 4) * 16
            rows = pl.ds(pl.multiple_of(slot * 64 + r, 16), 16)
            here = pl.ds(pl.multiple_of(a * 64 + r, 16), 16)
            term = ab_recv[0, a, rows, :].astype(F32) + ab_recv[1, a, rows, :].astype(F32)
            out_ref[slot, here, :] = out_ref[slot, here, :] - (nu_step * th_ref[slot]) * term
            return carry

        lax.fori_loop(0, OWN * 4, add_x, 0)

    @pl.when(m < 2)
    def _():
        for back in range(SPLIT):
            source = lax.rem(q + SPLIT - back, SPLIT)
            for sender in range(SPLIT):

                def take():
                    pltpu.make_async_remote_copy(
                        src_ref=gsend.at[0],
                        dst_ref=grecv.at[source, pl.ds(sender * PAD_N, PAD_N)],
                        send_sem=s3.at[0, 0],
                        recv_sem=r3.at[source, sender],
                        device_id={"mode": lax.rem(m + 1, SPLIT)},
                        device_id_type=MESH,
                    ).wait_recv()

                if back > 0 or sender > 1:
                    take()
                else:
                    pl.when(m != sender)(take)
            columns = pl.ds(pl.multiple_of(source * LANES, LANES), LANES)
            for slot in range(OWN):
                gained = dot(spread[...], grecv[source, :, slot * LANES : (slot + 1) * LANES])
                out_ref[slot, :, columns] = out_ref[slot, :, columns] + dt_step * gained

    @pl.when(m == 0)
    def _():
        for step in range(SPLIT):
            for item in head_copies(step):
                item.wait_send()

    @pl.when(m == 1)
    def _():
        for step in range(SPLIT):
            tail_copies(step).wait_send()

    for back in range(SPLIT):
        for step in range(1, SPLIT):
            forward(lax.rem(q + SPLIT - back, SPLIT), step).wait_send()

    @pl.when(m > 0)
    def _():
        halo(0).wait_send()

    @pl.when(m < SPLIT - 1)
    def _():
        halo(1).wait_send()

    for a in range(PER_VX):

        @pl.when(sx > 0)
        def _():
            layer(0, a).wait_send()

        @pl.when(sx < space_count - 1)
        def _():
            layer(1, a).wait_send()

    for step in range(SPLIT):
        pair = lax.rem(q + step, SPLIT)
        for target in range(2):
            if step > 0:
                give(pair, target).wait_send()
            else:

                @pl.when(m != target)
                def _():
                    give(pair, target).wait_send()


def per_device(space_count, distribution, kernels, pair_kind, low_map, thermal_speed, relax_rate):
    own, rows, layers, cells = distribution.shape
    assert (own, rows, layers, cells) == (OWN, ROWS, 1, SPLIT * LANES)
    kinds, out_rows, low_count, _ = kernels.shape
    field = distribution.reshape(own, rows, cells)
    ordered = jnp.pad(low_map, (0, PAD_J - low_count), constant_values=-2)
    by_block = jnp.pad(
        low_map.reshape(SPLIT, out_rows), ((0, 0), (0, PAD_N - out_rows)), constant_values=-2
    ).reshape(PAD_J)
    maps = jnp.stack([ordered, by_block])
    table = jnp.asarray(packed_table())
    vmem = pl.BlockSpec(memory_space=pltpu.VMEM)
    smem = pl.BlockSpec(memory_space=pltpu.SMEM)
    anywhere = pl.BlockSpec(memory_space=pl.ANY)
    dma = pltpu.SemaphoreType.DMA
    ab_type = F32
    result = pl.pallas_call(
        functools.partial(kernel, space_count),
        out_shape=jax.ShapeDtypeStruct((own, rows, cells), F32),
        in_specs=[anywhere, anywhere, vmem, vmem, smem, smem, smem],
        out_specs=vmem,
        scratch_shapes=[
            pltpu.VMEM((own, rows, cells), F32),
            pltpu.VMEM(kernels.shape, BF16),
            pltpu.VMEM((PAD_N, PAD_J, kinds * PAD_J), BF16),
            pltpu.VMEM((SPLIT, PACK, LANES), BF16),
            pltpu.VMEM((SPLIT, PACK, LANES), BF16),
            pltpu.VMEM((SPLIT, PAD_J, own * LANES), F32),
            pltpu.VMEM((SPLIT, kinds * PAD_J, own * LANES), BF16),
            pltpu.VMEM((PAD_N, own * LANES), F32),
            pltpu.VMEM((SPLIT, PAD_N, own * LANES), BF16),
            pltpu.VMEM((SPLIT, SPLIT * PAD_N, own * LANES), BF16),
            pltpu.VMEM((own, PAD_J, PACK), BF16),
            pltpu.VMEM((ROWS, PAD_J), BF16),
            pltpu.VMEM((2, own, 64, cells), BF16),
            pltpu.VMEM((2, own, 64, cells), BF16),
            pltpu.VMEM((2, PER_VX, own * 64, cells), ab_type),
            pltpu.VMEM((2, PER_VX, own * 64, cells), ab_type),
            dma((2,)),
            dma((SPLIT, SPLIT)),
            dma((SPLIT, 2)),
            dma((SPLIT, SPLIT)),
            dma((SPLIT, SPLIT)),
            dma((SPLIT, 2)),
            dma((SPLIT, SPLIT)),
            dma((2,)),
            dma((2,)),
            dma((2, PER_VX)),
            dma((2, PER_VX)),
        ],
        compiler_params=pltpu.CompilerParams(
            collective_id=0, has_side_effects=True, vmem_limit_bytes=48 * 1024 * 1024
        ),
    )(field, kernels, table, maps, pair_kind, thermal_speed, relax_rate)
    return result.reshape(own, rows, layers, cells)


def solution(mesh):
    in_specs = (
        P("species", "mode", "space", None),
        P(None, "mode", None, None),
        P(),
        P(),
        P("species"),
        P("species"),
    )
    out_specs = P("species", "mode", "space", None)
    return jax.shard_map(
        functools.partial(per_device, mesh.shape["space"]),
        mesh=mesh,
        in_specs=in_specs,
        out_specs=out_specs,
        check_vma=False,
    )
```

```python
import functools

import jax
import jax.numpy as jnp
import numpy as np
from jax import lax
from jax.experimental import pallas as pl
from jax.experimental.pallas import tpu as pltpu
from jax.sharding import PartitionSpec as P

MESH = pl.DeviceIdType.MESH
F32 = jnp.float32
BF16 = jnp.bfloat16

NVY = 8
NVZ = 8
DEG = 7
NKIND = 2
NY = 256

nu_step = 0.0625
dt_step = 0.05
bound_x = 6.7
bound_y = 4.2
bound_z = 4.2

SPLIT = 4
OWN = 2
ROWS = 256
PER_VX = 4
LANES = 128
HEAD = 208
PACK = 256
PIECE = 64
PAD_J = 128
PAD_N = 32


def packed_table():
    low = [
        (a * NVY + b) * NVZ + c
        for a in range(DEG + 1)
        for b in range(NVY)
        for c in range(NVZ)
        if a + b + c <= DEG
    ]
    table = np.full((PACK, 8), -1, np.int32)
    for start, first in ((0, 0), (HEAD, ROWS)):
        held = [mode for mode in low if first <= mode < first + ROWS]
        row = start
        for slot in range(OWN):
            for mode in held:
                table[row, 0] = slot * ROWS + mode - first
                table[row, 1 + slot] = mode
                row += 1
        assert row <= (HEAD if start == 0 else PACK)
    return table


def dot(left, right):
    return jnp.dot(left, right, preferred_element_type=F32)


def kernel(
    space_count,
    f_in,
    k_in,
    tab_in,
    map_in,
    kind_in,
    th_in,
    rx_in,
    result,
    f_ref,
    out_ref,
    tab_ref,
    lm_ref,
    kind_ref,
    th_ref,
    rx_ref,
    kraw,
    k2,
    low_send,
    full,
    low,
    pmat,
    gsum,
    gsend,
    grecv,
    pick,
    spread,
    halo_send,
    halo_recv,
    ab_send,
    ab_recv,
    copy_sem,
    small_sem,
    s1,
    r1,
    s2,
    r2,
    s3,
    r3,
    hs,
    hr,
    xs,
    xr,
):
    q = lax.axis_index("species")
    m = lax.axis_index("mode")
    sx = lax.axis_index("space")

    barrier = pltpu.get_barrier_semaphore()
    for step in range(1, SPLIT * SPLIT):
        other = lax.rem(q * SPLIT + m + step, SPLIT * SPLIT)
        pl.semaphore_signal(
            barrier,
            inc=1,
            device_id={"species": other // SPLIT, "mode": lax.rem(other, SPLIT)},
            device_id_type=MESH,
        )

    @pl.when(sx > 0)
    def _():
        pl.semaphore_signal(barrier, inc=1, device_id={"space": sx - 1}, device_id_type=MESH)

    @pl.when(sx < space_count - 1)
    def _():
        pl.semaphore_signal(barrier, inc=1, device_id={"space": sx + 1}, device_id_type=MESH)

    columns_in = [
        pltpu.make_async_copy(
            f_in.at[slot, :, 0, pl.ds(part * LANES, LANES)],
            f_ref.at[part, slot],
            copy_sem.at[part, slot],
        )
        for part in range(SPLIT)
        for slot in range(OWN)
    ]
    small = [
        pltpu.make_async_copy(tab_in, tab_ref, small_sem.at[0]),
        pltpu.make_async_copy(map_in, lm_ref, small_sem.at[1]),
        pltpu.make_async_copy(kind_in, kind_ref, small_sem.at[2]),
        pltpu.make_async_copy(th_in, th_ref, small_sem.at[3]),
        pltpu.make_async_copy(rx_in, rx_ref, small_sem.at[4]),
    ]
    copy_k = pltpu.make_async_copy(k_in, kraw, small_sem.at[5])
    for item in columns_in + small + [copy_k]:
        item.start()
    for item in small + columns_in:
        item.wait()

    def load(slot, rows):
        return jnp.concatenate([f_ref[part, slot, rows, :] for part in range(SPLIT)], axis=1)

    def extract(first, count):
        rows = lax.broadcasted_iota(jnp.int32, (count, OWN * ROWS), 1)
        chosen = jnp.where(tab_ref[first : first + count, 0:1] == rows, 1.0, 0.0).astype(BF16)
        for part in range(SPLIT):
            field = f_ref[part].reshape(OWN * ROWS, LANES).astype(BF16)
            low_send[part, first : first + count, :] = dot(chosen, field).astype(BF16)

    @pl.when(m == 0)
    def _():
        extract(0, HEAD)

    @pl.when(m == 1)
    def _():
        extract(HEAD, PACK - HEAD)

    for slot in range(OWN):
        halo_send[0, slot] = load(slot, slice(0, 64)).astype(BF16)
        halo_send[1, slot] = load(slot, slice(ROWS - 64, ROWS)).astype(BF16)

    inner = (sx > 0) & (sx < space_count - 1)
    peers = SPLIT * SPLIT - 1

    @pl.when(inner)
    def _():
        pl.semaphore_wait(barrier, peers + 2)

    @pl.when(jnp.logical_not(inner))
    def _():
        pl.semaphore_wait(barrier, peers + min(1, space_count - 1))

    def scatter(part, piece, first, count, source):
        return pltpu.make_async_remote_copy(
            src_ref=low_send.at[part, pl.ds(first, count)],
            dst_ref=full.at[q, pl.ds(first, count)],
            send_sem=s1.at[part, piece],
            recv_sem=r1.at[q, source],
            device_id={"species": part, "mode": piece},
            device_id_type=MESH,
        )

    head_last = HEAD - 3 * PIECE

    def head_copies(step):
        part = lax.rem(q + step, SPLIT)
        found = []
        for piece in (3, 1, 2, 0):
            if step == 0 and piece == 0:
                continue
            count = PIECE if piece < 3 else head_last
            found.append(scatter(part, piece, piece * PIECE, count, 0))
        return found

    def tail_copies(step):
        return scatter(lax.rem(q + step, SPLIT), 3, HEAD, PACK - HEAD, 1)

    @pl.when(m == 0)
    def _():
        for step in (1, 2, 3, 0):
            for item in head_copies(step):
                item.start()
        full[q, 0:PIECE, :] = low_send[q, 0:PIECE, :]

    @pl.when(m == 1)
    def _():
        for step in (1, 2, 3, 0):
            tail_copies(step).start()

    def halo(way):
        return pltpu.make_async_remote_copy(
            src_ref=halo_send.at[way],
            dst_ref=halo_recv.at[1 - way],
            send_sem=hs.at[way],
            recv_sem=hr.at[1 - way],
            device_id={"mode": m - 1 if way == 0 else m + 1},
            device_id_type=MESH,
        )

    @pl.when(m >= 2)
    def _():
        halo(0).start()

    @pl.when(m == 2)
    def _():
        halo(1).start()

    copy_k.wait()

    def lay(n, carry):
        k2[n] = jnp.zeros((PAD_J, NKIND * PAD_J), BF16)

        @pl.when(n < kraw.shape[1])
        def _():
            spot = jnp.minimum(n, kraw.shape[1] - 1)
            for kind in range(NKIND):
                k2[n, 0 : kraw.shape[2], kind * PAD_J : kind * PAD_J + kraw.shape[3]] = kraw[
                    kind, spot
                ]

        return carry

    lax.fori_loop(0, PAD_N, lay, 0)

    lanes = lax.broadcasted_iota(jnp.int32, (8, PAD_J), 1)
    low_count = kraw.shape[2]
    block_rows = kraw.shape[1]
    ordered = jnp.concatenate(
        [lm_ref[...], jnp.full((1, PAD_J - low_count), -2, jnp.int32)], axis=1
    )
    ordered = jnp.broadcast_to(ordered, (8, PAD_J))
    by_block = jnp.full((8, PAD_J), -2, jnp.int32)
    for block in range(SPLIT):
        moved = ordered
        if block > 0:
            moved = pltpu.roll(ordered, block * (PAD_N - block_rows), 1)
        inside = (lanes >= block * PAD_N) & (lanes < block * PAD_N + block_rows)
        by_block = jnp.where(inside, moved, by_block)
    for slot in range(OWN):
        same = tab_ref[:, 1 + slot : 2 + slot] == ordered[0:1, :]
        pick[slot] = jnp.where(same, 1.0, 0.0).T.astype(BF16)
    mode_of = lax.broadcasted_iota(jnp.int32, (ROWS, PAD_J), 0) + m * ROWS
    spread[...] = jnp.where(mode_of == by_block[0:1, :], 1.0, 0.0).astype(BF16)

    def piece_wait(source, count, sender):
        pltpu.make_async_remote_copy(
            src_ref=low_send.at[0, pl.ds(0, count)],
            dst_ref=full.at[source, pl.ds(0, count)],
            send_sem=s1.at[0, 0],
            recv_sem=r1.at[source, sender],
            device_id={"mode": lax.rem(m + 1, SPLIT)},
            device_id_type=MESH,
        ).wait_recv()

    def forward(source, step):
        rows = pl.ds(pl.multiple_of(m * PIECE, PIECE), PIECE)
        return pltpu.make_async_remote_copy(
            src_ref=full.at[source, rows],
            dst_ref=full.at[source, rows],
            send_sem=s2.at[source, step],
            recv_sem=r2.at[source, m],
            device_id={"mode": lax.rem(m + step, SPLIT)},
            device_id_type=MESH,
        )

    for back in range(SPLIT):
        source = lax.rem(q + SPLIT - back, SPLIT)

        if back > 0:

            @pl.when(m == 0)
            def _():
                piece_wait(source, PIECE, 0)

        @pl.when((m == 1) | (m == 2))
        def _():
            piece_wait(source, PIECE, 0)

        @pl.when(m == 3)
        def _():
            piece_wait(source, head_last, 0)
            piece_wait(source, PACK - HEAD, 1)

        for step in range(1, SPLIT):
            forward(source, step).start()

    @pl.when(m < 2)
    def _():
        halo(1).start()

    @pl.when(m == 1)
    def _():
        halo(0).start()

    degree_c = lax.broadcasted_iota(jnp.int32, (NVZ, 1), 0)
    sqrt_c = jnp.sqrt(degree_c.astype(F32))
    sqrt_c_up = jnp.where(degree_c == NVZ - 1, 0.0, jnp.sqrt(degree_c.astype(F32) + 1.0))
    planes = SPLIT * LANES // NY

    def own_terms(i, carry):
        slot = i // PER_VX
        a = lax.rem(i, PER_VX)
        scale = nu_step * th_ref[slot]
        relax = dt_step * rx_ref[slot]
        blocks = [
            load(slot, pl.ds(pl.multiple_of(a * 64 + b * NVZ, NVZ), NVZ)) for b in range(NVY)
        ]
        for b in range(NVY):
            here = blocks[b]
            flux_y = jnp.zeros_like(here)
            if b < NVY - 1:
                flux_y = flux_y + float(np.sqrt(np.float32(b + 1))) * blocks[b + 1]
            if b > 0:
                flux_y = flux_y + float(np.sqrt(np.float32(b))) * blocks[b - 1]
            up_y = 0.5 * flux_y - 0.5 * bound_y * here
            down_y = -0.5 * flux_y - 0.5 * bound_y * here
            turned = []
            for plane in range(planes):
                cut = slice(plane * NY, (plane + 1) * NY)
                turned.append(
                    pltpu.roll(up_y[:, cut], NY - 1, 1) + pltpu.roll(down_y[:, cut], 1, 1)
                )
            y_term = jnp.concatenate(turned, axis=1) + bound_y * here
            flux_z = sqrt_c_up * pltpu.roll(here, NVZ - 1, 0) + sqrt_c * pltpu.roll(here, 1, 0)
            wide = planes * NY
            up_z = 0.5 * flux_z - 0.5 * bound_z * here
            down_z = -0.5 * flux_z - 0.5 * bound_z * here
            z_term = (
                pltpu.roll(up_z, wide - NY, 1) + pltpu.roll(down_z, NY, 1) + bound_z * here
            )
            total = degree_c + (b + a + m * PER_VX)
            lost = jnp.where(total > DEG, relax, 0.0)
            value = here - scale * (y_term + z_term + bound_x * here) - lost * here
            rows = pl.ds(pl.multiple_of(a * 64 + b * NVZ, NVZ), NVZ)
            for part in range(SPLIT):
                out_ref[part, slot, rows, :] = value[:, part * LANES : (part + 1) * LANES]
        return carry

    lax.fori_loop(0, OWN * PER_VX, own_terms, 0)

    def x_parts(a):
        degree = (m * PER_VX + a).astype(F32)
        root = jnp.sqrt(jnp.full((8, 128), degree, F32))[0:1, 0:1]
        root_up = jnp.sqrt(jnp.full((8, 128), degree + 1.0, F32))[0:1, 0:1]

        def part(i, carry):
            slot = i // 4
            r = lax.rem(i, 4) * 16
            here = load(slot, pl.ds(pl.multiple_of(a * 64 + r, 16), 16))
            if a < PER_VX - 1:
                above = load(slot, pl.ds(pl.multiple_of((a + 1) * 64 + r, 16), 16))
            else:
                above = halo_recv[1, slot, pl.ds(pl.multiple_of(r, 16), 16), :].astype(F32)
            if a > 0:
                below = load(slot, pl.ds(pl.multiple_of((a - 1) * 64 + r, 16), 16))
            else:
                below = halo_recv[0, slot, pl.ds(pl.multiple_of(r, 16), 16), :].astype(F32)
            flux = root_up * above + root * below
            rows = pl.ds(pl.multiple_of(slot * 64 + r, 16), 16)
            ab_send[0, a, rows, :] = (0.5 * flux - 0.5 * bound_x * here).astype(ab_send.dtype)
            ab_send[1, a, rows, :] = (-0.5 * flux - 0.5 * bound_x * here).astype(ab_send.dtype)
            return carry

        lax.fori_loop(0, OWN * 4, part, 0)

    def layer(way, a):
        return pltpu.make_async_remote_copy(
            src_ref=ab_send.at[way, a],
            dst_ref=ab_recv.at[way, a],
            send_sem=xs.at[way, a],
            recv_sem=xr.at[way, a],
            device_id={"space": sx - 1 if way == 0 else sx + 1},
            device_id_type=MESH,
        )

    def send_layers(a):
        @pl.when(sx > 0)
        def _():
            layer(0, a).start()

        @pl.when(sx < space_count - 1)
        def _():
            layer(1, a).start()

    @pl.when(sx == space_count - 1)
    def _():
        ab_recv[0] = jnp.zeros(ab_recv.shape[1:], ab_recv.dtype)

    @pl.when(sx == 0)
    def _():
        ab_recv[1] = jnp.zeros(ab_recv.shape[1:], ab_recv.dtype)

    for a in (1, 2):
        x_parts(a)
        send_layers(a)

    def forward_wait(source, step):
        sender = lax.rem(m + step, SPLIT)
        pltpu.make_async_remote_copy(
            src_ref=full.at[source, pl.ds(0, PIECE)],
            dst_ref=full.at[source, pl.ds(0, PIECE)],
            send_sem=s2.at[source, step],
            recv_sem=r2.at[source, sender],
            device_id={"mode": sender},
            device_id_type=MESH,
        ).wait_recv()

    for back in range(SPLIT):
        source = lax.rem(q + SPLIT - back, SPLIT)
        for step in range(1, SPLIT):
            forward_wait(source, step)
        packed = full[source]
        for slot in range(OWN):
            low[source, :, slot * LANES : (slot + 1) * LANES] = dot(pick[slot], packed)

    def partners(pair, carry):
        for slot in range(OWN):
            sums = [jnp.zeros((PAD_J, LANES), F32) for _ in range(NKIND)]
            for r in range(SPLIT * OWN):
                values = low[r // OWN, :, (r % OWN) * LANES : (r % OWN + 1) * LANES]
                kind_here = kind_ref[pair * OWN + slot, r]
                for kind in range(NKIND):
                    sums[kind] = sums[kind] + jnp.where(kind_here == kind, 1.0, 0.0) * values
            for kind in range(NKIND):
                pmat[
                    pair,
                    kind * PAD_J : (kind + 1) * PAD_J,
                    slot * LANES : (slot + 1) * LANES,
                ] = sums[kind].astype(BF16)
        return carry

    lax.fori_loop(0, SPLIT, partners, 0)

    def give(pair, target):
        return pltpu.make_async_remote_copy(
            src_ref=gsend.at[pair],
            dst_ref=grecv.at[q, pl.ds(pl.multiple_of(m * PAD_N, PAD_N), PAD_N)],
            send_sem=s3.at[pair, target],
            recv_sem=r3.at[q, m],
            device_id={"species": pair, "mode": target},
            device_id_type=MESH,
        )

    group = 8

    def collide(pair):
        def some(i, carry):
            left = k2[pl.ds(pl.multiple_of(i * group, group), group)]
            product = dot(left.reshape(group * PAD_J, NKIND * PAD_J), pmat[pair])
            own = low[pair]
            gsum[pl.ds(pl.multiple_of(i * group, group), group), :] = jnp.sum(
                product.reshape(group, PAD_J, OWN * LANES) * own[None], axis=1
            )
            return carry

        lax.fori_loop(0, PAD_N // group, some, 0)
        gsend[pair] = gsum[...].astype(BF16)

    for step in (1, 2, 3, 0):
        pair = lax.rem(q + step, SPLIT)
        collide(pair)
        for target in range(2):
            if step > 0:
                give(pair, target).start()
            else:

                @pl.when(m != target)
                def _():
                    give(pair, target).start()

                @pl.when(m == target)
                def _():
                    grecv[q, target * PAD_N : (target + 1) * PAD_N, :] = gsend[pair]

    @pl.when(m > 0)
    def _():
        halo(1).wait_recv()

    @pl.when(m == 0)
    def _():
        halo_recv[0] = jnp.zeros(halo_recv.shape[1:], BF16)

    @pl.when(m < SPLIT - 1)
    def _():
        halo(0).wait_recv()

    @pl.when(m == SPLIT - 1)
    def _():
        halo_recv[1] = jnp.zeros(halo_recv.shape[1:], BF16)

    for a in (0, 3):
        x_parts(a)
        send_layers(a)

    for a in (1, 2, 0, 3):

        @pl.when(sx < space_count - 1)
        def _():
            layer(0, a).wait_recv()

        @pl.when(sx > 0)
        def _():
            layer(1, a).wait_recv()

        def add_x(i, carry):
            slot = i // 4
            r = lax.rem(i, 4) * 16
            rows = pl.ds(pl.multiple_of(slot * 64 + r, 16), 16)
            here = pl.ds(pl.multiple_of(a * 64 + r, 16), 16)
            term = ab_recv[0, a, rows, :].astype(F32) + ab_recv[1, a, rows, :].astype(F32)
            term = (nu_step * th_ref[slot]) * term
            for part in range(SPLIT):
                out_ref[part, slot, here, :] = (
                    out_ref[part, slot, here, :] - term[:, part * LANES : (part + 1) * LANES]
                )
            return carry

        lax.fori_loop(0, OWN * 4, add_x, 0)

    def column_out(part, slot):
        return pltpu.make_async_copy(
            out_ref.at[part, slot],
            result.at[slot, :, 0, pl.ds(pl.multiple_of(part * LANES, LANES), LANES)],
            copy_sem.at[part, slot],
        )

    @pl.when(m >= 2)
    def _():
        for part in range(SPLIT):
            for slot in range(OWN):
                column_out(part, slot).start()

    @pl.when(m < 2)
    def _():
        for back in range(SPLIT):
            source = lax.rem(q + SPLIT - back, SPLIT)
            for sender in range(SPLIT):

                def take():
                    pltpu.make_async_remote_copy(
                        src_ref=gsend.at[0],
                        dst_ref=grecv.at[source, pl.ds(sender * PAD_N, PAD_N)],
                        send_sem=s3.at[0, 0],
                        recv_sem=r3.at[source, sender],
                        device_id={"mode": lax.rem(m + 1, SPLIT)},
                        device_id_type=MESH,
                    ).wait_recv()

                if back > 0 or sender > 1:
                    take()
                else:
                    pl.when(m != sender)(take)
            for slot in range(OWN):
                gained = dot(spread[...], grecv[source, :, slot * LANES : (slot + 1) * LANES])
                out_ref[source, slot] = out_ref[source, slot] + dt_step * gained
                column_out(source, slot).start()

    @pl.when(m == 0)
    def _():
        for step in range(SPLIT):
            for item in head_copies(step):
                item.wait_send()

    @pl.when(m == 1)
    def _():
        for step in range(SPLIT):
            tail_copies(step).wait_send()

    for back in range(SPLIT):
        for step in range(1, SPLIT):
            forward(lax.rem(q + SPLIT - back, SPLIT), step).wait_send()

    @pl.when(m > 0)
    def _():
        halo(0).wait_send()

    @pl.when(m < SPLIT - 1)
    def _():
        halo(1).wait_send()

    for a in range(PER_VX):

        @pl.when(sx > 0)
        def _():
            layer(0, a).wait_send()

        @pl.when(sx < space_count - 1)
        def _():
            layer(1, a).wait_send()

    for step in range(SPLIT):
        pair = lax.rem(q + step, SPLIT)
        for target in range(2):
            if step > 0:
                give(pair, target).wait_send()
            else:

                @pl.when(m != target)
                def _():
                    give(pair, target).wait_send()

    for part in range(SPLIT):
        for slot in range(OWN):
            column_out(part, slot).wait()


def per_device(space_count, distribution, kernels, pair_kind, low_map, thermal_speed, relax_rate):
    own, rows, layers, cells = distribution.shape
    assert (own, rows, layers, cells) == (OWN, ROWS, 1, SPLIT * LANES)
    kinds, _, low_count, _ = kernels.shape
    table = jnp.asarray(packed_table())
    anywhere = pl.BlockSpec(memory_space=pl.ANY)
    dma = pltpu.SemaphoreType.DMA
    ab_type = F32
    result = pl.pallas_call(
        functools.partial(kernel, space_count),
        out_shape=jax.ShapeDtypeStruct(distribution.shape, F32),
        in_specs=[anywhere] * 7,
        out_specs=anywhere,
        scratch_shapes=[
            pltpu.VMEM((SPLIT, own, rows, LANES), F32),
            pltpu.VMEM((SPLIT, own, rows, LANES), F32),
            pltpu.VMEM(table.shape, jnp.int32),
            pltpu.VMEM((1, low_count), jnp.int32),
            pltpu.SMEM(pair_kind.shape, jnp.int32),
            pltpu.SMEM(thermal_speed.shape, F32),
            pltpu.SMEM(relax_rate.shape, F32),
            pltpu.VMEM(kernels.shape, BF16),
            pltpu.VMEM((PAD_N, PAD_J, kinds * PAD_J), BF16),
            pltpu.VMEM((SPLIT, PACK, LANES), BF16),
            pltpu.VMEM((SPLIT, PACK, LANES), BF16),
            pltpu.VMEM((SPLIT, PAD_J, own * LANES), F32),
            pltpu.VMEM((SPLIT, kinds * PAD_J, own * LANES), BF16),
            pltpu.VMEM((PAD_N, own * LANES), F32),
            pltpu.VMEM((SPLIT, PAD_N, own * LANES), BF16),
            pltpu.VMEM((SPLIT, SPLIT * PAD_N, own * LANES), BF16),
            pltpu.VMEM((own, PAD_J, PACK), BF16),
            pltpu.VMEM((ROWS, PAD_J), BF16),
            pltpu.VMEM((2, own, 64, cells), BF16),
            pltpu.VMEM((2, own, 64, cells), BF16),
            pltpu.VMEM((2, PER_VX, own * 64, cells), ab_type),
            pltpu.VMEM((2, PER_VX, own * 64, cells), ab_type),
            dma((SPLIT, OWN)),
            dma((6,)),
            dma((SPLIT, SPLIT)),
            dma((SPLIT, 2)),
            dma((SPLIT, SPLIT)),
            dma((SPLIT, SPLIT)),
            dma((SPLIT, 2)),
            dma((SPLIT, SPLIT)),
            dma((2,)),
            dma((2,)),
            dma((2, PER_VX)),
            dma((2, PER_VX)),
        ],
        compiler_params=pltpu.CompilerParams(
            collective_id=0, has_side_effects=True, vmem_limit_bytes=60 * 1024 * 1024
        ),
    )(
        distribution,
        kernels,
        table,
        low_map.reshape(1, low_count),
        pair_kind,
        thermal_speed,
        relax_rate,
    )
    return result


def solution(mesh):
    in_specs = (
        P("species", "mode", "space", None),
        P(None, "mode", None, None),
        P(),
        P(),
        P("species"),
        P("species"),
    )
    out_specs = P("species", "mode", "space", None)
    return jax.shard_map(
        functools.partial(per_device, mesh.shape["space"]),
        mesh=mesh,
        in_specs=in_specs,
        out_specs=out_specs,
        check_vma=False,
    )
```

```python
import functools

import jax
import jax.numpy as jnp
import numpy as np
from jax import lax
from jax.experimental import pallas as pl
from jax.experimental.pallas import tpu as pltpu
from jax.sharding import PartitionSpec as P

MESH = pl.DeviceIdType.MESH
F32 = jnp.float32
BF16 = jnp.bfloat16

NVY = 8
NVZ = 8
DEG = 7
NKIND = 2
NY = 256

nu_step = 0.0625
dt_step = 0.05
bound_x = 6.7
bound_y = 4.2
bound_z = 4.2

SPLIT = 4
OWN = 2
ROWS = 256
PER_VX = 4
LANES = 128
HEAD = 208
PACK = 256
PIECE = 64
PAD_J = 128
PAD_N = 32


def packed_table():
    low = [
        (a * NVY + b) * NVZ + c
        for a in range(DEG + 1)
        for b in range(NVY)
        for c in range(NVZ)
        if a + b + c <= DEG
    ]
    table = np.full((PACK, 8), -1, np.int32)
    for start, first in ((0, 0), (HEAD, ROWS)):
        held = [mode for mode in low if first <= mode < first + ROWS]
        row = start
        for slot in range(OWN):
            for mode in held:
                table[row, 0] = slot * ROWS + mode - first
                table[row, 1 + slot] = mode
                row += 1
        assert row <= (HEAD if start == 0 else PACK)
    return table


def dot(left, right):
    return jnp.dot(left, right, preferred_element_type=F32)


def kernel(
    space_count,
    f_in,
    k_in,
    tab_in,
    map_in,
    kind_in,
    th_in,
    rx_in,
    result,
    f_ref,
    out_ref,
    tab_ref,
    lm_ref,
    kind_ref,
    th_ref,
    rx_ref,
    kraw,
    k2,
    low_send,
    full,
    low,
    pmat,
    gsum,
    total,
    gsend,
    grecv,
    pick,
    spread,
    halo_send,
    halo_recv,
    ab_send,
    ab_recv,
    copy_sem,
    small_sem,
    s1,
    r1,
    s2,
    r2,
    s3,
    r3,
    hs,
    hr,
    xs,
    xr,
):
    q = lax.axis_index("species")
    m = lax.axis_index("mode")
    sx = lax.axis_index("space")

    columns_in = [
        pltpu.make_async_copy(
            f_in.at[slot, :, 0, pl.ds(part * LANES, LANES)],
            f_ref.at[part, slot],
            copy_sem.at[part, slot],
        )
        for part in range(SPLIT)
        for slot in range(OWN)
    ]
    small = [
        pltpu.make_async_copy(tab_in, tab_ref, small_sem.at[0]),
        pltpu.make_async_copy(map_in, lm_ref, small_sem.at[1]),
        pltpu.make_async_copy(kind_in, kind_ref, small_sem.at[2]),
        pltpu.make_async_copy(th_in, th_ref, small_sem.at[3]),
        pltpu.make_async_copy(rx_in, rx_ref, small_sem.at[4]),
    ]
    copy_k = pltpu.make_async_copy(k_in, kraw, small_sem.at[5])
    for item in columns_in + small[:1]:
        item.start()

    barrier = pltpu.get_barrier_semaphore()
    for step in range(1, SPLIT * SPLIT):
        other = lax.rem(q * SPLIT + m + step, SPLIT * SPLIT)
        pl.semaphore_signal(
            barrier,
            inc=1,
            device_id={"species": other // SPLIT, "mode": lax.rem(other, SPLIT)},
            device_id_type=MESH,
        )

    @pl.when(sx > 0)
    def _():
        pl.semaphore_signal(barrier, inc=1, device_id={"space": sx - 1}, device_id_type=MESH)

    @pl.when(sx < space_count - 1)
    def _():
        pl.semaphore_signal(barrier, inc=1, device_id={"space": sx + 1}, device_id_type=MESH)

    for item in small[1:] + [copy_k]:
        item.start()
    for item in columns_in + small[:1]:
        item.wait()

    def load(slot, rows):
        return jnp.concatenate([f_ref[part, slot, rows, :] for part in range(SPLIT)], axis=1)

    def extract(first, count):
        rows = lax.broadcasted_iota(jnp.int32, (count, OWN * ROWS), 1)
        chosen = jnp.where(tab_ref[first : first + count, 0:1] == rows, 1.0, 0.0).astype(BF16)
        for part in range(SPLIT):
            field = f_ref[part].reshape(OWN * ROWS, LANES).astype(BF16)
            low_send[part, first : first + count, :] = dot(chosen, field).astype(BF16)

    @pl.when(m == 0)
    def _():
        extract(0, HEAD)

    @pl.when(m == 1)
    def _():
        extract(HEAD, PACK - HEAD)

    inner = (sx > 0) & (sx < space_count - 1)
    peers = SPLIT * SPLIT - 1

    @pl.when(inner)
    def _():
        pl.semaphore_wait(barrier, peers + 2)

    @pl.when(jnp.logical_not(inner))
    def _():
        pl.semaphore_wait(barrier, peers + min(1, space_count - 1))

    def scatter(part, piece, first, count, source):
        return pltpu.make_async_remote_copy(
            src_ref=low_send.at[part, pl.ds(first, count)],
            dst_ref=full.at[q, pl.ds(first, count)],
            send_sem=s1.at[part, piece],
            recv_sem=r1.at[q, source],
            device_id={"species": part, "mode": piece},
            device_id_type=MESH,
        )

    head_last = HEAD - 3 * PIECE

    def head_copies(step):
        part = lax.rem(q + step, SPLIT)
        found = []
        for piece in (3, 1, 2, 0):
            if step == 0 and piece == 0:
                continue
            count = PIECE if piece < 3 else head_last
            found.append(scatter(part, piece, piece * PIECE, count, 0))
        return found

    def tail_copies(step):
        return scatter(lax.rem(q + step, SPLIT), 3, HEAD, PACK - HEAD, 1)

    @pl.when(m == 0)
    def _():
        for step in (1, 2, 3, 0):
            for item in head_copies(step):
                item.start()
        full[q, 0:PIECE, :] = low_send[q, 0:PIECE, :]

    @pl.when(m == 1)
    def _():
        for step in (1, 2, 3, 0):
            tail_copies(step).start()

    for slot in range(OWN):
        halo_send[0, slot] = load(slot, slice(0, 64)).astype(BF16)
        halo_send[1, slot] = load(slot, slice(ROWS - 64, ROWS)).astype(BF16)

    def halo(way):
        return pltpu.make_async_remote_copy(
            src_ref=halo_send.at[way],
            dst_ref=halo_recv.at[1 - way],
            send_sem=hs.at[way],
            recv_sem=hr.at[1 - way],
            device_id={"mode": m - 1 if way == 0 else m + 1},
            device_id_type=MESH,
        )

    @pl.when((m == 1) | (m == 3))
    def _():
        halo(0).start()

    @pl.when(m == 2)
    def _():
        halo(1).start()

    for item in small[1:] + [copy_k]:
        item.wait()

    def lay(n, carry):
        k2[n] = jnp.zeros((PAD_J, NKIND * PAD_J), BF16)

        @pl.when(n < kraw.shape[1])
        def _():
            spot = jnp.minimum(n, kraw.shape[1] - 1)
            for kind in range(NKIND):
                k2[n, 0 : kraw.shape[2], kind * PAD_J : kind * PAD_J + kraw.shape[3]] = kraw[
                    kind, spot
                ]

        return carry

    lax.fori_loop(0, PAD_N, lay, 0)

    lanes = lax.broadcasted_iota(jnp.int32, (8, PAD_J), 1)
    low_count = kraw.shape[2]
    block_rows = kraw.shape[1]
    ordered = jnp.concatenate(
        [lm_ref[...], jnp.full((1, PAD_J - low_count), -2, jnp.int32)], axis=1
    )
    ordered = jnp.broadcast_to(ordered, (8, PAD_J))
    by_block = jnp.full((8, PAD_J), -2, jnp.int32)
    for block in range(SPLIT):
        moved = ordered
        if block > 0:
            moved = pltpu.roll(ordered, block * (PAD_N - block_rows), 1)
        inside = (lanes >= block * PAD_N) & (lanes < block * PAD_N + block_rows)
        by_block = jnp.where(inside, moved, by_block)
    for slot in range(OWN):
        same = tab_ref[:, 1 + slot : 2 + slot] == ordered[0:1, :]
        pick[slot * PAD_J : (slot + 1) * PAD_J, :] = jnp.where(same, 1.0, 0.0).T.astype(BF16)
    mode_of = lax.broadcasted_iota(jnp.int32, (ROWS, PAD_J), 0) + m * ROWS
    spread[...] = jnp.where(mode_of == by_block[0:1, :], 1.0, 0.0).astype(BF16)

    def piece_wait(source, count, sender):
        pltpu.make_async_remote_copy(
            src_ref=low_send.at[0, pl.ds(0, count)],
            dst_ref=full.at[source, pl.ds(0, count)],
            send_sem=s1.at[0, 0],
            recv_sem=r1.at[source, sender],
            device_id={"mode": lax.rem(m + 1, SPLIT)},
            device_id_type=MESH,
        ).wait_recv()

    def forward(source, step):
        rows = pl.ds(pl.multiple_of(m * PIECE, PIECE), PIECE)
        return pltpu.make_async_remote_copy(
            src_ref=full.at[source, rows],
            dst_ref=full.at[source, rows],
            send_sem=s2.at[source, step],
            recv_sem=r2.at[source, m],
            device_id={"mode": lax.rem(m + step, SPLIT)},
            device_id_type=MESH,
        )

    for back in range(SPLIT):
        source = lax.rem(q + SPLIT - back, SPLIT)

        if back > 0:

            @pl.when(m == 0)
            def _():
                piece_wait(source, PIECE, 0)

        @pl.when((m == 1) | (m == 2))
        def _():
            piece_wait(source, PIECE, 0)

        @pl.when(m == 3)
        def _():
            piece_wait(source, head_last, 0)
            piece_wait(source, PACK - HEAD, 1)

        for step in range(1, SPLIT):
            forward(source, step).start()

    @pl.when(m < 2)
    def _():
        halo(1).start()

    @pl.when(m == 2)
    def _():
        halo(0).start()

    degree_c = lax.broadcasted_iota(jnp.int32, (NVZ, 1), 0)
    sqrt_c = jnp.sqrt(degree_c.astype(F32))
    sqrt_c_up = jnp.where(degree_c == NVZ - 1, 0.0, jnp.sqrt(degree_c.astype(F32) + 1.0))
    planes = SPLIT * LANES // NY

    def own_terms(i, carry):
        slot = i // PER_VX
        a = lax.rem(i, PER_VX)
        scale = nu_step * th_ref[slot]
        relax = dt_step * rx_ref[slot]
        blocks = [
            load(slot, pl.ds(pl.multiple_of(a * 64 + b * NVZ, NVZ), NVZ)) for b in range(NVY)
        ]
        for b in range(NVY):
            here = blocks[b]
            flux_y = jnp.zeros_like(here)
            if b < NVY - 1:
                flux_y = flux_y + float(np.sqrt(np.float32(b + 1))) * blocks[b + 1]
            if b > 0:
                flux_y = flux_y + float(np.sqrt(np.float32(b))) * blocks[b - 1]
            up_y = 0.5 * flux_y - 0.5 * bound_y * here
            down_y = -0.5 * flux_y - 0.5 * bound_y * here
            turned = []
            for plane in range(planes):
                cut = slice(plane * NY, (plane + 1) * NY)
                turned.append(
                    pltpu.roll(up_y[:, cut], NY - 1, 1) + pltpu.roll(down_y[:, cut], 1, 1)
                )
            y_term = jnp.concatenate(turned, axis=1) + bound_y * here
            flux_z = sqrt_c_up * pltpu.roll(here, NVZ - 1, 0) + sqrt_c * pltpu.roll(here, 1, 0)
            wide = planes * NY
            up_z = 0.5 * flux_z - 0.5 * bound_z * here
            down_z = -0.5 * flux_z - 0.5 * bound_z * here
            z_term = (
                pltpu.roll(up_z, wide - NY, 1) + pltpu.roll(down_z, NY, 1) + bound_z * here
            )
            total = degree_c + (b + a + m * PER_VX)
            lost = jnp.where(total > DEG, relax, 0.0)
            value = here - scale * (y_term + z_term + bound_x * here) - lost * here
            rows = pl.ds(pl.multiple_of(a * 64 + b * NVZ, NVZ), NVZ)
            for part in range(SPLIT):
                out_ref[part, slot, rows, :] = value[:, part * LANES : (part + 1) * LANES]
        return carry

    lax.fori_loop(0, OWN * PER_VX, own_terms, 0)

    def x_parts(a):
        degree = (m * PER_VX + a).astype(F32)
        root = jnp.sqrt(jnp.full((8, 128), degree, F32))[0:1, 0:1]
        root_up = jnp.sqrt(jnp.full((8, 128), degree + 1.0, F32))[0:1, 0:1]

        def part(i, carry):
            slot = i // 4
            r = lax.rem(i, 4) * 16
            here = load(slot, pl.ds(pl.multiple_of(a * 64 + r, 16), 16))
            if a < PER_VX - 1:
                above = load(slot, pl.ds(pl.multiple_of((a + 1) * 64 + r, 16), 16))
            else:
                above = halo_recv[1, slot, pl.ds(pl.multiple_of(r, 16), 16), :].astype(F32)
            if a > 0:
                below = load(slot, pl.ds(pl.multiple_of((a - 1) * 64 + r, 16), 16))
            else:
                below = halo_recv[0, slot, pl.ds(pl.multiple_of(r, 16), 16), :].astype(F32)
            flux = root_up * above + root * below
            rows = pl.ds(pl.multiple_of(slot * 64 + r, 16), 16)
            ab_send[0, a, rows, :] = (0.5 * flux - 0.5 * bound_x * here).astype(ab_send.dtype)
            ab_send[1, a, rows, :] = (-0.5 * flux - 0.5 * bound_x * here).astype(ab_send.dtype)
            return carry

        lax.fori_loop(0, OWN * 4, part, 0)

    def layer(way, a):
        return pltpu.make_async_remote_copy(
            src_ref=ab_send.at[way, a],
            dst_ref=ab_recv.at[way, a],
            send_sem=xs.at[way, a],
            recv_sem=xr.at[way, a],
            device_id={"space": sx - 1 if way == 0 else sx + 1},
            device_id_type=MESH,
        )

    def send_layers(a):
        @pl.when(sx > 0)
        def _():
            layer(0, a).start()

        @pl.when(sx < space_count - 1)
        def _():
            layer(1, a).start()

    @pl.when(sx == space_count - 1)
    def _():
        ab_recv[0] = jnp.zeros(ab_recv.shape[1:], ab_recv.dtype)

    @pl.when(sx == 0)
    def _():
        ab_recv[1] = jnp.zeros(ab_recv.shape[1:], ab_recv.dtype)

    for a in (1, 2):
        x_parts(a)
        send_layers(a)

    def forward_wait(source, step):
        sender = lax.rem(m + step, SPLIT)
        pltpu.make_async_remote_copy(
            src_ref=full.at[source, pl.ds(0, PIECE)],
            dst_ref=full.at[source, pl.ds(0, PIECE)],
            send_sem=s2.at[source, step],
            recv_sem=r2.at[source, sender],
            device_id={"mode": sender},
            device_id_type=MESH,
        ).wait_recv()

    for back in range(SPLIT):
        source = lax.rem(q + SPLIT - back, SPLIT)
        for step in range(1, SPLIT):
            forward_wait(source, step)
        picked = dot(pick[...], full[source])
        for slot in range(OWN):
            low[source, :, slot * LANES : (slot + 1) * LANES] = picked[
                slot * PAD_J : (slot + 1) * PAD_J
            ]

    def of_species(r):
        return low[r // OWN, :, (r % OWN) * LANES : (r % OWN + 1) * LANES]

    everyone = of_species(0)
    for r in range(1, SPLIT * OWN):
        everyone = everyone + of_species(r)
    total[...] = everyone

    def partners(pair):
        def one(slot):
            first = jnp.zeros((PAD_J, LANES), F32)
            for r in range(SPLIT * OWN):
                weight = jnp.where(kind_ref[pair * OWN + slot, r] == 0, 1.0, 0.0)
                first = first + weight * of_species(r)
            cut = slice(slot * LANES, (slot + 1) * LANES)
            pmat[pair, 0:PAD_J, cut] = first.astype(BF16)
            pmat[pair, PAD_J:, cut] = (total[...] - first).astype(BF16)

        for slot in range(OWN):
            one(slot)

    def give(pair, target):
        return pltpu.make_async_remote_copy(
            src_ref=gsend.at[pair],
            dst_ref=grecv.at[q, pl.ds(pl.multiple_of(m * PAD_N, PAD_N), PAD_N)],
            send_sem=s3.at[pair, target],
            recv_sem=r3.at[q, m],
            device_id={"species": pair, "mode": target},
            device_id_type=MESH,
        )

    group = 8

    def collide(pair):
        def some(i, carry):
            left = k2[pl.ds(pl.multiple_of(i * group, group), group)]
            product = dot(left.reshape(group * PAD_J, NKIND * PAD_J), pmat[pair])
            own = low[pair]
            gsum[pl.ds(pl.multiple_of(i * group, group), group), :] = jnp.sum(
                product.reshape(group, PAD_J, OWN * LANES) * own[None], axis=1
            )
            return carry

        lax.fori_loop(0, PAD_N // group, some, 0)
        gsend[pair] = gsum[...].astype(BF16)

    for step in (1, 2, 3, 0):
        pair = lax.rem(q + step, SPLIT)
        partners(pair)
        collide(pair)
        for target in range(2):
            if step > 0:
                give(pair, target).start()
            else:

                @pl.when(m != target)
                def _():
                    give(pair, target).start()

                @pl.when(m == target)
                def _():
                    grecv[q, target * PAD_N : (target + 1) * PAD_N, :] = gsend[pair]

    @pl.when(m > 0)
    def _():
        halo(1).wait_recv()

    @pl.when(m == 0)
    def _():
        halo_recv[0] = jnp.zeros(halo_recv.shape[1:], BF16)

    @pl.when(m < SPLIT - 1)
    def _():
        halo(0).wait_recv()

    @pl.when(m == SPLIT - 1)
    def _():
        halo_recv[1] = jnp.zeros(halo_recv.shape[1:], BF16)

    for a in (0, 3):
        x_parts(a)
        send_layers(a)

    for a in (1, 2, 0, 3):

        @pl.when(sx < space_count - 1)
        def _():
            layer(0, a).wait_recv()

        @pl.when(sx > 0)
        def _():
            layer(1, a).wait_recv()

        def add_x(i, carry):
            slot = i // 4
            r = lax.rem(i, 4) * 16
            rows = pl.ds(pl.multiple_of(slot * 64 + r, 16), 16)
            here = pl.ds(pl.multiple_of(a * 64 + r, 16), 16)
            term = ab_recv[0, a, rows, :].astype(F32) + ab_recv[1, a, rows, :].astype(F32)
            term = (nu_step * th_ref[slot]) * term
            for part in range(SPLIT):
                out_ref[part, slot, here, :] = (
                    out_ref[part, slot, here, :] - term[:, part * LANES : (part + 1) * LANES]
                )
            return carry

        lax.fori_loop(0, OWN * 4, add_x, 0)

    def column_out(part, slot):
        return pltpu.make_async_copy(
            out_ref.at[part, slot],
            result.at[slot, :, 0, pl.ds(pl.multiple_of(part * LANES, LANES), LANES)],
            copy_sem.at[part, slot],
        )

    @pl.when(m >= 2)
    def _():
        for part in range(SPLIT):
            for slot in range(OWN):
                column_out(part, slot).start()

    @pl.when(m < 2)
    def _():
        for back in range(SPLIT):
            source = lax.rem(q + SPLIT - back, SPLIT)
            for sender in range(SPLIT):

                def take():
                    pltpu.make_async_remote_copy(
                        src_ref=gsend.at[0],
                        dst_ref=grecv.at[source, pl.ds(sender * PAD_N, PAD_N)],
                        send_sem=s3.at[0, 0],
                        recv_sem=r3.at[source, sender],
                        device_id={"mode": lax.rem(m + 1, SPLIT)},
                        device_id_type=MESH,
                    ).wait_recv()

                if back > 0 or sender > 1:
                    take()
                else:
                    pl.when(m != sender)(take)
            gained = dot(spread[...], grecv[source])
            for slot in range(OWN):
                out_ref[source, slot] = (
                    out_ref[source, slot] + dt_step * gained[:, slot * LANES : (slot + 1) * LANES]
                )
                column_out(source, slot).start()

    @pl.when(m == 0)
    def _():
        for step in range(SPLIT):
            for item in head_copies(step):
                item.wait_send()

    @pl.when(m == 1)
    def _():
        for step in range(SPLIT):
            tail_copies(step).wait_send()

    for back in range(SPLIT):
        for step in range(1, SPLIT):
            forward(lax.rem(q + SPLIT - back, SPLIT), step).wait_send()

    @pl.when(m > 0)
    def _():
        halo(0).wait_send()

    @pl.when(m < SPLIT - 1)
    def _():
        halo(1).wait_send()

    for a in range(PER_VX):

        @pl.when(sx > 0)
        def _():
            layer(0, a).wait_send()

        @pl.when(sx < space_count - 1)
        def _():
            layer(1, a).wait_send()

    for step in range(SPLIT):
        pair = lax.rem(q + step, SPLIT)
        for target in range(2):
            if step > 0:
                give(pair, target).wait_send()
            else:

                @pl.when(m != target)
                def _():
                    give(pair, target).wait_send()

    for part in range(SPLIT):
        for slot in range(OWN):
            column_out(part, slot).wait()


def write_out(source, result, sems):
    count = sems.shape[0]
    rows = result.shape[1] // count
    copies = [
        pltpu.make_async_copy(
            source.at[:, pl.ds(piece * rows, rows)],
            result.at[:, pl.ds(piece * rows, rows)],
            sems.at[piece],
        )
        for piece in range(count)
    ]
    for item in copies:
        item.start()
    for item in copies:
        item.wait()


def per_device(space_count, distribution, kernels, pair_kind, low_map, thermal_speed, relax_rate):
    own, rows, layers, cells = distribution.shape
    assert (own, rows, layers, cells) == (OWN, ROWS, 1, SPLIT * LANES)
    kinds, _, low_count, _ = kernels.shape
    table = jnp.asarray(packed_table())
    anywhere = pl.BlockSpec(memory_space=pl.ANY)
    dma = pltpu.SemaphoreType.DMA
    ab_type = F32
    stepped = pl.pallas_call(
        functools.partial(kernel, space_count),
        out_shape=jax.ShapeDtypeStruct(distribution.shape, F32),
        in_specs=[anywhere] * 7,
        out_specs=anywhere,
        scratch_shapes=[
            pltpu.VMEM((SPLIT, own, rows, LANES), F32),
            pltpu.VMEM((SPLIT, own, rows, LANES), F32),
            pltpu.VMEM(table.shape, jnp.int32),
            pltpu.VMEM((1, low_count), jnp.int32),
            pltpu.SMEM(pair_kind.shape, jnp.int32),
            pltpu.SMEM(thermal_speed.shape, F32),
            pltpu.SMEM(relax_rate.shape, F32),
            pltpu.VMEM(kernels.shape, BF16),
            pltpu.VMEM((PAD_N, PAD_J, kinds * PAD_J), BF16),
            pltpu.VMEM((SPLIT, PACK, LANES), BF16),
            pltpu.VMEM((SPLIT, PACK, LANES), BF16),
            pltpu.VMEM((SPLIT, PAD_J, own * LANES), F32),
            pltpu.VMEM((SPLIT, kinds * PAD_J, own * LANES), BF16),
            pltpu.VMEM((PAD_N, own * LANES), F32),
            pltpu.VMEM((PAD_J, LANES), F32),
            pltpu.VMEM((SPLIT, PAD_N, own * LANES), BF16),
            pltpu.VMEM((SPLIT, SPLIT * PAD_N, own * LANES), BF16),
            pltpu.VMEM((own * PAD_J, PACK), BF16),
            pltpu.VMEM((ROWS, PAD_J), BF16),
            pltpu.VMEM((2, own, 64, cells), BF16),
            pltpu.VMEM((2, own, 64, cells), BF16),
            pltpu.VMEM((2, PER_VX, own * 64, cells), ab_type),
            pltpu.VMEM((2, PER_VX, own * 64, cells), ab_type),
            dma((SPLIT, OWN)),
            dma((6,)),
            dma((SPLIT, SPLIT)),
            dma((SPLIT, 2)),
            dma((SPLIT, SPLIT)),
            dma((SPLIT, SPLIT)),
            dma((SPLIT, 2)),
            dma((SPLIT, SPLIT)),
            dma((2,)),
            dma((2,)),
            dma((2, PER_VX)),
            dma((2, PER_VX)),
        ],
        compiler_params=pltpu.CompilerParams(
            collective_id=0, has_side_effects=True, vmem_limit_bytes=60 * 1024 * 1024
        ),
    )(
        distribution,
        kernels,
        table,
        low_map.reshape(1, low_count),
        pair_kind,
        thermal_speed,
        relax_rate,
    )
    return pl.pallas_call(
        write_out,
        out_shape=jax.ShapeDtypeStruct(distribution.shape, F32),
        in_specs=[anywhere],
        out_specs=anywhere,
        scratch_shapes=[dma((8,))],
        compiler_params=pltpu.CompilerParams(vmem_limit_bytes=60 * 1024 * 1024),
    )(stepped)


def solution(mesh):
    in_specs = (
        P("species", "mode", "space", None),
        P(None, "mode", None, None),
        P(),
        P(),
        P("species"),
        P("species"),
    )
    out_specs = P("species", "mode", "space", None)
    return jax.shard_map(
        functools.partial(per_device, mesh.shape["space"]),
        mesh=mesh,
        in_specs=in_specs,
        out_specs=out_specs,
        check_vma=False,
    )
```

```python
import functools

import jax
import jax.numpy as jnp
import numpy as np
from jax import lax
from jax.experimental import pallas as pl
from jax.experimental.pallas import tpu as pltpu
from jax.sharding import PartitionSpec as P

MESH = pl.DeviceIdType.MESH
F32 = jnp.float32
BF16 = jnp.bfloat16

NVY = 8
NVZ = 8
DEG = 7
NKIND = 2
NY = 256

nu_step = 0.0625
dt_step = 0.05
bound_x = 6.7
bound_y = 4.2
bound_z = 4.2

SPLIT = 4
OWN = 2
ROWS = 256
PER_VX = 4
LANES = 128
HEAD = 208
PACK = 256
PIECE = 64
PAD_J = 128
PAD_N = 32


def packed_table():
    low = [
        (a * NVY + b) * NVZ + c
        for a in range(DEG + 1)
        for b in range(NVY)
        for c in range(NVZ)
        if a + b + c <= DEG
    ]
    table = np.full((PACK, 8), -1, np.int32)
    for start, first in ((0, 0), (HEAD, ROWS)):
        held = [mode for mode in low if first <= mode < first + ROWS]
        row = start
        for slot in range(OWN):
            for mode in held:
                table[row, 0] = slot * ROWS + mode - first
                table[row, 1 + slot] = mode
                row += 1
        assert row <= (HEAD if start == 0 else PACK)
    return table


def dot(left, right):
    return jnp.dot(left, right, preferred_element_type=F32)


def kernel(
    space_count,
    f_in,
    k_in,
    tab_in,
    map_in,
    kind_in,
    th_in,
    rx_in,
    result,
    f_ref,
    out_ref,
    tab_ref,
    lm_ref,
    kind_ref,
    th_ref,
    rx_ref,
    kraw,
    k2,
    low_send,
    full,
    low,
    pmat,
    gsum,
    total,
    gsend,
    grecv,
    pick,
    spread,
    halo_send,
    halo_recv,
    edge_recv,
    ab_send,
    ab_recv,
    copy_sem,
    small_sem,
    s1,
    r1,
    s2,
    r2,
    s3,
    r3,
    hs,
    hr,
    xs,
    xr,
    es,
    er,
):
    q = lax.axis_index("species")
    m = lax.axis_index("mode")
    sx = lax.axis_index("space")

    columns_in = [
        pltpu.make_async_copy(
            f_in.at[slot, :, 0, pl.ds(part * LANES, LANES)],
            f_ref.at[part, slot],
            copy_sem.at[part, slot],
        )
        for part in range(SPLIT)
        for slot in range(OWN)
    ]
    small = [
        pltpu.make_async_copy(tab_in, tab_ref, small_sem.at[0]),
        pltpu.make_async_copy(map_in, lm_ref, small_sem.at[1]),
        pltpu.make_async_copy(kind_in, kind_ref, small_sem.at[2]),
        pltpu.make_async_copy(th_in, th_ref, small_sem.at[3]),
        pltpu.make_async_copy(rx_in, rx_ref, small_sem.at[4]),
    ]
    copy_k = pltpu.make_async_copy(k_in, kraw, small_sem.at[5])
    for item in columns_in + small[:1]:
        item.start()

    barrier = pltpu.get_barrier_semaphore()
    for step in range(1, SPLIT * SPLIT):
        other = lax.rem(q * SPLIT + m + step, SPLIT * SPLIT)
        pl.semaphore_signal(
            barrier,
            inc=1,
            device_id={"species": other // SPLIT, "mode": lax.rem(other, SPLIT)},
            device_id_type=MESH,
        )

    @pl.when(sx > 0)
    def _():
        pl.semaphore_signal(barrier, inc=1, device_id={"space": sx - 1}, device_id_type=MESH)

    @pl.when(sx < space_count - 1)
    def _():
        pl.semaphore_signal(barrier, inc=1, device_id={"space": sx + 1}, device_id_type=MESH)

    for item in small[1:] + [copy_k]:
        item.start()
    for item in columns_in + small[:1]:
        item.wait()

    def load(slot, rows):
        return jnp.concatenate([f_ref[part, slot, rows, :] for part in range(SPLIT)], axis=1)

    def extract(first, count):
        rows = lax.broadcasted_iota(jnp.int32, (count, OWN * ROWS), 1)
        chosen = jnp.where(tab_ref[first : first + count, 0:1] == rows, 1.0, 0.0).astype(BF16)
        for part in range(SPLIT):
            field = f_ref[part].reshape(OWN * ROWS, LANES).astype(BF16)
            low_send[part, first : first + count, :] = dot(chosen, field).astype(BF16)

    @pl.when(m == 0)
    def _():
        extract(0, HEAD)

    @pl.when(m == 1)
    def _():
        extract(HEAD, PACK - HEAD)

    inner = (sx > 0) & (sx < space_count - 1)
    peers = SPLIT * SPLIT - 1

    @pl.when(inner)
    def _():
        pl.semaphore_wait(barrier, peers + 2)

    @pl.when(jnp.logical_not(inner))
    def _():
        pl.semaphore_wait(barrier, peers + min(1, space_count - 1))

    def scatter(part, piece, first, count, source):
        return pltpu.make_async_remote_copy(
            src_ref=low_send.at[part, pl.ds(first, count)],
            dst_ref=full.at[q, pl.ds(first, count)],
            send_sem=s1.at[part, piece],
            recv_sem=r1.at[q, source],
            device_id={"species": part, "mode": piece},
            device_id_type=MESH,
        )

    head_last = HEAD - 3 * PIECE

    def head_copies(step):
        part = lax.rem(q + step, SPLIT)
        found = []
        for piece in (3, 1, 2, 0):
            if step == 0 and piece == 0:
                continue
            count = PIECE if piece < 3 else head_last
            found.append(scatter(part, piece, piece * PIECE, count, 0))
        return found

    def tail_copies(step):
        return scatter(lax.rem(q + step, SPLIT), 3, HEAD, PACK - HEAD, 1)

    @pl.when(m == 0)
    def _():
        for step in (1, 2, 3, 0):
            for item in head_copies(step):
                item.start()
        full[q, 0:PIECE, :] = low_send[q, 0:PIECE, :]

    @pl.when(m == 1)
    def _():
        for step in (1, 2, 3, 0):
            tail_copies(step).start()

    for slot in range(OWN):
        halo_send[0, slot] = load(slot, slice(0, 64)).astype(BF16)
        halo_send[1, slot] = load(slot, slice(ROWS - 64, ROWS)).astype(BF16)

    def halo(way):
        return pltpu.make_async_remote_copy(
            src_ref=halo_send.at[way],
            dst_ref=halo_recv.at[1 - way],
            send_sem=hs.at[way],
            recv_sem=hr.at[1 - way],
            device_id={"mode": m - 1 if way == 0 else m + 1},
            device_id_type=MESH,
        )

    @pl.when((m == 1) | (m == 3))
    def _():
        halo(0).start()

    @pl.when(m == 2)
    def _():
        halo(1).start()

    for item in small[1:] + [copy_k]:
        item.wait()

    def lay(n, carry):
        k2[n] = jnp.zeros((PAD_J, NKIND * PAD_J), BF16)

        @pl.when(n < kraw.shape[1])
        def _():
            spot = jnp.minimum(n, kraw.shape[1] - 1)
            for kind in range(NKIND):
                k2[n, 0 : kraw.shape[2], kind * PAD_J : kind * PAD_J + kraw.shape[3]] = kraw[
                    kind, spot
                ]

        return carry

    lax.fori_loop(0, PAD_N, lay, 0)

    lanes = lax.broadcasted_iota(jnp.int32, (8, PAD_J), 1)
    low_count = kraw.shape[2]
    block_rows = kraw.shape[1]
    ordered = jnp.concatenate(
        [lm_ref[...], jnp.full((1, PAD_J - low_count), -2, jnp.int32)], axis=1
    )
    ordered = jnp.broadcast_to(ordered, (8, PAD_J))
    by_block = jnp.full((8, PAD_J), -2, jnp.int32)
    for block in range(SPLIT):
        moved = ordered
        if block > 0:
            moved = pltpu.roll(ordered, block * (PAD_N - block_rows), 1)
        inside = (lanes >= block * PAD_N) & (lanes < block * PAD_N + block_rows)
        by_block = jnp.where(inside, moved, by_block)
    for slot in range(OWN):
        same = tab_ref[:, 1 + slot : 2 + slot] == ordered[0:1, :]
        pick[slot * PAD_J : (slot + 1) * PAD_J, :] = jnp.where(same, 1.0, 0.0).T.astype(BF16)
    mode_of = lax.broadcasted_iota(jnp.int32, (ROWS, PAD_J), 0) + m * ROWS
    spread[...] = jnp.where(mode_of == by_block[0:1, :], 1.0, 0.0).astype(BF16)

    def piece_wait(source, count, sender):
        pltpu.make_async_remote_copy(
            src_ref=low_send.at[0, pl.ds(0, count)],
            dst_ref=full.at[source, pl.ds(0, count)],
            send_sem=s1.at[0, 0],
            recv_sem=r1.at[source, sender],
            device_id={"mode": lax.rem(m + 1, SPLIT)},
            device_id_type=MESH,
        ).wait_recv()

    def forward(source, step):
        rows = pl.ds(pl.multiple_of(m * PIECE, PIECE), PIECE)
        return pltpu.make_async_remote_copy(
            src_ref=full.at[source, rows],
            dst_ref=full.at[source, rows],
            send_sem=s2.at[source, step],
            recv_sem=r2.at[source, m],
            device_id={"mode": lax.rem(m + step, SPLIT)},
            device_id_type=MESH,
        )

    for back in range(SPLIT):
        source = lax.rem(q + SPLIT - back, SPLIT)

        if back > 0:

            @pl.when(m == 0)
            def _():
                piece_wait(source, PIECE, 0)

        @pl.when((m == 1) | (m == 2))
        def _():
            piece_wait(source, PIECE, 0)

        @pl.when(m == 3)
        def _():
            piece_wait(source, head_last, 0)
            piece_wait(source, PACK - HEAD, 1)

        for step in range(1, SPLIT):
            forward(source, step).start()

    @pl.when(m < 2)
    def _():
        halo(1).start()

    @pl.when(m == 2)
    def _():
        halo(0).start()

    degree_c = lax.broadcasted_iota(jnp.int32, (NVZ, 1), 0)
    sqrt_c = jnp.sqrt(degree_c.astype(F32))
    sqrt_c_up = jnp.where(degree_c == NVZ - 1, 0.0, jnp.sqrt(degree_c.astype(F32) + 1.0))
    planes = SPLIT * LANES // NY

    def own_terms(i, carry):
        slot = i // PER_VX
        a = lax.rem(i, PER_VX)
        scale = nu_step * th_ref[slot]
        relax = dt_step * rx_ref[slot]
        blocks = [
            load(slot, pl.ds(pl.multiple_of(a * 64 + b * NVZ, NVZ), NVZ)) for b in range(NVY)
        ]
        for b in range(NVY):
            here = blocks[b]
            flux_y = jnp.zeros_like(here)
            if b < NVY - 1:
                flux_y = flux_y + float(np.sqrt(np.float32(b + 1))) * blocks[b + 1]
            if b > 0:
                flux_y = flux_y + float(np.sqrt(np.float32(b))) * blocks[b - 1]
            up_y = 0.5 * flux_y - 0.5 * bound_y * here
            down_y = -0.5 * flux_y - 0.5 * bound_y * here
            turned = []
            for plane in range(planes):
                cut = slice(plane * NY, (plane + 1) * NY)
                turned.append(
                    pltpu.roll(up_y[:, cut], NY - 1, 1) + pltpu.roll(down_y[:, cut], 1, 1)
                )
            y_term = jnp.concatenate(turned, axis=1) + bound_y * here
            flux_z = sqrt_c_up * pltpu.roll(here, NVZ - 1, 0) + sqrt_c * pltpu.roll(here, 1, 0)
            wide = planes * NY
            up_z = 0.5 * flux_z - 0.5 * bound_z * here
            down_z = -0.5 * flux_z - 0.5 * bound_z * here
            z_term = (
                pltpu.roll(up_z, wide - NY, 1) + pltpu.roll(down_z, NY, 1) + bound_z * here
            )
            total = degree_c + (b + a + m * PER_VX)
            lost = jnp.where(total > DEG, relax, 0.0)
            value = here - scale * (y_term + z_term + bound_x * here) - lost * here
            rows = pl.ds(pl.multiple_of(a * 64 + b * NVZ, NVZ), NVZ)
            for part in range(SPLIT):
                out_ref[part, slot, rows, :] = value[:, part * LANES : (part + 1) * LANES]
        return carry

    lax.fori_loop(0, OWN * PER_VX, own_terms, 0)

    def degree_roots(a):
        degree = (m * PER_VX + a).astype(F32)
        below = jnp.sqrt(jnp.full((8, 128), degree, F32))[0:1, 0:1]
        above = jnp.sqrt(jnp.full((8, 128), degree + 1.0, F32))[0:1, 0:1]
        return below, above

    def x_parts(a):
        root, root_up = degree_roots(a)

        def part(i, carry):
            slot = i // 4
            r = lax.rem(i, 4) * 16
            here = load(slot, pl.ds(pl.multiple_of(a * 64 + r, 16), 16))
            flux = jnp.zeros_like(here)
            if a < PER_VX - 1:
                flux = flux + root_up * load(slot, pl.ds(pl.multiple_of((a + 1) * 64 + r, 16), 16))
            if a > 0:
                flux = flux + root * load(slot, pl.ds(pl.multiple_of((a - 1) * 64 + r, 16), 16))
            rows = pl.ds(pl.multiple_of(slot * 64 + r, 16), 16)
            ab_send[0, a, rows, :] = (0.5 * flux - 0.5 * bound_x * here).astype(ab_send.dtype)
            ab_send[1, a, rows, :] = (-0.5 * flux - 0.5 * bound_x * here).astype(ab_send.dtype)
            return carry

        lax.fori_loop(0, OWN * 4, part, 0)

    def layer(way, a):
        return pltpu.make_async_remote_copy(
            src_ref=ab_send.at[way, a],
            dst_ref=ab_recv.at[way, a],
            send_sem=xs.at[way, a],
            recv_sem=xr.at[way, a],
            device_id={"space": sx - 1 if way == 0 else sx + 1},
            device_id_type=MESH,
        )

    def send_layers(a):
        @pl.when(sx > 0)
        def _():
            layer(0, a).start()

        @pl.when(sx < space_count - 1)
        def _():
            layer(1, a).start()

    @pl.when(sx == space_count - 1)
    def _():
        ab_recv[0] = jnp.zeros(ab_recv.shape[1:], ab_recv.dtype)
        edge_recv[0] = jnp.zeros(edge_recv.shape[1:], BF16)

    @pl.when(sx == 0)
    def _():
        ab_recv[1] = jnp.zeros(ab_recv.shape[1:], ab_recv.dtype)
        edge_recv[1] = jnp.zeros(edge_recv.shape[1:], BF16)

    for a in range(PER_VX):
        x_parts(a)
        send_layers(a)

    def forward_wait(source, step):
        sender = lax.rem(m + step, SPLIT)
        pltpu.make_async_remote_copy(
            src_ref=full.at[source, pl.ds(0, PIECE)],
            dst_ref=full.at[source, pl.ds(0, PIECE)],
            send_sem=s2.at[source, step],
            recv_sem=r2.at[source, sender],
            device_id={"mode": sender},
            device_id_type=MESH,
        ).wait_recv()

    for back in range(SPLIT):
        source = lax.rem(q + SPLIT - back, SPLIT)
        for step in range(1, SPLIT):
            forward_wait(source, step)
        picked = dot(pick[...], full[source])
        for slot in range(OWN):
            low[source, :, slot * LANES : (slot + 1) * LANES] = picked[
                slot * PAD_J : (slot + 1) * PAD_J
            ]

    def of_species(r):
        return low[r // OWN, :, (r % OWN) * LANES : (r % OWN + 1) * LANES]

    everyone = of_species(0)
    for r in range(1, SPLIT * OWN):
        everyone = everyone + of_species(r)
    total[...] = everyone

    def partners(pair):
        def one(slot):
            first = jnp.zeros((PAD_J, LANES), F32)
            for r in range(SPLIT * OWN):
                weight = jnp.where(kind_ref[pair * OWN + slot, r] == 0, 1.0, 0.0)
                first = first + weight * of_species(r)
            cut = slice(slot * LANES, (slot + 1) * LANES)
            pmat[pair, 0:PAD_J, cut] = first.astype(BF16)
            pmat[pair, PAD_J:, cut] = (total[...] - first).astype(BF16)

        for slot in range(OWN):
            one(slot)

    def give(pair, target):
        return pltpu.make_async_remote_copy(
            src_ref=gsend.at[pair],
            dst_ref=grecv.at[q, pl.ds(pl.multiple_of(m * PAD_N, PAD_N), PAD_N)],
            send_sem=s3.at[pair, target],
            recv_sem=r3.at[q, m],
            device_id={"species": pair, "mode": target},
            device_id_type=MESH,
        )

    group = 8

    def collide(pair):
        def some(i, carry):
            left = k2[pl.ds(pl.multiple_of(i * group, group), group)]
            product = dot(left.reshape(group * PAD_J, NKIND * PAD_J), pmat[pair])
            own = low[pair]
            gsum[pl.ds(pl.multiple_of(i * group, group), group), :] = jnp.sum(
                product.reshape(group, PAD_J, OWN * LANES) * own[None], axis=1
            )
            return carry

        lax.fori_loop(0, PAD_N // group, some, 0)
        gsend[pair] = gsum[...].astype(BF16)

    for step in (1, 2, 3, 0):
        pair = lax.rem(q + step, SPLIT)
        partners(pair)
        collide(pair)
        for target in range(2):
            if step > 0:
                give(pair, target).start()
            else:

                @pl.when(m != target)
                def _():
                    give(pair, target).start()

                @pl.when(m == target)
                def _():
                    grecv[q, target * PAD_N : (target + 1) * PAD_N, :] = gsend[pair]

    @pl.when(m > 0)
    def _():
        halo(1).wait_recv()

    @pl.when(m == 0)
    def _():
        halo_recv[0] = jnp.zeros(halo_recv.shape[1:], BF16)

    @pl.when(m < SPLIT - 1)
    def _():
        halo(0).wait_recv()

    @pl.when(m == SPLIT - 1)
    def _():
        halo_recv[1] = jnp.zeros(halo_recv.shape[1:], BF16)

    def edges(way):
        return pltpu.make_async_remote_copy(
            src_ref=halo_recv,
            dst_ref=edge_recv.at[way],
            send_sem=es.at[way],
            recv_sem=er.at[way],
            device_id={"space": sx - 1 if way == 0 else sx + 1},
            device_id_type=MESH,
        )

    @pl.when(sx > 0)
    def _():
        edges(0).start()

    @pl.when(sx < space_count - 1)
    def _():
        edges(1).start()

    for a in range(PER_VX):

        @pl.when(sx < space_count - 1)
        def _():
            layer(0, a).wait_recv()

        @pl.when(sx > 0)
        def _():
            layer(1, a).wait_recv()

    @pl.when(sx < space_count - 1)
    def _():
        edges(0).wait_recv()

    @pl.when(sx > 0)
    def _():
        edges(1).wait_recv()

    for a in range(PER_VX):
        root, root_up = degree_roots(a)

        def add_x(i, carry):
            slot = i // 4
            r = pl.multiple_of(lax.rem(i, 4) * 16, 16)
            rows = pl.ds(pl.multiple_of(slot * 64 + r, 16), 16)
            here = pl.ds(pl.multiple_of(a * 64 + r, 16), 16)
            term = ab_recv[0, a, rows, :] + ab_recv[1, a, rows, :]
            side = {0: 0, PER_VX - 1: 1}.get(a)
            if side is not None:
                up = edge_recv[0, side, slot, pl.ds(r, 16), :].astype(F32)
                down = edge_recv[1, side, slot, pl.ds(r, 16), :].astype(F32)
                term = term + (0.5 * (root_up if side else root)) * (up - down)
            term = (nu_step * th_ref[slot]) * term
            for part in range(SPLIT):
                out_ref[part, slot, here, :] = (
                    out_ref[part, slot, here, :] - term[:, part * LANES : (part + 1) * LANES]
                )
            return carry

        lax.fori_loop(0, OWN * 4, add_x, 0)

    def column_out(part, slot):
        return pltpu.make_async_copy(
            out_ref.at[part, slot],
            result.at[slot, :, 0, pl.ds(pl.multiple_of(part * LANES, LANES), LANES)],
            copy_sem.at[part, slot],
        )

    @pl.when(m >= 2)
    def _():
        for part in range(SPLIT):
            for slot in range(OWN):
                column_out(part, slot).start()

    @pl.when(m < 2)
    def _():
        for back in range(SPLIT):
            source = lax.rem(q + SPLIT - back, SPLIT)
            for sender in range(SPLIT):

                def take():
                    pltpu.make_async_remote_copy(
                        src_ref=gsend.at[0],
                        dst_ref=grecv.at[source, pl.ds(sender * PAD_N, PAD_N)],
                        send_sem=s3.at[0, 0],
                        recv_sem=r3.at[source, sender],
                        device_id={"mode": lax.rem(m + 1, SPLIT)},
                        device_id_type=MESH,
                    ).wait_recv()

                if back > 0 or sender > 1:
                    take()
                else:
                    pl.when(m != sender)(take)
            gained = dot(spread[...], grecv[source])
            for slot in range(OWN):
                out_ref[source, slot] = (
                    out_ref[source, slot] + dt_step * gained[:, slot * LANES : (slot + 1) * LANES]
                )
                column_out(source, slot).start()

    @pl.when(m == 0)
    def _():
        for step in range(SPLIT):
            for item in head_copies(step):
                item.wait_send()

    @pl.when(m == 1)
    def _():
        for step in range(SPLIT):
            tail_copies(step).wait_send()

    for back in range(SPLIT):
        for step in range(1, SPLIT):
            forward(lax.rem(q + SPLIT - back, SPLIT), step).wait_send()

    @pl.when(m > 0)
    def _():
        halo(0).wait_send()

    @pl.when(m < SPLIT - 1)
    def _():
        halo(1).wait_send()

    for a in range(PER_VX):

        @pl.when(sx > 0)
        def _():
            layer(0, a).wait_send()

        @pl.when(sx < space_count - 1)
        def _():
            layer(1, a).wait_send()

    @pl.when(sx > 0)
    def _():
        edges(0).wait_send()

    @pl.when(sx < space_count - 1)
    def _():
        edges(1).wait_send()

    for step in range(SPLIT):
        pair = lax.rem(q + step, SPLIT)
        for target in range(2):
            if step > 0:
                give(pair, target).wait_send()
            else:

                @pl.when(m != target)
                def _():
                    give(pair, target).wait_send()

    for part in range(SPLIT):
        for slot in range(OWN):
            column_out(part, slot).wait()


def write_out(source, result, held, sems):
    count = sems.shape[1]
    rows = result.shape[1] // count

    def move(src, dst, way, piece):
        cut = pl.ds(piece * rows, rows)
        return pltpu.make_async_copy(src.at[:, cut], dst.at[:, cut], sems.at[way, piece])

    for piece in range(count):
        move(source, held, 0, piece).start()
    for piece in range(count):
        move(source, held, 0, piece).wait()
        move(held, result, 1, piece).start()
    for piece in range(count):
        move(held, result, 1, piece).wait()


def per_device(space_count, distribution, kernels, pair_kind, low_map, thermal_speed, relax_rate):
    own, rows, layers, cells = distribution.shape
    assert (own, rows, layers, cells) == (OWN, ROWS, 1, SPLIT * LANES)
    kinds, _, low_count, _ = kernels.shape
    table = jnp.asarray(packed_table())
    anywhere = pl.BlockSpec(memory_space=pl.ANY)
    dma = pltpu.SemaphoreType.DMA
    ab_type = F32
    stepped = pl.pallas_call(
        functools.partial(kernel, space_count),
        out_shape=jax.ShapeDtypeStruct(distribution.shape, F32),
        in_specs=[anywhere] * 7,
        out_specs=anywhere,
        scratch_shapes=[
            pltpu.VMEM((SPLIT, own, rows, LANES), F32),
            pltpu.VMEM((SPLIT, own, rows, LANES), F32),
            pltpu.VMEM(table.shape, jnp.int32),
            pltpu.VMEM((1, low_count), jnp.int32),
            pltpu.SMEM(pair_kind.shape, jnp.int32),
            pltpu.SMEM(thermal_speed.shape, F32),
            pltpu.SMEM(relax_rate.shape, F32),
            pltpu.VMEM(kernels.shape, BF16),
            pltpu.VMEM((PAD_N, PAD_J, kinds * PAD_J), BF16),
            pltpu.VMEM((SPLIT, PACK, LANES), BF16),
            pltpu.VMEM((SPLIT, PACK, LANES), BF16),
            pltpu.VMEM((SPLIT, PAD_J, own * LANES), F32),
            pltpu.VMEM((SPLIT, kinds * PAD_J, own * LANES), BF16),
            pltpu.VMEM((PAD_N, own * LANES), F32),
            pltpu.VMEM((PAD_J, LANES), F32),
            pltpu.VMEM((SPLIT, PAD_N, own * LANES), BF16),
            pltpu.VMEM((SPLIT, SPLIT * PAD_N, own * LANES), BF16),
            pltpu.VMEM((own * PAD_J, PACK), BF16),
            pltpu.VMEM((ROWS, PAD_J), BF16),
            pltpu.VMEM((2, own, 64, cells), BF16),
            pltpu.VMEM((2, own, 64, cells), BF16),
            pltpu.VMEM((2, 2, own, 64, cells), BF16),
            pltpu.VMEM((2, PER_VX, own * 64, cells), ab_type),
            pltpu.VMEM((2, PER_VX, own * 64, cells), ab_type),
            dma((SPLIT, OWN)),
            dma((6,)),
            dma((SPLIT, SPLIT)),
            dma((SPLIT, 2)),
            dma((SPLIT, SPLIT)),
            dma((SPLIT, SPLIT)),
            dma((SPLIT, 2)),
            dma((SPLIT, SPLIT)),
            dma((2,)),
            dma((2,)),
            dma((2, PER_VX)),
            dma((2, PER_VX)),
            dma((2,)),
            dma((2,)),
        ],
        compiler_params=pltpu.CompilerParams(
            collective_id=0, has_side_effects=True, vmem_limit_bytes=60 * 1024 * 1024
        ),
    )(
        distribution,
        kernels,
        table,
        low_map.reshape(1, low_count),
        pair_kind,
        thermal_speed,
        relax_rate,
    )
    return pl.pallas_call(
        write_out,
        out_shape=jax.ShapeDtypeStruct(distribution.shape, F32),
        in_specs=[anywhere],
        out_specs=anywhere,
        scratch_shapes=[pltpu.VMEM(distribution.shape, F32), dma((2, 4))],
        compiler_params=pltpu.CompilerParams(vmem_limit_bytes=60 * 1024 * 1024),
    )(stepped)


def solution(mesh):
    in_specs = (
        P("species", "mode", "space", None),
        P(None, "mode", None, None),
        P(),
        P(),
        P("species"),
        P("species"),
    )
    out_specs = P("species", "mode", "space", None)
    return jax.shard_map(
        functools.partial(per_device, mesh.shape["space"]),
        mesh=mesh,
        in_specs=in_specs,
        out_specs=out_specs,
        check_vma=False,
    )
```

```python
import functools

import jax
import jax.numpy as jnp
import numpy as np
from jax import lax
from jax.experimental import pallas as pl
from jax.experimental.pallas import tpu as pltpu
from jax.sharding import PartitionSpec as P

MESH = pl.DeviceIdType.MESH
F32 = jnp.float32
BF16 = jnp.bfloat16

NVY = 8
NVZ = 8
DEG = 7
NKIND = 2
NY = 256

nu_step = 0.0625
dt_step = 0.05
bound_x = 6.7
bound_y = 4.2
bound_z = 4.2

SPLIT = 4
OWN = 2
ROWS = 256
PER_VX = 4
LANES = 128
HEAD = 208
PACK = 256
PIECE = 64
PAD_J = 128
PAD_N = 32


def packed_table():
    low = [
        (a * NVY + b) * NVZ + c
        for a in range(DEG + 1)
        for b in range(NVY)
        for c in range(NVZ)
        if a + b + c <= DEG
    ]
    table = np.full((PACK, 8), -1, np.int32)
    for start, first in ((0, 0), (HEAD, ROWS)):
        held = [mode for mode in low if first <= mode < first + ROWS]
        row = start
        for slot in range(OWN):
            for mode in held:
                table[row, 0] = slot * ROWS + mode - first
                table[row, 1 + slot] = mode
                row += 1
        assert row <= (HEAD if start == 0 else PACK)
    return table


def dot(left, right):
    return jnp.dot(left, right, preferred_element_type=F32)


def kernel(
    space_count,
    f_in,
    k_in,
    tab_in,
    map_in,
    kind_in,
    th_in,
    rx_in,
    result,
    f_ref,
    out_ref,
    tab_ref,
    lm_ref,
    kind_ref,
    th_ref,
    rx_ref,
    kraw,
    k2,
    low_send,
    full,
    low,
    pmat,
    total,
    gsend,
    grecv,
    pick,
    spread,
    halo_send,
    halo_recv,
    edge_recv,
    ab_send,
    ab_recv,
    copy_sem,
    small_sem,
    s1,
    r1,
    s2,
    r2,
    s3,
    r3,
    hs,
    hr,
    xs,
    xr,
    es,
    er,
):
    q = lax.axis_index("species")
    m = lax.axis_index("mode")
    sx = lax.axis_index("space")

    columns_in = [
        pltpu.make_async_copy(
            f_in.at[slot, :, 0, pl.ds(part * LANES, LANES)],
            f_ref.at[part, slot],
            copy_sem.at[part, slot],
        )
        for part in range(SPLIT)
        for slot in range(OWN)
    ]
    small = [
        pltpu.make_async_copy(tab_in, tab_ref, small_sem.at[0]),
        pltpu.make_async_copy(map_in, lm_ref, small_sem.at[1]),
        pltpu.make_async_copy(kind_in, kind_ref, small_sem.at[2]),
        pltpu.make_async_copy(th_in, th_ref, small_sem.at[3]),
        pltpu.make_async_copy(rx_in, rx_ref, small_sem.at[4]),
    ]
    copy_k = pltpu.make_async_copy(k_in, kraw, small_sem.at[5])
    for item in columns_in + small[:1]:
        item.start()

    barrier = pltpu.get_barrier_semaphore()
    for step in range(1, SPLIT * SPLIT):
        other = lax.rem(q * SPLIT + m + step, SPLIT * SPLIT)
        pl.semaphore_signal(
            barrier,
            inc=1,
            device_id={"species": other // SPLIT, "mode": lax.rem(other, SPLIT)},
            device_id_type=MESH,
        )

    @pl.when(sx > 0)
    def _():
        pl.semaphore_signal(barrier, inc=1, device_id={"space": sx - 1}, device_id_type=MESH)

    @pl.when(sx < space_count - 1)
    def _():
        pl.semaphore_signal(barrier, inc=1, device_id={"space": sx + 1}, device_id_type=MESH)

    for item in small[1:] + [copy_k]:
        item.start()
    for item in columns_in + small[:1]:
        item.wait()

    def load(slot, rows):
        return jnp.concatenate([f_ref[part, slot, rows, :] for part in range(SPLIT)], axis=1)

    def extract(first, count):
        rows = lax.broadcasted_iota(jnp.int32, (count, OWN * ROWS), 1)
        chosen = jnp.where(tab_ref[first : first + count, 0:1] == rows, 1.0, 0.0).astype(BF16)
        for part in range(SPLIT):
            field = f_ref[part].reshape(OWN * ROWS, LANES).astype(BF16)
            low_send[part, first : first + count, :] = dot(chosen, field).astype(BF16)

    @pl.when(m == 0)
    def _():
        extract(0, HEAD)

    @pl.when(m == 1)
    def _():
        extract(HEAD, PACK - HEAD)

    inner = (sx > 0) & (sx < space_count - 1)
    peers = SPLIT * SPLIT - 1

    @pl.when(inner)
    def _():
        pl.semaphore_wait(barrier, peers + 2)

    @pl.when(jnp.logical_not(inner))
    def _():
        pl.semaphore_wait(barrier, peers + min(1, space_count - 1))

    def scatter(part, piece, first, count, source):
        return pltpu.make_async_remote_copy(
            src_ref=low_send.at[part, pl.ds(first, count)],
            dst_ref=full.at[q, pl.ds(first, count)],
            send_sem=s1.at[part, piece],
            recv_sem=r1.at[q, source],
            device_id={"species": part, "mode": piece},
            device_id_type=MESH,
        )

    head_last = HEAD - 3 * PIECE

    def head_copies(step):
        part = lax.rem(q + step, SPLIT)
        found = []
        for piece in (3, 1, 2, 0):
            if step == 0 and piece == 0:
                continue
            count = PIECE if piece < 3 else head_last
            found.append(scatter(part, piece, piece * PIECE, count, 0))
        return found

    def tail_copies(step):
        return scatter(lax.rem(q + step, SPLIT), 3, HEAD, PACK - HEAD, 1)

    @pl.when(m == 0)
    def _():
        for step in (1, 2, 3, 0):
            for item in head_copies(step):
                item.start()
        full[q, 0:PIECE, :] = low_send[q, 0:PIECE, :]

    @pl.when(m == 1)
    def _():
        for step in (1, 2, 3, 0):
            tail_copies(step).start()

    for slot in range(OWN):
        halo_send[0, slot] = load(slot, slice(0, 64)).astype(BF16)
        halo_send[1, slot] = load(slot, slice(ROWS - 64, ROWS)).astype(BF16)

    def halo(way):
        return pltpu.make_async_remote_copy(
            src_ref=halo_send.at[way],
            dst_ref=halo_recv.at[1 - way],
            send_sem=hs.at[way],
            recv_sem=hr.at[1 - way],
            device_id={"mode": m - 1 if way == 0 else m + 1},
            device_id_type=MESH,
        )

    @pl.when((m == 1) | (m == 3))
    def _():
        halo(0).start()

    @pl.when(m == 2)
    def _():
        halo(1).start()

    for item in small[1:] + [copy_k]:
        item.wait()

    def lay(n, carry):
        k2[n] = jnp.zeros((PAD_J, NKIND * PAD_J), BF16)

        @pl.when(n < kraw.shape[1])
        def _():
            spot = jnp.minimum(n, kraw.shape[1] - 1)
            for kind in range(NKIND):
                k2[n, 0 : kraw.shape[2], kind * PAD_J : kind * PAD_J + kraw.shape[3]] = kraw[
                    kind, spot
                ]

        return carry

    lax.fori_loop(0, PAD_N, lay, 0)

    lanes = lax.broadcasted_iota(jnp.int32, (8, PAD_J), 1)
    low_count = kraw.shape[2]
    block_rows = kraw.shape[1]
    ordered = jnp.concatenate(
        [lm_ref[...], jnp.full((1, PAD_J - low_count), -2, jnp.int32)], axis=1
    )
    ordered = jnp.broadcast_to(ordered, (8, PAD_J))
    by_block = jnp.full((8, PAD_J), -2, jnp.int32)
    for block in range(SPLIT):
        moved = ordered
        if block > 0:
            moved = pltpu.roll(ordered, block * (PAD_N - block_rows), 1)
        inside = (lanes >= block * PAD_N) & (lanes < block * PAD_N + block_rows)
        by_block = jnp.where(inside, moved, by_block)
    for slot in range(OWN):
        same = tab_ref[:, 1 + slot : 2 + slot] == ordered[0:1, :]
        pick[slot * PAD_J : (slot + 1) * PAD_J, :] = jnp.where(same, 1.0, 0.0).T.astype(BF16)
    mode_of = lax.broadcasted_iota(jnp.int32, (ROWS, PAD_J), 0) + m * ROWS
    spread[...] = jnp.where(mode_of == by_block[0:1, :], 1.0, 0.0).astype(BF16)

    def piece_wait(source, count, sender):
        pltpu.make_async_remote_copy(
            src_ref=low_send.at[0, pl.ds(0, count)],
            dst_ref=full.at[source, pl.ds(0, count)],
            send_sem=s1.at[0, 0],
            recv_sem=r1.at[source, sender],
            device_id={"mode": lax.rem(m + 1, SPLIT)},
            device_id_type=MESH,
        ).wait_recv()

    def forward(source, step):
        rows = pl.ds(pl.multiple_of(m * PIECE, PIECE), PIECE)
        return pltpu.make_async_remote_copy(
            src_ref=full.at[source, rows],
            dst_ref=full.at[source, rows],
            send_sem=s2.at[source, step],
            recv_sem=r2.at[source, m],
            device_id={"mode": lax.rem(m + step, SPLIT)},
            device_id_type=MESH,
        )

    for back in (1, 2, 3, 0):
        source = lax.rem(q + SPLIT - back, SPLIT)

        if back > 0:

            @pl.when(m == 0)
            def _():
                piece_wait(source, PIECE, 0)

        @pl.when((m == 1) | (m == 2))
        def _():
            piece_wait(source, PIECE, 0)

        @pl.when(m == 3)
        def _():
            piece_wait(source, head_last, 0)
            piece_wait(source, PACK - HEAD, 1)

        for step in range(1, SPLIT):
            forward(source, step).start()

    @pl.when(m < 2)
    def _():
        halo(1).start()

    @pl.when(m == 2)
    def _():
        halo(0).start()

    degree_c = lax.broadcasted_iota(jnp.int32, (NVZ, 1), 0)
    sqrt_c = jnp.sqrt(degree_c.astype(F32))
    sqrt_c_up = jnp.where(degree_c == NVZ - 1, 0.0, jnp.sqrt(degree_c.astype(F32) + 1.0))
    planes = SPLIT * LANES // NY

    def own_terms(i, carry):
        slot = i // PER_VX
        a = lax.rem(i, PER_VX)
        scale = nu_step * th_ref[slot]
        relax = dt_step * rx_ref[slot]
        blocks = [
            load(slot, pl.ds(pl.multiple_of(a * 64 + b * NVZ, NVZ), NVZ)) for b in range(NVY)
        ]
        for b in range(NVY):
            here = blocks[b]
            flux_y = jnp.zeros_like(here)
            if b < NVY - 1:
                flux_y = flux_y + float(np.sqrt(np.float32(b + 1))) * blocks[b + 1]
            if b > 0:
                flux_y = flux_y + float(np.sqrt(np.float32(b))) * blocks[b - 1]
            up_y = 0.5 * flux_y - 0.5 * bound_y * here
            down_y = -0.5 * flux_y - 0.5 * bound_y * here
            turned = []
            for plane in range(planes):
                cut = slice(plane * NY, (plane + 1) * NY)
                turned.append(
                    pltpu.roll(up_y[:, cut], NY - 1, 1) + pltpu.roll(down_y[:, cut], 1, 1)
                )
            y_term = jnp.concatenate(turned, axis=1) + bound_y * here
            flux_z = sqrt_c_up * pltpu.roll(here, NVZ - 1, 0) + sqrt_c * pltpu.roll(here, 1, 0)
            wide = planes * NY
            up_z = 0.5 * flux_z - 0.5 * bound_z * here
            down_z = -0.5 * flux_z - 0.5 * bound_z * here
            z_term = (
                pltpu.roll(up_z, wide - NY, 1) + pltpu.roll(down_z, NY, 1) + bound_z * here
            )
            total = degree_c + (b + a + m * PER_VX)
            lost = jnp.where(total > DEG, relax, 0.0)
            value = here - scale * (y_term + z_term + bound_x * here) - lost * here
            rows = pl.ds(pl.multiple_of(a * 64 + b * NVZ, NVZ), NVZ)
            for part in range(SPLIT):
                out_ref[part, slot, rows, :] = value[:, part * LANES : (part + 1) * LANES]
        return carry

    lax.fori_loop(0, OWN * PER_VX, own_terms, 0)

    def degree_roots(a):
        degree = (m * PER_VX + a).astype(F32)
        below = jnp.sqrt(jnp.full((8, 128), degree, F32))[0:1, 0:1]
        above = jnp.sqrt(jnp.full((8, 128), degree + 1.0, F32))[0:1, 0:1]
        return below, above

    def x_parts(a):
        root, root_up = degree_roots(a)

        def part(i, carry):
            slot = i // 4
            r = lax.rem(i, 4) * 16
            here = load(slot, pl.ds(pl.multiple_of(a * 64 + r, 16), 16))
            flux = jnp.zeros_like(here)
            if a < PER_VX - 1:
                flux = flux + root_up * load(slot, pl.ds(pl.multiple_of((a + 1) * 64 + r, 16), 16))
            if a > 0:
                flux = flux + root * load(slot, pl.ds(pl.multiple_of((a - 1) * 64 + r, 16), 16))
            rows = pl.ds(pl.multiple_of(slot * 64 + r, 16), 16)
            ab_send[0, a, rows, :] = (0.5 * flux - 0.5 * bound_x * here).astype(ab_send.dtype)
            ab_send[1, a, rows, :] = (-0.5 * flux - 0.5 * bound_x * here).astype(ab_send.dtype)
            return carry

        lax.fori_loop(0, OWN * 4, part, 0)

    def layer(way, a):
        return pltpu.make_async_remote_copy(
            src_ref=ab_send.at[way, a],
            dst_ref=ab_recv.at[way, a],
            send_sem=xs.at[way, a],
            recv_sem=xr.at[way, a],
            device_id={"space": sx - 1 if way == 0 else sx + 1},
            device_id_type=MESH,
        )

    def send_layers(a):
        @pl.when(sx > 0)
        def _():
            layer(0, a).start()

        @pl.when(sx < space_count - 1)
        def _():
            layer(1, a).start()

    @pl.when(sx == space_count - 1)
    def _():
        ab_recv[0] = jnp.zeros(ab_recv.shape[1:], ab_recv.dtype)
        edge_recv[0] = jnp.zeros(edge_recv.shape[1:], BF16)

    @pl.when(sx == 0)
    def _():
        ab_recv[1] = jnp.zeros(ab_recv.shape[1:], ab_recv.dtype)
        edge_recv[1] = jnp.zeros(edge_recv.shape[1:], BF16)

    for a in range(PER_VX):
        x_parts(a)
        send_layers(a)

    def forward_wait(source, step):
        sender = lax.rem(m + step, SPLIT)
        pltpu.make_async_remote_copy(
            src_ref=full.at[source, pl.ds(0, PIECE)],
            dst_ref=full.at[source, pl.ds(0, PIECE)],
            send_sem=s2.at[source, step],
            recv_sem=r2.at[source, sender],
            device_id={"mode": sender},
            device_id_type=MESH,
        ).wait_recv()

    for back in (1, 2, 3, 0):
        source = lax.rem(q + SPLIT - back, SPLIT)
        for step in range(1, SPLIT):
            forward_wait(source, step)
        picked = dot(pick[...], full[source])
        for slot in range(OWN):
            low[source, :, slot * LANES : (slot + 1) * LANES] = picked[
                slot * PAD_J : (slot + 1) * PAD_J
            ]

    def of_species(r):
        return low[r // OWN, :, (r % OWN) * LANES : (r % OWN + 1) * LANES]

    everyone = of_species(0)
    for r in range(1, SPLIT * OWN):
        everyone = everyone + of_species(r)
    total[...] = everyone

    def partners(pair):
        def one(slot):
            first = jnp.zeros((PAD_J, LANES), F32)
            for r in range(SPLIT * OWN):
                weight = jnp.where(kind_ref[pair * OWN + slot, r] == 0, 1.0, 0.0)
                first = first + weight * of_species(r)
            cut = slice(slot * LANES, (slot + 1) * LANES)
            pmat[pair, 0:PAD_J, cut] = first.astype(BF16)
            pmat[pair, PAD_J:, cut] = (total[...] - first).astype(BF16)

        for slot in range(OWN):
            one(slot)

    def give(pair, target):
        return pltpu.make_async_remote_copy(
            src_ref=gsend.at[pair],
            dst_ref=grecv.at[q, pl.ds(pl.multiple_of(m * PAD_N, PAD_N), PAD_N)],
            send_sem=s3.at[pair, target],
            recv_sem=r3.at[q, m],
            device_id={"species": pair, "mode": target},
            device_id_type=MESH,
        )

    def collide(pair):
        product = dot(k2[...].reshape(PAD_N * PAD_J, NKIND * PAD_J), pmat[pair])
        own = low[pair]
        gained = jnp.sum(product.reshape(PAD_N, PAD_J, OWN * LANES) * own[None], axis=1)
        gsend[pair] = gained.astype(BF16)

    for step in (1, 2, 3, 0):
        pair = lax.rem(q + step, SPLIT)
        partners(pair)
        collide(pair)
        for target in range(2):
            if step > 0:
                give(pair, target).start()
            else:

                @pl.when(m != target)
                def _():
                    give(pair, target).start()

                @pl.when(m == target)
                def _():
                    grecv[q, target * PAD_N : (target + 1) * PAD_N, :] = gsend[pair]

    @pl.when(m > 0)
    def _():
        halo(1).wait_recv()

    @pl.when(m == 0)
    def _():
        halo_recv[0] = jnp.zeros(halo_recv.shape[1:], BF16)

    @pl.when(m < SPLIT - 1)
    def _():
        halo(0).wait_recv()

    @pl.when(m == SPLIT - 1)
    def _():
        halo_recv[1] = jnp.zeros(halo_recv.shape[1:], BF16)

    def edges(way):
        return pltpu.make_async_remote_copy(
            src_ref=halo_recv,
            dst_ref=edge_recv.at[way],
            send_sem=es.at[way],
            recv_sem=er.at[way],
            device_id={"space": sx - 1 if way == 0 else sx + 1},
            device_id_type=MESH,
        )

    @pl.when(sx > 0)
    def _():
        edges(0).start()

    @pl.when(sx < space_count - 1)
    def _():
        edges(1).start()

    for a in range(PER_VX):

        @pl.when(sx < space_count - 1)
        def _():
            layer(0, a).wait_recv()

        @pl.when(sx > 0)
        def _():
            layer(1, a).wait_recv()

    @pl.when(sx < space_count - 1)
    def _():
        edges(0).wait_recv()

    @pl.when(sx > 0)
    def _():
        edges(1).wait_recv()

    for a in range(PER_VX):
        root, root_up = degree_roots(a)

        def add_x(i, carry):
            slot = i // 4
            r = pl.multiple_of(lax.rem(i, 4) * 16, 16)
            rows = pl.ds(pl.multiple_of(slot * 64 + r, 16), 16)
            here = pl.ds(pl.multiple_of(a * 64 + r, 16), 16)
            term = ab_recv[0, a, rows, :] + ab_recv[1, a, rows, :]
            side = {0: 0, PER_VX - 1: 1}.get(a)
            if side is not None:
                up = edge_recv[0, side, slot, pl.ds(r, 16), :].astype(F32)
                down = edge_recv[1, side, slot, pl.ds(r, 16), :].astype(F32)
                term = term + (0.5 * (root_up if side else root)) * (up - down)
            term = (nu_step * th_ref[slot]) * term
            for part in range(SPLIT):
                out_ref[part, slot, here, :] = (
                    out_ref[part, slot, here, :] - term[:, part * LANES : (part + 1) * LANES]
                )
            return carry

        lax.fori_loop(0, OWN * 4, add_x, 0)

    def column_out(part, slot):
        return pltpu.make_async_copy(
            out_ref.at[part, slot],
            result.at[slot, :, 0, pl.ds(pl.multiple_of(part * LANES, LANES), LANES)],
            copy_sem.at[part, slot],
        )

    @pl.when(m >= 2)
    def _():
        for part in range(SPLIT):
            for slot in range(OWN):
                column_out(part, slot).start()

    @pl.when(m < 2)
    def _():
        for back in (1, 2, 3, 0):
            source = lax.rem(q + SPLIT - back, SPLIT)
            for sender in range(SPLIT):

                def take():
                    pltpu.make_async_remote_copy(
                        src_ref=gsend.at[0],
                        dst_ref=grecv.at[source, pl.ds(sender * PAD_N, PAD_N)],
                        send_sem=s3.at[0, 0],
                        recv_sem=r3.at[source, sender],
                        device_id={"mode": lax.rem(m + 1, SPLIT)},
                        device_id_type=MESH,
                    ).wait_recv()

                if back > 0 or sender > 1:
                    take()
                else:
                    pl.when(m != sender)(take)
            gained = dot(spread[...], grecv[source])
            for slot in range(OWN):
                out_ref[source, slot] = (
                    out_ref[source, slot] + dt_step * gained[:, slot * LANES : (slot + 1) * LANES]
                )
                column_out(source, slot).start()

    @pl.when(m == 0)
    def _():
        for step in range(SPLIT):
            for item in head_copies(step):
                item.wait_send()

    @pl.when(m == 1)
    def _():
        for step in range(SPLIT):
            tail_copies(step).wait_send()

    for back in range(SPLIT):
        for step in range(1, SPLIT):
            forward(lax.rem(q + SPLIT - back, SPLIT), step).wait_send()

    @pl.when(m > 0)
    def _():
        halo(0).wait_send()

    @pl.when(m < SPLIT - 1)
    def _():
        halo(1).wait_send()

    for a in range(PER_VX):

        @pl.when(sx > 0)
        def _():
            layer(0, a).wait_send()

        @pl.when(sx < space_count - 1)
        def _():
            layer(1, a).wait_send()

    @pl.when(sx > 0)
    def _():
        edges(0).wait_send()

    @pl.when(sx < space_count - 1)
    def _():
        edges(1).wait_send()

    for step in range(SPLIT):
        pair = lax.rem(q + step, SPLIT)
        for target in range(2):
            if step > 0:
                give(pair, target).wait_send()
            else:

                @pl.when(m != target)
                def _():
                    give(pair, target).wait_send()

    for part in range(SPLIT):
        for slot in range(OWN):
            column_out(part, slot).wait()


def write_out(source, result, held, sems):
    count = sems.shape[1]
    rows = result.shape[1] // count

    def move(src, dst, way, piece):
        cut = pl.ds(piece * rows, rows)
        return pltpu.make_async_copy(src.at[:, cut], dst.at[:, cut], sems.at[way, piece])

    for piece in range(count):
        move(source, held, 0, piece).start()
    for piece in range(count):
        move(source, held, 0, piece).wait()
        move(held, result, 1, piece).start()
    for piece in range(count):
        move(held, result, 1, piece).wait()


def per_device(space_count, distribution, kernels, pair_kind, low_map, thermal_speed, relax_rate):
    own, rows, layers, cells = distribution.shape
    assert (own, rows, layers, cells) == (OWN, ROWS, 1, SPLIT * LANES)
    kinds, _, low_count, _ = kernels.shape
    table = jnp.asarray(packed_table())
    anywhere = pl.BlockSpec(memory_space=pl.ANY)
    dma = pltpu.SemaphoreType.DMA
    ab_type = F32
    stepped = pl.pallas_call(
        functools.partial(kernel, space_count),
        out_shape=jax.ShapeDtypeStruct(distribution.shape, F32),
        in_specs=[anywhere] * 7,
        out_specs=anywhere,
        scratch_shapes=[
            pltpu.VMEM((SPLIT, own, rows, LANES), F32),
            pltpu.VMEM((SPLIT, own, rows, LANES), F32),
            pltpu.VMEM(table.shape, jnp.int32),
            pltpu.VMEM((1, low_count), jnp.int32),
            pltpu.SMEM(pair_kind.shape, jnp.int32),
            pltpu.SMEM(thermal_speed.shape, F32),
            pltpu.SMEM(relax_rate.shape, F32),
            pltpu.VMEM(kernels.shape, BF16),
            pltpu.VMEM((PAD_N, PAD_J, kinds * PAD_J), BF16),
            pltpu.VMEM((SPLIT, PACK, LANES), BF16),
            pltpu.VMEM((SPLIT, PACK, LANES), BF16),
            pltpu.VMEM((SPLIT, PAD_J, own * LANES), F32),
            pltpu.VMEM((SPLIT, kinds * PAD_J, own * LANES), BF16),
            pltpu.VMEM((PAD_J, LANES), F32),
            pltpu.VMEM((SPLIT, PAD_N, own * LANES), BF16),
            pltpu.VMEM((SPLIT, SPLIT * PAD_N, own * LANES), BF16),
            pltpu.VMEM((own * PAD_J, PACK), BF16),
            pltpu.VMEM((ROWS, PAD_J), BF16),
            pltpu.VMEM((2, own, 64, cells), BF16),
            pltpu.VMEM((2, own, 64, cells), BF16),
            pltpu.VMEM((2, 2, own, 64, cells), BF16),
            pltpu.VMEM((2, PER_VX, own * 64, cells), ab_type),
            pltpu.VMEM((2, PER_VX, own * 64, cells), ab_type),
            dma((SPLIT, OWN)),
            dma((6,)),
            dma((SPLIT, SPLIT)),
            dma((SPLIT, 2)),
            dma((SPLIT, SPLIT)),
            dma((SPLIT, SPLIT)),
            dma((SPLIT, 2)),
            dma((SPLIT, SPLIT)),
            dma((2,)),
            dma((2,)),
            dma((2, PER_VX)),
            dma((2, PER_VX)),
            dma((2,)),
            dma((2,)),
        ],
        compiler_params=pltpu.CompilerParams(
            collective_id=0, has_side_effects=True, vmem_limit_bytes=60 * 1024 * 1024
        ),
    )(
        distribution,
        kernels,
        table,
        low_map.reshape(1, low_count),
        pair_kind,
        thermal_speed,
        relax_rate,
    )
    return pl.pallas_call(
        write_out,
        out_shape=jax.ShapeDtypeStruct(distribution.shape, F32),
        in_specs=[anywhere],
        out_specs=anywhere,
        scratch_shapes=[pltpu.VMEM(distribution.shape, F32), dma((2, 8))],
        compiler_params=pltpu.CompilerParams(vmem_limit_bytes=60 * 1024 * 1024),
    )(stepped)


def solution(mesh):
    in_specs = (
        P("species", "mode", "space", None),
        P(None, "mode", None, None),
        P(),
        P(),
        P("species"),
        P("species"),
    )
    out_specs = P("species", "mode", "space", None)
    return jax.shard_map(
        functools.partial(per_device, mesh.shape["space"]),
        mesh=mesh,
        in_specs=in_specs,
        out_specs=out_specs,
        check_vma=False,
    )
```

```python
import functools

import jax
import jax.numpy as jnp
import numpy as np
from jax import lax
from jax.experimental import pallas as pl
from jax.experimental.pallas import tpu as pltpu
from jax.sharding import PartitionSpec as P

MESH = pl.DeviceIdType.MESH
F32 = jnp.float32
BF16 = jnp.bfloat16

NVY = 8
NVZ = 8
DEG = 7
NKIND = 2
NY = 256

nu_step = 0.0625
dt_step = 0.05
bound_x = 6.7
bound_y = 4.2
bound_z = 4.2

SPLIT = 4
OWN = 2
ROWS = 256
PER_VX = 4
LANES = 128
HEAD = 208
PACK = 256
PIECE = 64
PAD_J = 128
PAD_N = 32


def packed_table():
    low = [
        (a * NVY + b) * NVZ + c
        for a in range(DEG + 1)
        for b in range(NVY)
        for c in range(NVZ)
        if a + b + c <= DEG
    ]
    table = np.full((PACK, 8), -1, np.int32)
    for start, first in ((0, 0), (HEAD, ROWS)):
        held = [mode for mode in low if first <= mode < first + ROWS]
        row = start
        for slot in range(OWN):
            for mode in held:
                table[row, 0] = slot * ROWS + mode - first
                table[row, 1 + slot] = mode
                table[row, 3] = first // ROWS
                row += 1
        assert row <= (HEAD if start == 0 else PACK)
    return table


def each(count, body):
    lax.fori_loop(0, count, lambda i, carry: (body(i), carry)[1], 0)


def dot(left, right):
    return jnp.dot(left, right, preferred_element_type=F32)


def kernel(
    space_count,
    f_in,
    k_in,
    tab_in,
    map_in,
    kind_in,
    th_in,
    rx_in,
    result,
    f_ref,
    out_ref,
    tab_ref,
    lm_ref,
    kind_ref,
    th_ref,
    rx_ref,
    kraw,
    k2,
    low_send,
    full,
    low,
    pmat,
    gsum,
    total,
    gsend,
    grecv,
    pick,
    spread,
    chooser,
    halo_send,
    halo_recv,
    edge_recv,
    ab_send,
    ab_recv,
    copy_sem,
    small_sem,
    s1,
    r1,
    s2,
    r2,
    s3,
    r3,
    hs,
    hr,
    xs,
    xr,
    es,
    er,
):
    q = lax.axis_index("species")
    m = lax.axis_index("mode")
    sx = lax.axis_index("space")

    columns_in = [
        pltpu.make_async_copy(
            f_in.at[slot, :, 0, pl.ds(part * LANES, LANES)],
            f_ref.at[part, slot],
            copy_sem.at[part, slot],
        )
        for part in range(SPLIT)
        for slot in range(OWN)
    ]
    small = [
        pltpu.make_async_copy(tab_in, tab_ref, small_sem.at[0]),
        pltpu.make_async_copy(map_in, lm_ref, small_sem.at[1]),
        pltpu.make_async_copy(kind_in, kind_ref, small_sem.at[2]),
        pltpu.make_async_copy(th_in, th_ref, small_sem.at[3]),
        pltpu.make_async_copy(rx_in, rx_ref, small_sem.at[4]),
    ]
    copy_k = pltpu.make_async_copy(k_in, kraw, small_sem.at[5])
    for item in columns_in + small[:1]:
        item.start()

    barrier = pltpu.get_barrier_semaphore()
    def greet(step):
        other = lax.rem(q * SPLIT + m + 1 + step, SPLIT * SPLIT)
        pl.semaphore_signal(
            barrier,
            inc=1,
            device_id={"species": other // SPLIT, "mode": lax.rem(other, SPLIT)},
            device_id_type=MESH,
        )

    each(SPLIT * SPLIT - 1, greet)

    @pl.when(sx > 0)
    def _():
        pl.semaphore_signal(barrier, inc=1, device_id={"space": sx - 1}, device_id_type=MESH)

    @pl.when(sx < space_count - 1)
    def _():
        pl.semaphore_signal(barrier, inc=1, device_id={"space": sx + 1}, device_id_type=MESH)

    for item in small[1:] + [copy_k]:
        item.start()
    for item in columns_in + small[:1]:
        item.wait()

    def load(slot, rows):
        return jnp.concatenate([f_ref[part, slot, rows, :] for part in range(SPLIT)], axis=1)

    @pl.when(m < 2)
    def _():
        rows = lax.broadcasted_iota(jnp.int32, (PACK, OWN * ROWS), 1)
        chosen = (tab_ref[:, 0:1] == rows) & (tab_ref[:, 3:4] == m)
        chooser[...] = jnp.where(chosen, 1.0, 0.0).astype(BF16)

        def extract(part):
            field = f_ref[part].reshape(OWN * ROWS, LANES).astype(BF16)
            low_send[part] = dot(chooser[...], field).astype(BF16)

        each(SPLIT, extract)

    inner = (sx > 0) & (sx < space_count - 1)
    peers = SPLIT * SPLIT - 1

    @pl.when(inner)
    def _():
        pl.semaphore_wait(barrier, peers + 2)

    @pl.when(jnp.logical_not(inner))
    def _():
        pl.semaphore_wait(barrier, peers + min(1, space_count - 1))

    def scatter(part, piece, first, count, source):
        return pltpu.make_async_remote_copy(
            src_ref=low_send.at[part, pl.ds(first, count)],
            dst_ref=full.at[q, pl.ds(first, count)],
            send_sem=s1.at[part, piece],
            recv_sem=r1.at[q, source],
            device_id={"species": part, "mode": piece},
            device_id_type=MESH,
        )

    head_last = HEAD - 3 * PIECE

    def head_copies(act):
        def one(i):
            part = lax.rem(q + 1 + i // 3, SPLIT)
            piece = lax.rem(i, 3)

            @pl.when((part != q) | (piece != 0))
            def _():
                act(scatter(part, piece, pl.multiple_of(piece * PIECE, PIECE), PIECE, 0))

        each(SPLIT * 3, one)
        each(
            SPLIT,
            lambda i: act(scatter(lax.rem(q + 1 + i, SPLIT), 3, 3 * PIECE, head_last, 0)),
        )

    def tail_copies(act):
        each(
            SPLIT,
            lambda i: act(scatter(lax.rem(q + 1 + i, SPLIT), 3, HEAD, PACK - HEAD, 1)),
        )

    def start(item):
        item.start()

    def sent(item):
        item.wait_send()

    @pl.when(m == 0)
    def _():
        head_copies(start)
        full[q, 0:PIECE, :] = low_send[q, 0:PIECE, :]

    @pl.when(m == 1)
    def _():
        tail_copies(start)

    def narrow(i):
        slot = i // 4
        r = pl.multiple_of(lax.rem(i, 4) * 16, 16)
        for way in range(2):
            plane = load(slot, pl.ds(way * (ROWS - 64) + r, 16))
            halo_send[way, slot, pl.ds(r, 16), :] = plane.astype(BF16)

    each(OWN * 4, narrow)

    def halo(way):
        return pltpu.make_async_remote_copy(
            src_ref=halo_send.at[way],
            dst_ref=halo_recv.at[1 - way],
            send_sem=hs.at[way],
            recv_sem=hr.at[1 - way],
            device_id={"mode": m - 1 if way == 0 else m + 1},
            device_id_type=MESH,
        )

    @pl.when((m == 1) | (m == 3))
    def _():
        halo(0).start()

    @pl.when(m == 2)
    def _():
        halo(1).start()

    for item in small[1:] + [copy_k]:
        item.wait()

    def lay(n, carry):
        k2[n] = jnp.zeros((PAD_J, NKIND * PAD_J), BF16)

        @pl.when(n < kraw.shape[1])
        def _():
            spot = jnp.minimum(n, kraw.shape[1] - 1)
            for kind in range(NKIND):
                k2[n, 0 : kraw.shape[2], kind * PAD_J : kind * PAD_J + kraw.shape[3]] = kraw[
                    kind, spot
                ]

        return carry

    lax.fori_loop(0, PAD_N, lay, 0)

    lanes = lax.broadcasted_iota(jnp.int32, (8, PAD_J), 1)
    low_count = kraw.shape[2]
    block_rows = kraw.shape[1]
    ordered = jnp.concatenate(
        [lm_ref[...], jnp.full((1, PAD_J - low_count), -2, jnp.int32)], axis=1
    )
    ordered = jnp.broadcast_to(ordered, (8, PAD_J))
    by_block = jnp.full((8, PAD_J), -2, jnp.int32)
    for block in range(SPLIT):
        moved = ordered
        if block > 0:
            moved = pltpu.roll(ordered, block * (PAD_N - block_rows), 1)
        inside = (lanes >= block * PAD_N) & (lanes < block * PAD_N + block_rows)
        by_block = jnp.where(inside, moved, by_block)
    for slot in range(OWN):
        same = tab_ref[:, 1 + slot : 2 + slot] == ordered[0:1, :]
        pick[slot * PAD_J : (slot + 1) * PAD_J, :] = jnp.where(same, 1.0, 0.0).T.astype(BF16)
    mode_of = lax.broadcasted_iota(jnp.int32, (ROWS, PAD_J), 0) + m * ROWS
    spread[...] = jnp.where(mode_of == by_block[0:1, :], 1.0, 0.0).astype(BF16)

    def piece_wait(source, count, sender):
        pltpu.make_async_remote_copy(
            src_ref=low_send.at[0, pl.ds(0, count)],
            dst_ref=full.at[source, pl.ds(0, count)],
            send_sem=s1.at[0, 0],
            recv_sem=r1.at[source, sender],
            device_id={"mode": lax.rem(m + 1, SPLIT)},
            device_id_type=MESH,
        ).wait_recv()

    def forward(source, step):
        rows = pl.ds(pl.multiple_of(m * PIECE, PIECE), PIECE)
        return pltpu.make_async_remote_copy(
            src_ref=full.at[source, rows],
            dst_ref=full.at[source, rows],
            send_sem=s2.at[source, step],
            recv_sem=r2.at[source, m],
            device_id={"mode": lax.rem(m + step, SPLIT)},
            device_id_type=MESH,
        )

    def pass_on(i):
        source = lax.rem(q + 2 * SPLIT - 1 - i, SPLIT)

        @pl.when((m < 3) & ((m > 0) | (source != q)))
        def _():
            piece_wait(source, PIECE, 0)

        @pl.when(m == 3)
        def _():
            piece_wait(source, head_last, 0)
            piece_wait(source, PACK - HEAD, 1)

        each(SPLIT - 1, lambda step: forward(source, step + 1).start())

    each(SPLIT, pass_on)

    @pl.when(m < 2)
    def _():
        halo(1).start()

    @pl.when(m == 2)
    def _():
        halo(0).start()

    degree_c = lax.broadcasted_iota(jnp.int32, (NVZ, 1), 0)
    sqrt_c = jnp.sqrt(degree_c.astype(F32))
    sqrt_c_up = jnp.where(degree_c == NVZ - 1, 0.0, jnp.sqrt(degree_c.astype(F32) + 1.0))
    planes = SPLIT * LANES // NY

    def own_terms(i, carry):
        slot = i // PER_VX
        a = lax.rem(i, PER_VX)
        scale = nu_step * th_ref[slot]
        relax = dt_step * rx_ref[slot]
        blocks = [
            load(slot, pl.ds(pl.multiple_of(a * 64 + b * NVZ, NVZ), NVZ)) for b in range(NVY)
        ]
        for b in range(NVY):
            here = blocks[b]
            flux_y = jnp.zeros_like(here)
            if b < NVY - 1:
                flux_y = flux_y + float(np.sqrt(np.float32(b + 1))) * blocks[b + 1]
            if b > 0:
                flux_y = flux_y + float(np.sqrt(np.float32(b))) * blocks[b - 1]
            up_y = 0.5 * flux_y - 0.5 * bound_y * here
            down_y = -0.5 * flux_y - 0.5 * bound_y * here
            turned = []
            for plane in range(planes):
                cut = slice(plane * NY, (plane + 1) * NY)
                turned.append(
                    pltpu.roll(up_y[:, cut], NY - 1, 1) + pltpu.roll(down_y[:, cut], 1, 1)
                )
            y_term = jnp.concatenate(turned, axis=1) + bound_y * here
            flux_z = sqrt_c_up * pltpu.roll(here, NVZ - 1, 0) + sqrt_c * pltpu.roll(here, 1, 0)
            wide = planes * NY
            up_z = 0.5 * flux_z - 0.5 * bound_z * here
            down_z = -0.5 * flux_z - 0.5 * bound_z * here
            z_term = (
                pltpu.roll(up_z, wide - NY, 1) + pltpu.roll(down_z, NY, 1) + bound_z * here
            )
            total = degree_c + (b + a + m * PER_VX)
            lost = jnp.where(total > DEG, relax, 0.0)
            value = here - scale * (y_term + z_term + bound_x * here) - lost * here
            rows = pl.ds(pl.multiple_of(a * 64 + b * NVZ, NVZ), NVZ)
            for part in range(SPLIT):
                out_ref[part, slot, rows, :] = value[:, part * LANES : (part + 1) * LANES]
        return carry

    lax.fori_loop(0, OWN * PER_VX, own_terms, 0)

    def degree_roots(a):
        degree = jnp.asarray(m * PER_VX + a, jnp.int32).astype(F32)
        below = jnp.sqrt(jnp.full((8, 128), degree, F32))[0:1, 0:1]
        above = jnp.sqrt(jnp.full((8, 128), degree + 1.0, F32))[0:1, 0:1]
        return below, above

    def x_parts(a):
        root, root_up = degree_roots(a)
        root_up = jnp.where(a < PER_VX - 1, root_up, 0.0)
        root = jnp.where(a > 0, root, 0.0)
        above = jnp.minimum(a + 1, PER_VX - 1) * 64
        below = jnp.maximum(a - 1, 0) * 64

        def part(i):
            slot = i // 4
            r = lax.rem(i, 4) * 16
            here = load(slot, pl.ds(pl.multiple_of(a * 64 + r, 16), 16))
            flux = root_up * load(slot, pl.ds(pl.multiple_of(above + r, 16), 16))
            flux = flux + root * load(slot, pl.ds(pl.multiple_of(below + r, 16), 16))
            rows = pl.ds(pl.multiple_of(slot * 64 + r, 16), 16)
            ab_send[0, a, rows, :] = 0.5 * flux - 0.5 * bound_x * here
            ab_send[1, a, rows, :] = -0.5 * flux - 0.5 * bound_x * here

        each(OWN * 4, part)

    def layer(way, a):
        return pltpu.make_async_remote_copy(
            src_ref=ab_send.at[way, a],
            dst_ref=ab_recv.at[way, a],
            send_sem=xs.at[way, a],
            recv_sem=xr.at[way, a],
            device_id={"space": sx - 1 if way == 0 else sx + 1},
            device_id_type=MESH,
        )

    def send_layers(a):
        @pl.when(sx > 0)
        def _():
            layer(0, a).start()

        @pl.when(sx < space_count - 1)
        def _():
            layer(1, a).start()

    def clear(way):
        def one(i):
            wide = ab_recv.shape[2:]
            ab_recv[way, i // 8, pl.ds(pl.multiple_of(lax.rem(i, 8) * 16, 16), 16), :] = jnp.zeros(
                (16, wide[1]), F32
            )

        each(PER_VX * 8, one)

        def edge(i):
            edge_recv[way, i // OWN, lax.rem(i, OWN)] = jnp.zeros(edge_recv.shape[3:], BF16)

        each(2 * OWN, edge)

    @pl.when(sx == space_count - 1)
    def _():
        clear(0)

    @pl.when(sx == 0)
    def _():
        clear(1)

    def out_layers(a):
        x_parts(a)
        send_layers(a)

    each(PER_VX, out_layers)

    def forward_wait(source, step):
        sender = lax.rem(m + step, SPLIT)
        pltpu.make_async_remote_copy(
            src_ref=full.at[source, pl.ds(0, PIECE)],
            dst_ref=full.at[source, pl.ds(0, PIECE)],
            send_sem=s2.at[source, step],
            recv_sem=r2.at[source, sender],
            device_id={"mode": sender},
            device_id_type=MESH,
        ).wait_recv()

    def arrive(i):
        source = lax.rem(q + 2 * SPLIT - 1 - i, SPLIT)
        each(SPLIT - 1, lambda step: forward_wait(source, step + 1))
        picked = dot(pick[...], full[source])
        for slot in range(OWN):
            low[source, :, slot * LANES : (slot + 1) * LANES] = picked[
                slot * PAD_J : (slot + 1) * PAD_J
            ]

    each(SPLIT, arrive)

    def of_species(r):
        return low[r // OWN, :, (r % OWN) * LANES : (r % OWN + 1) * LANES]

    everyone = of_species(0)
    for r in range(1, SPLIT * OWN):
        everyone = everyone + of_species(r)
    total[...] = everyone

    def partners(pair):
        def one(slot):
            first = jnp.zeros((PAD_J, LANES), F32)
            for r in range(SPLIT * OWN):
                weight = jnp.where(kind_ref[pair * OWN + slot, r] == 0, 1.0, 0.0)
                first = first + weight * of_species(r)
            cut = slice(slot * LANES, (slot + 1) * LANES)
            pmat[pair, 0:PAD_J, cut] = first.astype(BF16)
            pmat[pair, PAD_J:, cut] = (total[...] - first).astype(BF16)

        for slot in range(OWN):
            one(slot)

    def give(pair, target):
        return pltpu.make_async_remote_copy(
            src_ref=gsend.at[pair],
            dst_ref=grecv.at[q, pl.ds(pl.multiple_of(m * PAD_N, PAD_N), PAD_N)],
            send_sem=s3.at[pair, target],
            recv_sem=r3.at[q, m],
            device_id={"species": pair, "mode": target},
            device_id_type=MESH,
        )

    group = 8

    def collide(pair):
        def some(i, carry):
            left = k2[pl.ds(pl.multiple_of(i * group, group), group)]
            product = dot(left.reshape(group * PAD_J, NKIND * PAD_J), pmat[pair])
            own = low[pair]
            gsum[pl.ds(pl.multiple_of(i * group, group), group), :] = jnp.sum(
                product.reshape(group, PAD_J, OWN * LANES) * own[None], axis=1
            )
            return carry

        lax.fori_loop(0, PAD_N // group, some, 0)
        gsend[pair] = gsum[...].astype(BF16)

    def results(i):
        pair = lax.rem(q + 1 + i, SPLIT)
        partners(pair)
        collide(pair)

        def to(target):
            @pl.when((pair != q) | (m != target))
            def _():
                give(pair, target).start()

        each(2, to)

    each(SPLIT, results)

    @pl.when(m < 2)
    def _():
        grecv[q, pl.ds(pl.multiple_of(m * PAD_N, PAD_N), PAD_N), :] = gsend[q]

    @pl.when(m > 0)
    def _():
        halo(1).wait_recv()

    @pl.when(m == 0)
    def _():
        halo_recv[0] = jnp.zeros(halo_recv.shape[1:], BF16)

    @pl.when(m < SPLIT - 1)
    def _():
        halo(0).wait_recv()

    @pl.when(m == SPLIT - 1)
    def _():
        halo_recv[1] = jnp.zeros(halo_recv.shape[1:], BF16)

    def edges(way):
        return pltpu.make_async_remote_copy(
            src_ref=halo_recv,
            dst_ref=edge_recv.at[way],
            send_sem=es.at[way],
            recv_sem=er.at[way],
            device_id={"space": sx - 1 if way == 0 else sx + 1},
            device_id_type=MESH,
        )

    @pl.when(sx > 0)
    def _():
        edges(0).start()

    @pl.when(sx < space_count - 1)
    def _():
        edges(1).start()

    def spend(slot, rows, term):
        term = (nu_step * th_ref[slot]) * term
        for part in range(SPLIT):
            out_ref[part, slot, rows, :] = (
                out_ref[part, slot, rows, :] - term[:, part * LANES : (part + 1) * LANES]
            )

    def add_x(i):
        a = i // 8

        @pl.when((lax.rem(i, 8) == 0) & (sx < space_count - 1))
        def _():
            layer(0, a).wait_recv()

        @pl.when((lax.rem(i, 8) == 0) & (sx > 0))
        def _():
            layer(1, a).wait_recv()

        slot = lax.rem(i, 8) // 4
        r = lax.rem(i, 4) * 16
        rows = pl.ds(pl.multiple_of(slot * 64 + r, 16), 16)
        spend(
            slot,
            pl.ds(pl.multiple_of(a * 64 + r, 16), 16),
            ab_recv[0, a, rows, :] + ab_recv[1, a, rows, :],
        )

    each(PER_VX * 8, add_x)

    @pl.when(sx < space_count - 1)
    def _():
        edges(0).wait_recv()

    @pl.when(sx > 0)
    def _():
        edges(1).wait_recv()

    def add_edge(i):
        side = i // 8
        slot = lax.rem(i, 8) // 4
        r = pl.multiple_of(lax.rem(i, 4) * 16, 16)
        degree = jnp.asarray((m + side) * PER_VX, jnp.int32).astype(F32)
        half = 0.5 * jnp.sqrt(jnp.full((8, 128), degree, F32))[0:1, 0:1]
        up = edge_recv[0, side, slot, pl.ds(r, 16), :].astype(F32)
        down = edge_recv[1, side, slot, pl.ds(r, 16), :].astype(F32)
        spend(
            slot,
            pl.ds(pl.multiple_of(side * (ROWS - 64) + r, 16), 16),
            half * (up - down),
        )

    each(16, add_edge)

    def column_out(part, slot):
        return pltpu.make_async_copy(
            out_ref.at[part, slot],
            result.at[slot, :, 0, pl.ds(pl.multiple_of(part * LANES, LANES), LANES)],
            copy_sem.at[part, slot],
        )

    @pl.when(m >= 2)
    def _():
        each(SPLIT * OWN, lambda i: column_out(i // OWN, lax.rem(i, OWN)).start())

    def finish(i):
        source = lax.rem(q + 2 * SPLIT - 1 - i, SPLIT)

        def take(sender):
            @pl.when((source != q) | (m != sender))
            def _():
                pltpu.make_async_remote_copy(
                    src_ref=gsend.at[0],
                    dst_ref=grecv.at[
                        source, pl.ds(pl.multiple_of(sender * PAD_N, PAD_N), PAD_N)
                    ],
                    send_sem=s3.at[0, 0],
                    recv_sem=r3.at[source, sender],
                    device_id={"mode": lax.rem(m + 1, SPLIT)},
                    device_id_type=MESH,
                ).wait_recv()

        each(SPLIT, take)
        gained = dot(spread[...], grecv[source])
        for slot in range(OWN):
            out_ref[source, slot] = (
                out_ref[source, slot] + dt_step * gained[:, slot * LANES : (slot + 1) * LANES]
            )
            column_out(source, slot).start()

    @pl.when(m < 2)
    def _():
        each(SPLIT, finish)

    @pl.when(m == 0)
    def _():
        head_copies(sent)

    @pl.when(m == 1)
    def _():
        tail_copies(sent)

    each(
        SPLIT * (SPLIT - 1),
        lambda i: forward(i // (SPLIT - 1), lax.rem(i, SPLIT - 1) + 1).wait_send(),
    )

    @pl.when(m > 0)
    def _():
        halo(0).wait_send()

    @pl.when(m < SPLIT - 1)
    def _():
        halo(1).wait_send()

    @pl.when(sx > 0)
    def _():
        each(PER_VX, lambda a: layer(0, a).wait_send())

    @pl.when(sx < space_count - 1)
    def _():
        each(PER_VX, lambda a: layer(1, a).wait_send())

    @pl.when(sx > 0)
    def _():
        edges(0).wait_send()

    @pl.when(sx < space_count - 1)
    def _():
        edges(1).wait_send()

    def given(i):
        @pl.when((i // 2 != q) | (m != lax.rem(i, 2)))
        def _():
            give(i // 2, lax.rem(i, 2)).wait_send()

    each(SPLIT * 2, given)

    each(SPLIT * OWN, lambda i: column_out(i // OWN, lax.rem(i, OWN)).wait())


def write_out(source, result, held, sems):
    count = sems.shape[1]
    rows = result.shape[1] // count

    def move(src, dst, way, piece):
        cut = pl.ds(piece * rows, rows)
        return pltpu.make_async_copy(src.at[:, cut], dst.at[:, cut], sems.at[way, piece])

    for piece in range(count):
        move(source, held, 0, piece).start()
    for piece in range(count):
        move(source, held, 0, piece).wait()
        move(held, result, 1, piece).start()
    for piece in range(count):
        move(held, result, 1, piece).wait()


def per_device(space_count, distribution, kernels, pair_kind, low_map, thermal_speed, relax_rate):
    own, rows, layers, cells = distribution.shape
    assert (own, rows, layers, cells) == (OWN, ROWS, 1, SPLIT * LANES)
    kinds, _, low_count, _ = kernels.shape
    table = jnp.asarray(packed_table())
    anywhere = pl.BlockSpec(memory_space=pl.ANY)
    dma = pltpu.SemaphoreType.DMA
    ab_type = F32
    stepped = pl.pallas_call(
        functools.partial(kernel, space_count),
        out_shape=jax.ShapeDtypeStruct(distribution.shape, F32),
        in_specs=[anywhere] * 7,
        out_specs=anywhere,
        scratch_shapes=[
            pltpu.VMEM((SPLIT, own, rows, LANES), F32),
            pltpu.VMEM((SPLIT, own, rows, LANES), F32),
            pltpu.VMEM(table.shape, jnp.int32),
            pltpu.VMEM((1, low_count), jnp.int32),
            pltpu.SMEM(pair_kind.shape, jnp.int32),
            pltpu.SMEM(thermal_speed.shape, F32),
            pltpu.SMEM(relax_rate.shape, F32),
            pltpu.VMEM(kernels.shape, BF16),
            pltpu.VMEM((PAD_N, PAD_J, kinds * PAD_J), BF16),
            pltpu.VMEM((SPLIT, PACK, LANES), BF16),
            pltpu.VMEM((SPLIT, PACK, LANES), BF16),
            pltpu.VMEM((SPLIT, PAD_J, own * LANES), F32),
            pltpu.VMEM((SPLIT, kinds * PAD_J, own * LANES), BF16),
            pltpu.VMEM((PAD_N, own * LANES), F32),
            pltpu.VMEM((PAD_J, LANES), F32),
            pltpu.VMEM((SPLIT, PAD_N, own * LANES), BF16),
            pltpu.VMEM((SPLIT, SPLIT * PAD_N, own * LANES), BF16),
            pltpu.VMEM((own * PAD_J, PACK), BF16),
            pltpu.VMEM((ROWS, PAD_J), BF16),
            pltpu.VMEM((PACK, own * rows), BF16),
            pltpu.VMEM((2, own, 64, cells), BF16),
            pltpu.VMEM((2, own, 64, cells), BF16),
            pltpu.VMEM((2, 2, own, 64, cells), BF16),
            pltpu.VMEM((2, PER_VX, own * 64, cells), ab_type),
            pltpu.VMEM((2, PER_VX, own * 64, cells), ab_type),
            dma((SPLIT, OWN)),
            dma((6,)),
            dma((SPLIT, SPLIT)),
            dma((SPLIT, 2)),
            dma((SPLIT, SPLIT)),
            dma((SPLIT, SPLIT)),
            dma((SPLIT, 2)),
            dma((SPLIT, SPLIT)),
            dma((2,)),
            dma((2,)),
            dma((2, PER_VX)),
            dma((2, PER_VX)),
            dma((2,)),
            dma((2,)),
        ],
        compiler_params=pltpu.CompilerParams(
            collective_id=0, has_side_effects=True, vmem_limit_bytes=60 * 1024 * 1024
        ),
    )(
        distribution,
        kernels,
        table,
        low_map.reshape(1, low_count),
        pair_kind,
        thermal_speed,
        relax_rate,
    )
    return pl.pallas_call(
        write_out,
        out_shape=jax.ShapeDtypeStruct(distribution.shape, F32),
        in_specs=[anywhere],
        out_specs=anywhere,
        scratch_shapes=[pltpu.VMEM(distribution.shape, F32), dma((2, 4))],
        compiler_params=pltpu.CompilerParams(vmem_limit_bytes=60 * 1024 * 1024),
    )(stepped)


def solution(mesh):
    in_specs = (
        P("species", "mode", "space", None),
        P(None, "mode", None, None),
        P(),
        P(),
        P("species"),
        P("species"),
    )
    out_specs = P("species", "mode", "space", None)
    return jax.shard_map(
        functools.partial(per_device, mesh.shape["space"]),
        mesh=mesh,
        in_specs=in_specs,
        out_specs=out_specs,
        check_vma=False,
    )
```

```python
import functools

import jax
import jax.numpy as jnp
import numpy as np
from jax import lax
from jax.experimental import pallas as pl
from jax.experimental.pallas import tpu as pltpu
from jax.sharding import PartitionSpec as P

MESH = pl.DeviceIdType.MESH
F32 = jnp.float32
BF16 = jnp.bfloat16

NVY = 8
NVZ = 8
DEG = 7
NKIND = 2
NY = 256

nu_step = 0.0625
dt_step = 0.05
bound_x = 6.7
bound_y = 4.2
bound_z = 4.2

SPLIT = 4
OWN = 2
ROWS = 256
PER_VX = 4
LANES = 128
HEAD = 208
PACK = 256
PIECE = 64
PAD_J = 128
PAD_N = 32


def packed_table():
    low = [
        (a * NVY + b) * NVZ + c
        for a in range(DEG + 1)
        for b in range(NVY)
        for c in range(NVZ)
        if a + b + c <= DEG
    ]
    table = np.full((PACK, 8), -1, np.int32)
    for start, first in ((0, 0), (HEAD, ROWS)):
        held = [mode for mode in low if first <= mode < first + ROWS]
        row = start
        for slot in range(OWN):
            for mode in held:
                table[row, 0] = slot * ROWS + mode - first
                table[row, 1 + slot] = mode
                row += 1
        assert row <= (HEAD if start == 0 else PACK)
    return table


def dot(left, right):
    return jnp.dot(left, right, preferred_element_type=F32)


def kernel(
    space_count,
    f_in,
    k_in,
    tab_in,
    map_in,
    kind_in,
    th_in,
    rx_in,
    result,
    f_ref,
    out_ref,
    tab_ref,
    lm_ref,
    kind_ref,
    th_ref,
    rx_ref,
    kraw,
    k2,
    low_send,
    full,
    low,
    pmat,
    gsum,
    total,
    gsend,
    grecv,
    pick,
    spread,
    halo_send,
    halo_recv,
    edge_recv,
    ab_send,
    ab_recv,
    copy_sem,
    small_sem,
    s1,
    r1,
    s2,
    r2,
    s3,
    r3,
    hs,
    hr,
    xs,
    xr,
    es,
    er,
):
    q = lax.axis_index("species")
    m = lax.axis_index("mode")
    sx = lax.axis_index("space")

    columns_in = [
        pltpu.make_async_copy(
            f_in.at[slot, :, 0, pl.ds(part * LANES, LANES)],
            f_ref.at[part, slot],
            copy_sem.at[part, slot],
        )
        for part in range(SPLIT)
        for slot in range(OWN)
    ]
    small = [
        pltpu.make_async_copy(tab_in, tab_ref, small_sem.at[0]),
        pltpu.make_async_copy(map_in, lm_ref, small_sem.at[1]),
        pltpu.make_async_copy(kind_in, kind_ref, small_sem.at[2]),
        pltpu.make_async_copy(th_in, th_ref, small_sem.at[3]),
        pltpu.make_async_copy(rx_in, rx_ref, small_sem.at[4]),
    ]
    copy_k = pltpu.make_async_copy(k_in, kraw, small_sem.at[5])
    for item in columns_in + small[:1]:
        item.start()

    barrier = pltpu.get_barrier_semaphore()
    for step in range(1, SPLIT * SPLIT):
        other = lax.rem(q * SPLIT + m + step, SPLIT * SPLIT)
        pl.semaphore_signal(
            barrier,
            inc=1,
            device_id={"species": other // SPLIT, "mode": lax.rem(other, SPLIT)},
            device_id_type=MESH,
        )

    @pl.when(sx > 0)
    def _():
        pl.semaphore_signal(barrier, inc=1, device_id={"space": sx - 1}, device_id_type=MESH)

    @pl.when(sx < space_count - 1)
    def _():
        pl.semaphore_signal(barrier, inc=1, device_id={"space": sx + 1}, device_id_type=MESH)

    for item in small[1:] + [copy_k]:
        item.start()
    for item in columns_in + small[:1]:
        item.wait()

    def load(slot, rows):
        return jnp.concatenate([f_ref[part, slot, rows, :] for part in range(SPLIT)], axis=1)

    def extract(first, count):
        rows = lax.broadcasted_iota(jnp.int32, (count, OWN * ROWS), 1)
        chosen = jnp.where(tab_ref[first : first + count, 0:1] == rows, 1.0, 0.0).astype(BF16)
        for part in range(SPLIT):
            field = f_ref[part].reshape(OWN * ROWS, LANES).astype(BF16)
            low_send[part, first : first + count, :] = dot(chosen, field).astype(BF16)

    @pl.when(m == 0)
    def _():
        extract(0, HEAD)

    @pl.when(m == 1)
    def _():
        extract(HEAD, PACK - HEAD)

    inner = (sx > 0) & (sx < space_count - 1)
    peers = SPLIT * SPLIT - 1

    @pl.when(inner)
    def _():
        pl.semaphore_wait(barrier, peers + 2)

    @pl.when(jnp.logical_not(inner))
    def _():
        pl.semaphore_wait(barrier, peers + min(1, space_count - 1))

    def scatter(part, piece, first, count):
        return pltpu.make_async_remote_copy(
            src_ref=low_send.at[part, pl.ds(first, count)],
            dst_ref=full.at[q, pl.ds(first, count)],
            send_sem=s1,
            recv_sem=r1.at[q],
            device_id={"species": part, "mode": piece},
            device_id_type=MESH,
        )

    head_last = HEAD - 3 * PIECE

    def head_copies(step):
        part = lax.rem(q + step, SPLIT)
        found = []
        for piece in (3, 1, 2, 0):
            if step == 0 and piece == 0:
                continue
            count = PIECE if piece < 3 else head_last
            found.append(scatter(part, piece, piece * PIECE, count))
        return found

    def tail_copies(step):
        return scatter(lax.rem(q + step, SPLIT), 3, HEAD, PACK - HEAD)

    @pl.when(m == 0)
    def _():
        for step in (1, 2, 3, 0):
            for item in head_copies(step):
                item.start()
        full[q, 0:PIECE, :] = low_send[q, 0:PIECE, :]

    @pl.when(m == 1)
    def _():
        for step in (1, 2, 3, 0):
            tail_copies(step).start()

    for slot in range(OWN):
        halo_send[0, slot] = load(slot, slice(0, 64)).astype(BF16)
        halo_send[1, slot] = load(slot, slice(ROWS - 64, ROWS)).astype(BF16)

    def halo(way):
        return pltpu.make_async_remote_copy(
            src_ref=halo_send.at[way],
            dst_ref=halo_recv.at[1 - way],
            send_sem=hs.at[way],
            recv_sem=hr.at[1 - way],
            device_id={"mode": m - 1 if way == 0 else m + 1},
            device_id_type=MESH,
        )

    @pl.when((m == 1) | (m == 3))
    def _():
        halo(0).start()

    @pl.when(m == 2)
    def _():
        halo(1).start()

    for item in small[1:] + [copy_k]:
        item.wait()

    def lay(n, carry):
        k2[n] = jnp.zeros((PAD_J, NKIND * PAD_J), BF16)

        @pl.when(n < kraw.shape[1])
        def _():
            spot = jnp.minimum(n, kraw.shape[1] - 1)
            for kind in range(NKIND):
                k2[n, 0 : kraw.shape[2], kind * PAD_J : kind * PAD_J + kraw.shape[3]] = kraw[
                    kind, spot
                ]

        return carry

    lax.fori_loop(0, PAD_N, lay, 0)

    lanes = lax.broadcasted_iota(jnp.int32, (8, PAD_J), 1)
    low_count = kraw.shape[2]
    block_rows = kraw.shape[1]
    ordered = jnp.concatenate(
        [lm_ref[...], jnp.full((1, PAD_J - low_count), -2, jnp.int32)], axis=1
    )
    ordered = jnp.broadcast_to(ordered, (8, PAD_J))
    by_block = jnp.full((8, PAD_J), -2, jnp.int32)
    for block in range(SPLIT):
        moved = ordered
        if block > 0:
            moved = pltpu.roll(ordered, block * (PAD_N - block_rows), 1)
        inside = (lanes >= block * PAD_N) & (lanes < block * PAD_N + block_rows)
        by_block = jnp.where(inside, moved, by_block)
    for slot in range(OWN):
        same = tab_ref[:, 1 + slot : 2 + slot] == ordered[0:1, :]
        pick[slot * PAD_J : (slot + 1) * PAD_J, :] = jnp.where(same, 1.0, 0.0).T.astype(BF16)
    mode_of = lax.broadcasted_iota(jnp.int32, (ROWS, PAD_J), 0) + m * ROWS
    spread[...] = jnp.where(mode_of == by_block[0:1, :], 1.0, 0.0).astype(BF16)

    def piece_wait(source):
        pltpu.make_async_remote_copy(
            src_ref=low_send.at[0, pl.ds(0, PIECE)],
            dst_ref=full.at[source, pl.ds(0, PIECE)],
            send_sem=s1,
            recv_sem=r1.at[source],
            device_id={"mode": lax.rem(m + 1, SPLIT)},
            device_id_type=MESH,
        ).wait_recv()

    def forward(half, step):
        rows = pl.ds(pl.multiple_of(m * PIECE, PIECE), PIECE)
        return pltpu.make_async_remote_copy(
            src_ref=full.at[pl.ds(half * 2, 2), rows],
            dst_ref=full.at[pl.ds(half * 2, 2), rows],
            send_sem=s2,
            recv_sem=r2.at[half],
            device_id={"mode": lax.rem(m + step, SPLIT)},
            device_id_type=MESH,
        )

    near = q // 2
    halves = (near, 1 - near)
    for half in halves:
        for spot in range(2):
            source = half * 2 + spot

            @pl.when((m > 0) | (source != q))
            def _():
                piece_wait(source)

        for step in (2, 1, 3):
            forward(half, step).start()

    @pl.when(m < 2)
    def _():
        halo(1).start()

    @pl.when(m == 2)
    def _():
        halo(0).start()

    degree_c = lax.broadcasted_iota(jnp.int32, (NVZ, 1), 0)
    sqrt_c = jnp.sqrt(degree_c.astype(F32))
    sqrt_c_up = jnp.where(degree_c == NVZ - 1, 0.0, jnp.sqrt(degree_c.astype(F32) + 1.0))
    planes = SPLIT * LANES // NY

    def own_terms(i, carry):
        slot = i // PER_VX
        a = lax.rem(i, PER_VX)
        scale = nu_step * th_ref[slot]
        relax = dt_step * rx_ref[slot]
        blocks = [
            load(slot, pl.ds(pl.multiple_of(a * 64 + b * NVZ, NVZ), NVZ)) for b in range(NVY)
        ]
        for b in range(NVY):
            here = blocks[b]
            flux_y = jnp.zeros_like(here)
            if b < NVY - 1:
                flux_y = flux_y + float(np.sqrt(np.float32(b + 1))) * blocks[b + 1]
            if b > 0:
                flux_y = flux_y + float(np.sqrt(np.float32(b))) * blocks[b - 1]
            up_y = 0.5 * flux_y - 0.5 * bound_y * here
            down_y = -0.5 * flux_y - 0.5 * bound_y * here
            turned = []
            for plane in range(planes):
                cut = slice(plane * NY, (plane + 1) * NY)
                turned.append(
                    pltpu.roll(up_y[:, cut], NY - 1, 1) + pltpu.roll(down_y[:, cut], 1, 1)
                )
            y_term = jnp.concatenate(turned, axis=1) + bound_y * here
            flux_z = sqrt_c_up * pltpu.roll(here, NVZ - 1, 0) + sqrt_c * pltpu.roll(here, 1, 0)
            wide = planes * NY
            up_z = 0.5 * flux_z - 0.5 * bound_z * here
            down_z = -0.5 * flux_z - 0.5 * bound_z * here
            z_term = (
                pltpu.roll(up_z, wide - NY, 1) + pltpu.roll(down_z, NY, 1) + bound_z * here
            )
            total = degree_c + (b + a + m * PER_VX)
            lost = jnp.where(total > DEG, relax, 0.0)
            value = here - scale * (y_term + z_term + bound_x * here) - lost * here
            rows = pl.ds(pl.multiple_of(a * 64 + b * NVZ, NVZ), NVZ)
            for part in range(SPLIT):
                out_ref[part, slot, rows, :] = value[:, part * LANES : (part + 1) * LANES]
        return carry

    lax.fori_loop(0, OWN * PER_VX, own_terms, 0)

    def degree_roots(a):
        degree = (m * PER_VX + a).astype(F32)
        below = jnp.sqrt(jnp.full((8, 128), degree, F32))[0:1, 0:1]
        above = jnp.sqrt(jnp.full((8, 128), degree + 1.0, F32))[0:1, 0:1]
        return below, above

    def x_parts(a):
        root, root_up = degree_roots(a)

        def part(i, carry):
            slot = i // 4
            r = lax.rem(i, 4) * 16
            here = load(slot, pl.ds(pl.multiple_of(a * 64 + r, 16), 16))
            flux = jnp.zeros_like(here)
            if a < PER_VX - 1:
                flux = flux + root_up * load(slot, pl.ds(pl.multiple_of((a + 1) * 64 + r, 16), 16))
            if a > 0:
                flux = flux + root * load(slot, pl.ds(pl.multiple_of((a - 1) * 64 + r, 16), 16))
            rows = pl.ds(pl.multiple_of(slot * 64 + r, 16), 16)
            ab_send[0, a, rows, :] = (0.5 * flux - 0.5 * bound_x * here).astype(ab_send.dtype)
            ab_send[1, a, rows, :] = (-0.5 * flux - 0.5 * bound_x * here).astype(ab_send.dtype)
            return carry

        lax.fori_loop(0, OWN * 4, part, 0)

    def layer(way):
        return pltpu.make_async_remote_copy(
            src_ref=ab_send.at[way],
            dst_ref=ab_recv.at[way],
            send_sem=xs.at[way],
            recv_sem=xr.at[way],
            device_id={"space": sx - 1 if way == 0 else sx + 1},
            device_id_type=MESH,
        )

    @pl.when(sx == space_count - 1)
    def _():
        ab_recv[0] = jnp.zeros(ab_recv.shape[1:], ab_recv.dtype)
        edge_recv[0] = jnp.zeros(edge_recv.shape[1:], BF16)

    @pl.when(sx == 0)
    def _():
        ab_recv[1] = jnp.zeros(ab_recv.shape[1:], ab_recv.dtype)
        edge_recv[1] = jnp.zeros(edge_recv.shape[1:], BF16)

    for a in range(PER_VX):
        x_parts(a)

    @pl.when(sx > 0)
    def _():
        layer(0).start()

    @pl.when(sx < space_count - 1)
    def _():
        layer(1).start()

    def forward_wait(half):
        others = full.at[pl.ds(half * 2, 2), pl.ds(0, 3 * PIECE)]
        pltpu.make_async_remote_copy(
            src_ref=others,
            dst_ref=others,
            send_sem=s2,
            recv_sem=r2.at[half],
            device_id={"mode": lax.rem(m + 1, SPLIT)},
            device_id_type=MESH,
        ).wait_recv()

    for half in halves:
        forward_wait(half)
        for spot in range(2):
            source = half * 2 + spot
            picked = dot(pick[...], full[source])
            for slot in range(OWN):
                low[source, :, slot * LANES : (slot + 1) * LANES] = picked[
                    slot * PAD_J : (slot + 1) * PAD_J
                ]

    def of_species(r):
        return low[r // OWN, :, (r % OWN) * LANES : (r % OWN + 1) * LANES]

    everyone = of_species(0)
    for r in range(1, SPLIT * OWN):
        everyone = everyone + of_species(r)
    total[...] = everyone

    def partners(pair):
        def one(slot):
            first = jnp.zeros((PAD_J, LANES), F32)
            for r in range(SPLIT * OWN):
                weight = jnp.where(kind_ref[pair * OWN + slot, r] == 0, 1.0, 0.0)
                first = first + weight * of_species(r)
            cut = slice(slot * LANES, (slot + 1) * LANES)
            pmat[pair, 0:PAD_J, cut] = first.astype(BF16)
            pmat[pair, PAD_J:, cut] = (total[...] - first).astype(BF16)

        for slot in range(OWN):
            one(slot)

    def give(pair, target):
        return pltpu.make_async_remote_copy(
            src_ref=gsend.at[pair],
            dst_ref=grecv.at[q, pl.ds(pl.multiple_of(m * PAD_N, PAD_N), PAD_N)],
            send_sem=s3,
            recv_sem=r3.at[q],
            device_id={"species": pair, "mode": target},
            device_id_type=MESH,
        )

    group = 8

    def collide(pair):
        def some(i, carry):
            left = k2[pl.ds(pl.multiple_of(i * group, group), group)]
            product = dot(left.reshape(group * PAD_J, NKIND * PAD_J), pmat[pair])
            own = low[pair]
            gsum[pl.ds(pl.multiple_of(i * group, group), group), :] = jnp.sum(
                product.reshape(group, PAD_J, OWN * LANES) * own[None], axis=1
            )
            return carry

        lax.fori_loop(0, PAD_N // group, some, 0)
        gsend[pair] = gsum[...].astype(BF16)

    for step in (1, 2, 3, 0):
        pair = lax.rem(q + step, SPLIT)
        partners(pair)
        collide(pair)
        for target in range(2):
            if step > 0:
                give(pair, target).start()
            else:

                @pl.when(m != target)
                def _():
                    give(pair, target).start()

                @pl.when(m == target)
                def _():
                    grecv[q, target * PAD_N : (target + 1) * PAD_N, :] = gsend[pair]

    @pl.when(m > 0)
    def _():
        halo(1).wait_recv()

    @pl.when(m == 0)
    def _():
        halo_recv[0] = jnp.zeros(halo_recv.shape[1:], BF16)

    @pl.when(m < SPLIT - 1)
    def _():
        halo(0).wait_recv()

    @pl.when(m == SPLIT - 1)
    def _():
        halo_recv[1] = jnp.zeros(halo_recv.shape[1:], BF16)

    def edges(way):
        return pltpu.make_async_remote_copy(
            src_ref=halo_recv,
            dst_ref=edge_recv.at[way],
            send_sem=es.at[way],
            recv_sem=er.at[way],
            device_id={"space": sx - 1 if way == 0 else sx + 1},
            device_id_type=MESH,
        )

    @pl.when(sx > 0)
    def _():
        edges(0).start()

    @pl.when(sx < space_count - 1)
    def _():
        edges(1).start()

    @pl.when(sx < space_count - 1)
    def _():
        layer(0).wait_recv()
        edges(0).wait_recv()

    @pl.when(sx > 0)
    def _():
        layer(1).wait_recv()
        edges(1).wait_recv()

    for a in range(PER_VX):
        root, root_up = degree_roots(a)

        def add_x(i, carry):
            slot = i // 4
            r = pl.multiple_of(lax.rem(i, 4) * 16, 16)
            rows = pl.ds(pl.multiple_of(slot * 64 + r, 16), 16)
            here = pl.ds(pl.multiple_of(a * 64 + r, 16), 16)
            term = ab_recv[0, a, rows, :] + ab_recv[1, a, rows, :]
            side = {0: 0, PER_VX - 1: 1}.get(a)
            if side is not None:
                up = edge_recv[0, side, slot, pl.ds(r, 16), :].astype(F32)
                down = edge_recv[1, side, slot, pl.ds(r, 16), :].astype(F32)
                term = term + (0.5 * (root_up if side else root)) * (up - down)
            term = (nu_step * th_ref[slot]) * term
            for part in range(SPLIT):
                out_ref[part, slot, here, :] = (
                    out_ref[part, slot, here, :] - term[:, part * LANES : (part + 1) * LANES]
                )
            return carry

        lax.fori_loop(0, OWN * 4, add_x, 0)

    def column_out(part, slot):
        return pltpu.make_async_copy(
            out_ref.at[part, slot],
            result.at[slot, :, 0, pl.ds(pl.multiple_of(part * LANES, LANES), LANES)],
            copy_sem.at[part, slot],
        )

    @pl.when(m >= 2)
    def _():
        for part in range(SPLIT):
            for slot in range(OWN):
                column_out(part, slot).start()

    @pl.when(m < 2)
    def _():
        for back in (1, 2, 3, 0):
            source = lax.rem(q + SPLIT - back, SPLIT)
            came = grecv.at[source, pl.ds(0, (SPLIT if back else SPLIT - 1) * PAD_N)]
            pltpu.make_async_remote_copy(
                src_ref=came,
                dst_ref=came,
                send_sem=s3,
                recv_sem=r3.at[source],
                device_id={"mode": lax.rem(m + 1, SPLIT)},
                device_id_type=MESH,
            ).wait_recv()
            gained = dot(spread[...], grecv[source])
            for slot in range(OWN):
                out_ref[source, slot] = (
                    out_ref[source, slot] + dt_step * gained[:, slot * LANES : (slot + 1) * LANES]
                )
                column_out(source, slot).start()

    def all_sent(rows, sem):
        pltpu.make_async_remote_copy(
            src_ref=rows,
            dst_ref=rows,
            send_sem=sem,
            recv_sem=r1.at[0],
            device_id={"mode": lax.rem(m + 1, SPLIT)},
            device_id_type=MESH,
        ).wait_send()

    @pl.when(m == 0)
    def _():
        all_sent(low_send.at[:, pl.ds(0, HEAD - PIECE // SPLIT)], s1)

    @pl.when(m == 1)
    def _():
        all_sent(low_send.at[:, pl.ds(0, PACK - HEAD)], s1)

    all_sent(full.at[:, pl.ds(0, 3 * PIECE)], s2)

    @pl.when(m > 0)
    def _():
        halo(0).wait_send()

    @pl.when(m < SPLIT - 1)
    def _():
        halo(1).wait_send()

    @pl.when(sx > 0)
    def _():
        layer(0).wait_send()

    @pl.when(sx < space_count - 1)
    def _():
        layer(1).wait_send()

    @pl.when(sx > 0)
    def _():
        edges(0).wait_send()

    @pl.when(sx < space_count - 1)
    def _():
        edges(1).wait_send()

    @pl.when(m < 2)
    def _():
        all_sent(grecv.at[pl.ds(0, 2), pl.ds(0, 7 * PAD_N // 2)], s3)

    @pl.when(m >= 2)
    def _():
        all_sent(grecv.at[pl.ds(0, 2)], s3)

    for part in range(SPLIT):
        for slot in range(OWN):
            column_out(part, slot).wait()


def write_out(source, result, held, sems):
    count = sems.shape[1]
    rows = result.shape[1] // count

    def move(src, dst, way, piece):
        cut = pl.ds(piece * rows, rows)
        return pltpu.make_async_copy(src.at[:, cut], dst.at[:, cut], sems.at[way, piece])

    for piece in range(count):
        move(source, held, 0, piece).start()
    for piece in range(count):
        move(source, held, 0, piece).wait()
        move(held, result, 1, piece).start()
    for piece in range(count):
        move(held, result, 1, piece).wait()


def per_device(space_count, distribution, kernels, pair_kind, low_map, thermal_speed, relax_rate):
    own, rows, layers, cells = distribution.shape
    assert (own, rows, layers, cells) == (OWN, ROWS, 1, SPLIT * LANES)
    kinds, _, low_count, _ = kernels.shape
    table = jnp.asarray(packed_table())
    anywhere = pl.BlockSpec(memory_space=pl.ANY)
    dma = pltpu.SemaphoreType.DMA
    ab_type = F32
    stepped = pl.pallas_call(
        functools.partial(kernel, space_count),
        out_shape=jax.ShapeDtypeStruct(distribution.shape, F32),
        in_specs=[anywhere] * 7,
        out_specs=anywhere,
        scratch_shapes=[
            pltpu.VMEM((SPLIT, own, rows, LANES), F32),
            pltpu.VMEM((SPLIT, own, rows, LANES), F32),
            pltpu.VMEM(table.shape, jnp.int32),
            pltpu.VMEM((1, low_count), jnp.int32),
            pltpu.SMEM(pair_kind.shape, jnp.int32),
            pltpu.SMEM(thermal_speed.shape, F32),
            pltpu.SMEM(relax_rate.shape, F32),
            pltpu.VMEM(kernels.shape, BF16),
            pltpu.VMEM((PAD_N, PAD_J, kinds * PAD_J), BF16),
            pltpu.VMEM((SPLIT, PACK, LANES), BF16),
            pltpu.VMEM((SPLIT, PACK, LANES), BF16),
            pltpu.VMEM((SPLIT, PAD_J, own * LANES), F32),
            pltpu.VMEM((SPLIT, kinds * PAD_J, own * LANES), BF16),
            pltpu.VMEM((PAD_N, own * LANES), F32),
            pltpu.VMEM((PAD_J, LANES), F32),
            pltpu.VMEM((SPLIT, PAD_N, own * LANES), BF16),
            pltpu.VMEM((SPLIT, SPLIT * PAD_N, own * LANES), BF16),
            pltpu.VMEM((own * PAD_J, PACK), BF16),
            pltpu.VMEM((ROWS, PAD_J), BF16),
            pltpu.VMEM((2, own, 64, cells), BF16),
            pltpu.VMEM((2, own, 64, cells), BF16),
            pltpu.VMEM((2, 2, own, 64, cells), BF16),
            pltpu.VMEM((2, PER_VX, own * 64, cells), ab_type),
            pltpu.VMEM((2, PER_VX, own * 64, cells), ab_type),
            dma((SPLIT, OWN)),
            dma((6,)),
            dma,
            dma((SPLIT,)),
            dma,
            dma((2,)),
            dma,
            dma((SPLIT,)),
            dma((2,)),
            dma((2,)),
            dma((2,)),
            dma((2,)),
            dma((2,)),
            dma((2,)),
        ],
        compiler_params=pltpu.CompilerParams(
            collective_id=0, has_side_effects=True, vmem_limit_bytes=60 * 1024 * 1024
        ),
    )(
        distribution,
        kernels,
        table,
        low_map.reshape(1, low_count),
        pair_kind,
        thermal_speed,
        relax_rate,
    )
    return pl.pallas_call(
        write_out,
        out_shape=jax.ShapeDtypeStruct(distribution.shape, F32),
        in_specs=[anywhere],
        out_specs=anywhere,
        scratch_shapes=[pltpu.VMEM(distribution.shape, F32), dma((2, 4))],
        compiler_params=pltpu.CompilerParams(vmem_limit_bytes=60 * 1024 * 1024),
    )(stepped)


def solution(mesh):
    in_specs = (
        P("species", "mode", "space", None),
        P(None, "mode", None, None),
        P(),
        P(),
        P("species"),
        P("species"),
    )
    out_specs = P("species", "mode", "space", None)
    return jax.shard_map(
        functools.partial(per_device, mesh.shape["space"]),
        mesh=mesh,
        in_specs=in_specs,
        out_specs=out_specs,
        check_vma=False,
    )
```

```python
import functools

import jax
import jax.numpy as jnp
import numpy as np
from jax import lax
from jax.experimental import pallas as pl
from jax.experimental.pallas import tpu as pltpu
from jax.sharding import PartitionSpec as P

MESH = pl.DeviceIdType.MESH
F32 = jnp.float32
BF16 = jnp.bfloat16

NVY = 8
NVZ = 8
DEG = 7
NKIND = 2
NY = 256

nu_step = 0.0625
dt_step = 0.05
bound_x = 6.7
bound_y = 4.2
bound_z = 4.2

SPLIT = 4
OWN = 2
ROWS = 256
PER_VX = 4
LANES = 128
HEAD = 208
PACK = 256
PIECE = 64
PAD_J = 128
PAD_N = 32


def packed_table():
    low = [
        (a * NVY + b) * NVZ + c
        for a in range(DEG + 1)
        for b in range(NVY)
        for c in range(NVZ)
        if a + b + c <= DEG
    ]
    table = np.full((PACK, 8), -1, np.int32)
    for start, first in ((0, 0), (HEAD, ROWS)):
        held = [mode for mode in low if first <= mode < first + ROWS]
        row = start
        for slot in range(OWN):
            for mode in held:
                table[row, 0] = slot * ROWS + mode - first
                table[row, 1 + slot] = mode
                row += 1
        assert row <= (HEAD if start == 0 else PACK)
    return table


def dot(left, right):
    return jnp.dot(left, right, preferred_element_type=F32)


def kernel(
    space_count,
    f_in,
    k_in,
    tab_in,
    map_in,
    kind_in,
    th_in,
    rx_in,
    result,
    f_ref,
    out_ref,
    tab_ref,
    lm_ref,
    kind_ref,
    th_ref,
    rx_ref,
    kraw,
    k2,
    low_send,
    full,
    low,
    pmat,
    gsum,
    total,
    gsend,
    grecv,
    pick,
    spread,
    halo_send,
    halo_recv,
    edge_recv,
    ab_send,
    ab_recv,
    copy_sem,
    small_sem,
    s1,
    r1,
    s2,
    r2,
    s3,
    r3,
    hs,
    hr,
    xs,
    xr,
    es,
    er,
):
    q = lax.axis_index("species")
    m = lax.axis_index("mode")
    sx = lax.axis_index("space")

    columns_in = [
        pltpu.make_async_copy(
            f_in.at[slot, :, 0, pl.ds(part * LANES, LANES)],
            f_ref.at[part, slot],
            copy_sem.at[part, slot],
        )
        for part in range(SPLIT)
        for slot in range(OWN)
    ]
    small = [
        pltpu.make_async_copy(tab_in, tab_ref, small_sem.at[0]),
        pltpu.make_async_copy(map_in, lm_ref, small_sem.at[1]),
        pltpu.make_async_copy(kind_in, kind_ref, small_sem.at[2]),
        pltpu.make_async_copy(th_in, th_ref, small_sem.at[3]),
        pltpu.make_async_copy(rx_in, rx_ref, small_sem.at[4]),
    ]
    copy_k = pltpu.make_async_copy(k_in, kraw, small_sem.at[5])
    for item in columns_in + small[:1]:
        item.start()

    barrier = pltpu.get_barrier_semaphore()
    for step in range(1, SPLIT * SPLIT):
        other = lax.rem(q * SPLIT + m + step, SPLIT * SPLIT)
        pl.semaphore_signal(
            barrier,
            inc=1,
            device_id={"species": other // SPLIT, "mode": lax.rem(other, SPLIT)},
            device_id_type=MESH,
        )

    @pl.when(sx > 0)
    def _():
        pl.semaphore_signal(barrier, inc=1, device_id={"space": sx - 1}, device_id_type=MESH)

    @pl.when(sx < space_count - 1)
    def _():
        pl.semaphore_signal(barrier, inc=1, device_id={"space": sx + 1}, device_id_type=MESH)

    for item in small[1:] + [copy_k]:
        item.start()
    for item in columns_in + small[:1]:
        item.wait()

    def load(slot, rows):
        return jnp.concatenate([f_ref[part, slot, rows, :] for part in range(SPLIT)], axis=1)

    def extract(first, count):
        rows = lax.broadcasted_iota(jnp.int32, (count, OWN * ROWS), 1)
        chosen = jnp.where(tab_ref[first : first + count, 0:1] == rows, 1.0, 0.0).astype(BF16)
        for part in range(SPLIT):
            field = f_ref[part].reshape(OWN * ROWS, LANES).astype(BF16)
            low_send[part, first : first + count, :] = dot(chosen, field).astype(BF16)

    @pl.when(m == 0)
    def _():
        extract(0, HEAD)

    @pl.when(m == 1)
    def _():
        extract(HEAD, PACK - HEAD)

    inner = (sx > 0) & (sx < space_count - 1)
    peers = SPLIT * SPLIT - 1

    @pl.when(inner)
    def _():
        pl.semaphore_wait(barrier, peers + 2)

    @pl.when(jnp.logical_not(inner))
    def _():
        pl.semaphore_wait(barrier, peers + min(1, space_count - 1))

    def scatter(part, piece, first, count):
        return pltpu.make_async_remote_copy(
            src_ref=low_send.at[part, pl.ds(first, count)],
            dst_ref=full.at[q, pl.ds(first, count)],
            send_sem=s1,
            recv_sem=r1.at[q],
            device_id={"species": part, "mode": piece},
            device_id_type=MESH,
        )

    head_last = HEAD - 3 * PIECE

    def head_copies(step):
        part = lax.rem(q + step, SPLIT)
        found = []
        for piece in (3, 1, 2, 0):
            if step == 0 and piece == 0:
                continue
            count = PIECE if piece < 3 else head_last
            found.append(scatter(part, piece, piece * PIECE, count))
        return found

    def tail_copies(step):
        return scatter(lax.rem(q + step, SPLIT), 3, HEAD, PACK - HEAD)

    @pl.when(m == 0)
    def _():
        for step in (1, 2, 3, 0):
            for item in head_copies(step):
                item.start()
        full[q, 0:PIECE, :] = low_send[q, 0:PIECE, :]

    @pl.when(m == 1)
    def _():
        for step in (1, 2, 3, 0):
            tail_copies(step).start()

    for slot in range(OWN):
        halo_send[0, slot] = load(slot, slice(0, 64)).astype(BF16)
        halo_send[1, slot] = load(slot, slice(ROWS - 64, ROWS)).astype(BF16)

    def halo(way):
        return pltpu.make_async_remote_copy(
            src_ref=halo_send.at[way],
            dst_ref=halo_recv.at[1 - way],
            send_sem=hs.at[way],
            recv_sem=hr.at[1 - way],
            device_id={"mode": m - 1 if way == 0 else m + 1},
            device_id_type=MESH,
        )

    @pl.when((m == 1) | (m == 3))
    def _():
        halo(0).start()

    @pl.when(m == 2)
    def _():
        halo(1).start()

    def piece_wait(source):
        pltpu.make_async_remote_copy(
            src_ref=low_send.at[0, pl.ds(0, PIECE)],
            dst_ref=full.at[source, pl.ds(0, PIECE)],
            send_sem=s1,
            recv_sem=r1.at[source],
            device_id={"mode": lax.rem(m + 1, SPLIT)},
            device_id_type=MESH,
        ).wait_recv()

    def forward(half, step):
        rows = pl.ds(pl.multiple_of(m * PIECE, PIECE), PIECE)
        return pltpu.make_async_remote_copy(
            src_ref=full.at[pl.ds(half * 2, 2), rows],
            dst_ref=full.at[pl.ds(half * 2, 2), rows],
            send_sem=s2,
            recv_sem=r2.at[half],
            device_id={"mode": lax.rem(m + step, SPLIT)},
            device_id_type=MESH,
        )

    near = q // 2
    halves = (near, 1 - near)
    for half in halves:
        for spot in range(2):
            source = half * 2 + spot

            @pl.when((m > 0) | (source != q))
            def _():
                piece_wait(source)

        for step in (2, 1, 3):
            forward(half, step).start()

    @pl.when(m < 2)
    def _():
        halo(1).start()

    @pl.when(m == 2)
    def _():
        halo(0).start()

    for item in small[1:] + [copy_k]:
        item.wait()

    def lay(n, carry):
        k2[n] = jnp.zeros((PAD_J, NKIND * PAD_J), BF16)

        @pl.when(n < kraw.shape[1])
        def _():
            spot = jnp.minimum(n, kraw.shape[1] - 1)
            for kind in range(NKIND):
                k2[n, 0 : kraw.shape[2], kind * PAD_J : kind * PAD_J + kraw.shape[3]] = kraw[
                    kind, spot
                ]

        return carry

    lax.fori_loop(0, PAD_N, lay, 0)

    lanes = lax.broadcasted_iota(jnp.int32, (8, PAD_J), 1)
    low_count = kraw.shape[2]
    block_rows = kraw.shape[1]
    ordered = jnp.concatenate(
        [lm_ref[...], jnp.full((1, PAD_J - low_count), -2, jnp.int32)], axis=1
    )
    ordered = jnp.broadcast_to(ordered, (8, PAD_J))
    by_block = jnp.full((8, PAD_J), -2, jnp.int32)
    for block in range(SPLIT):
        moved = ordered
        if block > 0:
            moved = pltpu.roll(ordered, block * (PAD_N - block_rows), 1)
        inside = (lanes >= block * PAD_N) & (lanes < block * PAD_N + block_rows)
        by_block = jnp.where(inside, moved, by_block)
    for slot in range(OWN):
        same = tab_ref[:, 1 + slot : 2 + slot] == ordered[0:1, :]
        pick[slot * PAD_J : (slot + 1) * PAD_J, :] = jnp.where(same, 1.0, 0.0).T.astype(BF16)
    def degree_roots(a):
        degree = (m * PER_VX + a).astype(F32)
        below = jnp.sqrt(jnp.full((8, 128), degree, F32))[0:1, 0:1]
        above = jnp.sqrt(jnp.full((8, 128), degree + 1.0, F32))[0:1, 0:1]
        return below, above

    def x_parts(a):
        root, root_up = degree_roots(a)

        def part(i, carry):
            slot = i // 4
            r = lax.rem(i, 4) * 16
            here = load(slot, pl.ds(pl.multiple_of(a * 64 + r, 16), 16))
            flux = jnp.zeros_like(here)
            if a < PER_VX - 1:
                flux = flux + root_up * load(slot, pl.ds(pl.multiple_of((a + 1) * 64 + r, 16), 16))
            if a > 0:
                flux = flux + root * load(slot, pl.ds(pl.multiple_of((a - 1) * 64 + r, 16), 16))
            rows = pl.ds(pl.multiple_of(slot * 64 + r, 16), 16)
            ab_send[0, a, rows, :] = (0.5 * flux - 0.5 * bound_x * here).astype(ab_send.dtype)
            ab_send[1, a, rows, :] = (-0.5 * flux - 0.5 * bound_x * here).astype(ab_send.dtype)
            return carry

        lax.fori_loop(0, OWN * 4, part, 0)

    def layer(way):
        return pltpu.make_async_remote_copy(
            src_ref=ab_send.at[way],
            dst_ref=ab_recv.at[way],
            send_sem=xs.at[way],
            recv_sem=xr.at[way],
            device_id={"space": sx - 1 if way == 0 else sx + 1},
            device_id_type=MESH,
        )

    @pl.when(sx == space_count - 1)
    def _():
        ab_recv[0] = jnp.zeros(ab_recv.shape[1:], ab_recv.dtype)
        edge_recv[0] = jnp.zeros(edge_recv.shape[1:], BF16)

    @pl.when(sx == 0)
    def _():
        ab_recv[1] = jnp.zeros(ab_recv.shape[1:], ab_recv.dtype)
        edge_recv[1] = jnp.zeros(edge_recv.shape[1:], BF16)

    for a in range(PER_VX):
        x_parts(a)

    @pl.when(sx > 0)
    def _():
        layer(0).start()

    @pl.when(sx < space_count - 1)
    def _():
        layer(1).start()

    def forward_wait(half):
        others = full.at[pl.ds(half * 2, 2), pl.ds(0, 3 * PIECE)]
        pltpu.make_async_remote_copy(
            src_ref=others,
            dst_ref=others,
            send_sem=s2,
            recv_sem=r2.at[half],
            device_id={"mode": lax.rem(m + 1, SPLIT)},
            device_id_type=MESH,
        ).wait_recv()

    for half in halves:
        forward_wait(half)
        for spot in range(2):
            source = half * 2 + spot
            picked = dot(pick[...], full[source])
            for slot in range(OWN):
                low[source, :, slot * LANES : (slot + 1) * LANES] = picked[
                    slot * PAD_J : (slot + 1) * PAD_J
                ]

    def of_species(r):
        return low[r // OWN, :, (r % OWN) * LANES : (r % OWN + 1) * LANES]

    everyone = of_species(0)
    for r in range(1, SPLIT * OWN):
        everyone = everyone + of_species(r)
    total[...] = everyone

    def partners(pair):
        def one(slot):
            first = jnp.zeros((PAD_J, LANES), F32)
            for r in range(SPLIT * OWN):
                weight = jnp.where(kind_ref[pair * OWN + slot, r] == 0, 1.0, 0.0)
                first = first + weight * of_species(r)
            cut = slice(slot * LANES, (slot + 1) * LANES)
            pmat[pair, 0:PAD_J, cut] = first.astype(BF16)
            pmat[pair, PAD_J:, cut] = (total[...] - first).astype(BF16)

        for slot in range(OWN):
            one(slot)

    def give(pair, target):
        return pltpu.make_async_remote_copy(
            src_ref=gsend.at[pair],
            dst_ref=grecv.at[q, pl.ds(pl.multiple_of(m * PAD_N, PAD_N), PAD_N)],
            send_sem=s3,
            recv_sem=r3.at[q],
            device_id={"species": pair, "mode": target},
            device_id_type=MESH,
        )

    group = 8

    def collide(pair):
        def some(i, carry):
            left = k2[pl.ds(pl.multiple_of(i * group, group), group)]
            product = dot(left.reshape(group * PAD_J, NKIND * PAD_J), pmat[pair])
            own = low[pair]
            gsum[pl.ds(pl.multiple_of(i * group, group), group), :] = jnp.sum(
                product.reshape(group, PAD_J, OWN * LANES) * own[None], axis=1
            )
            return carry

        lax.fori_loop(0, PAD_N // group, some, 0)
        gsend[pair] = gsum[...].astype(BF16)

    for step in (1, 2, 3, 0):
        pair = lax.rem(q + step, SPLIT)
        partners(pair)
        collide(pair)
        for target in range(2):
            if step > 0:
                give(pair, target).start()
            else:

                @pl.when(m != target)
                def _():
                    give(pair, target).start()

                @pl.when(m == target)
                def _():
                    grecv[q, target * PAD_N : (target + 1) * PAD_N, :] = gsend[pair]

    degree_c = lax.broadcasted_iota(jnp.int32, (NVZ, 1), 0)
    sqrt_c = jnp.sqrt(degree_c.astype(F32))
    sqrt_c_up = jnp.where(degree_c == NVZ - 1, 0.0, jnp.sqrt(degree_c.astype(F32) + 1.0))
    planes = SPLIT * LANES // NY

    def own_terms(i, carry):
        slot = i // PER_VX
        a = lax.rem(i, PER_VX)
        scale = nu_step * th_ref[slot]
        relax = dt_step * rx_ref[slot]
        blocks = [
            load(slot, pl.ds(pl.multiple_of(a * 64 + b * NVZ, NVZ), NVZ)) for b in range(NVY)
        ]
        for b in range(NVY):
            here = blocks[b]
            flux_y = jnp.zeros_like(here)
            if b < NVY - 1:
                flux_y = flux_y + float(np.sqrt(np.float32(b + 1))) * blocks[b + 1]
            if b > 0:
                flux_y = flux_y + float(np.sqrt(np.float32(b))) * blocks[b - 1]
            up_y = 0.5 * flux_y - 0.5 * bound_y * here
            down_y = -0.5 * flux_y - 0.5 * bound_y * here
            turned = []
            for plane in range(planes):
                cut = slice(plane * NY, (plane + 1) * NY)
                turned.append(
                    pltpu.roll(up_y[:, cut], NY - 1, 1) + pltpu.roll(down_y[:, cut], 1, 1)
                )
            y_term = jnp.concatenate(turned, axis=1) + bound_y * here
            flux_z = sqrt_c_up * pltpu.roll(here, NVZ - 1, 0) + sqrt_c * pltpu.roll(here, 1, 0)
            wide = planes * NY
            up_z = 0.5 * flux_z - 0.5 * bound_z * here
            down_z = -0.5 * flux_z - 0.5 * bound_z * here
            z_term = (
                pltpu.roll(up_z, wide - NY, 1) + pltpu.roll(down_z, NY, 1) + bound_z * here
            )
            total = degree_c + (b + a + m * PER_VX)
            lost = jnp.where(total > DEG, relax, 0.0)
            value = here - scale * (y_term + z_term + bound_x * here) - lost * here
            rows = pl.ds(pl.multiple_of(a * 64 + b * NVZ, NVZ), NVZ)
            for part in range(SPLIT):
                out_ref[part, slot, rows, :] = value[:, part * LANES : (part + 1) * LANES]
        return carry

    lax.fori_loop(0, OWN * PER_VX, own_terms, 0)

    mode_of = lax.broadcasted_iota(jnp.int32, (ROWS, PAD_J), 0) + m * ROWS
    spread[...] = jnp.where(mode_of == by_block[0:1, :], 1.0, 0.0).astype(BF16)

    @pl.when(m > 0)
    def _():
        halo(1).wait_recv()

    @pl.when(m == 0)
    def _():
        halo_recv[0] = jnp.zeros(halo_recv.shape[1:], BF16)

    @pl.when(m < SPLIT - 1)
    def _():
        halo(0).wait_recv()

    @pl.when(m == SPLIT - 1)
    def _():
        halo_recv[1] = jnp.zeros(halo_recv.shape[1:], BF16)

    def edges(way):
        return pltpu.make_async_remote_copy(
            src_ref=halo_recv,
            dst_ref=edge_recv.at[way],
            send_sem=es.at[way],
            recv_sem=er.at[way],
            device_id={"space": sx - 1 if way == 0 else sx + 1},
            device_id_type=MESH,
        )

    @pl.when(sx > 0)
    def _():
        edges(0).start()

    @pl.when(sx < space_count - 1)
    def _():
        edges(1).start()

    @pl.when(sx < space_count - 1)
    def _():
        layer(0).wait_recv()
        edges(0).wait_recv()

    @pl.when(sx > 0)
    def _():
        layer(1).wait_recv()
        edges(1).wait_recv()

    for a in range(PER_VX):
        root, root_up = degree_roots(a)

        def add_x(i, carry):
            slot = i // 4
            r = pl.multiple_of(lax.rem(i, 4) * 16, 16)
            rows = pl.ds(pl.multiple_of(slot * 64 + r, 16), 16)
            here = pl.ds(pl.multiple_of(a * 64 + r, 16), 16)
            term = ab_recv[0, a, rows, :] + ab_recv[1, a, rows, :]
            side = {0: 0, PER_VX - 1: 1}.get(a)
            if side is not None:
                up = edge_recv[0, side, slot, pl.ds(r, 16), :].astype(F32)
                down = edge_recv[1, side, slot, pl.ds(r, 16), :].astype(F32)
                term = term + (0.5 * (root_up if side else root)) * (up - down)
            term = (nu_step * th_ref[slot]) * term
            for part in range(SPLIT):
                out_ref[part, slot, here, :] = (
                    out_ref[part, slot, here, :] - term[:, part * LANES : (part + 1) * LANES]
                )
            return carry

        lax.fori_loop(0, OWN * 4, add_x, 0)

    def column_out(part, slot):
        return pltpu.make_async_copy(
            out_ref.at[part, slot],
            result.at[slot, :, 0, pl.ds(pl.multiple_of(part * LANES, LANES), LANES)],
            copy_sem.at[part, slot],
        )

    @pl.when(m >= 2)
    def _():
        for part in range(SPLIT):
            for slot in range(OWN):
                column_out(part, slot).start()

    @pl.when(m < 2)
    def _():
        for back in (1, 2, 3, 0):
            source = lax.rem(q + SPLIT - back, SPLIT)
            came = grecv.at[source, pl.ds(0, (SPLIT if back else SPLIT - 1) * PAD_N)]
            pltpu.make_async_remote_copy(
                src_ref=came,
                dst_ref=came,
                send_sem=s3,
                recv_sem=r3.at[source],
                device_id={"mode": lax.rem(m + 1, SPLIT)},
                device_id_type=MESH,
            ).wait_recv()
            gained = dot(spread[...], grecv[source])
            for slot in range(OWN):
                out_ref[source, slot] = (
                    out_ref[source, slot] + dt_step * gained[:, slot * LANES : (slot + 1) * LANES]
                )
                column_out(source, slot).start()

    def all_sent(rows, sem):
        pltpu.make_async_remote_copy(
            src_ref=rows,
            dst_ref=rows,
            send_sem=sem,
            recv_sem=r1.at[0],
            device_id={"mode": lax.rem(m + 1, SPLIT)},
            device_id_type=MESH,
        ).wait_send()

    @pl.when(m == 0)
    def _():
        all_sent(low_send.at[:, pl.ds(0, HEAD - PIECE // SPLIT)], s1)

    @pl.when(m == 1)
    def _():
        all_sent(low_send.at[:, pl.ds(0, PACK - HEAD)], s1)

    all_sent(full.at[:, pl.ds(0, 3 * PIECE)], s2)

    @pl.when(m > 0)
    def _():
        halo(0).wait_send()

    @pl.when(m < SPLIT - 1)
    def _():
        halo(1).wait_send()

    @pl.when(sx > 0)
    def _():
        layer(0).wait_send()

    @pl.when(sx < space_count - 1)
    def _():
        layer(1).wait_send()

    @pl.when(sx > 0)
    def _():
        edges(0).wait_send()

    @pl.when(sx < space_count - 1)
    def _():
        edges(1).wait_send()

    @pl.when(m < 2)
    def _():
        all_sent(grecv.at[pl.ds(0, 2), pl.ds(0, 7 * PAD_N // 2)], s3)

    @pl.when(m >= 2)
    def _():
        all_sent(grecv.at[pl.ds(0, 2)], s3)

    for part in range(SPLIT):
        for slot in range(OWN):
            column_out(part, slot).wait()


def write_out(source, result, held, sems):
    count = sems.shape[1]
    rows = result.shape[1] // count

    def move(src, dst, way, piece):
        cut = pl.ds(piece * rows, rows)
        return pltpu.make_async_copy(src.at[:, cut], dst.at[:, cut], sems.at[way, piece])

    for piece in range(count):
        move(source, held, 0, piece).start()
    for piece in range(count):
        move(source, held, 0, piece).wait()
        move(held, result, 1, piece).start()
    for piece in range(count):
        move(held, result, 1, piece).wait()


def per_device(space_count, distribution, kernels, pair_kind, low_map, thermal_speed, relax_rate):
    own, rows, layers, cells = distribution.shape
    assert (own, rows, layers, cells) == (OWN, ROWS, 1, SPLIT * LANES)
    kinds, _, low_count, _ = kernels.shape
    table = jnp.asarray(packed_table())
    anywhere = pl.BlockSpec(memory_space=pl.ANY)
    dma = pltpu.SemaphoreType.DMA
    ab_type = F32
    stepped = pl.pallas_call(
        functools.partial(kernel, space_count),
        out_shape=jax.ShapeDtypeStruct(distribution.shape, F32),
        in_specs=[anywhere] * 7,
        out_specs=anywhere,
        scratch_shapes=[
            pltpu.VMEM((SPLIT, own, rows, LANES), F32),
            pltpu.VMEM((SPLIT, own, rows, LANES), F32),
            pltpu.VMEM(table.shape, jnp.int32),
            pltpu.VMEM((1, low_count), jnp.int32),
            pltpu.SMEM(pair_kind.shape, jnp.int32),
            pltpu.SMEM(thermal_speed.shape, F32),
            pltpu.SMEM(relax_rate.shape, F32),
            pltpu.VMEM(kernels.shape, BF16),
            pltpu.VMEM((PAD_N, PAD_J, kinds * PAD_J), BF16),
            pltpu.VMEM((SPLIT, PACK, LANES), BF16),
            pltpu.VMEM((SPLIT, PACK, LANES), BF16),
            pltpu.VMEM((SPLIT, PAD_J, own * LANES), F32),
            pltpu.VMEM((SPLIT, kinds * PAD_J, own * LANES), BF16),
            pltpu.VMEM((PAD_N, own * LANES), F32),
            pltpu.VMEM((PAD_J, LANES), F32),
            pltpu.VMEM((SPLIT, PAD_N, own * LANES), BF16),
            pltpu.VMEM((SPLIT, SPLIT * PAD_N, own * LANES), BF16),
            pltpu.VMEM((own * PAD_J, PACK), BF16),
            pltpu.VMEM((ROWS, PAD_J), BF16),
            pltpu.VMEM((2, own, 64, cells), BF16),
            pltpu.VMEM((2, own, 64, cells), BF16),
            pltpu.VMEM((2, 2, own, 64, cells), BF16),
            pltpu.VMEM((2, PER_VX, own * 64, cells), ab_type),
            pltpu.VMEM((2, PER_VX, own * 64, cells), ab_type),
            dma((SPLIT, OWN)),
            dma((6,)),
            dma,
            dma((SPLIT,)),
            dma,
            dma((2,)),
            dma,
            dma((SPLIT,)),
            dma((2,)),
            dma((2,)),
            dma((2,)),
            dma((2,)),
            dma((2,)),
            dma((2,)),
        ],
        compiler_params=pltpu.CompilerParams(
            collective_id=0, has_side_effects=True, vmem_limit_bytes=60 * 1024 * 1024
        ),
    )(
        distribution,
        kernels,
        table,
        low_map.reshape(1, low_count),
        pair_kind,
        thermal_speed,
        relax_rate,
    )
    return pl.pallas_call(
        write_out,
        out_shape=jax.ShapeDtypeStruct(distribution.shape, F32),
        in_specs=[anywhere],
        out_specs=anywhere,
        scratch_shapes=[pltpu.VMEM(distribution.shape, F32), dma((2, 4))],
        compiler_params=pltpu.CompilerParams(vmem_limit_bytes=60 * 1024 * 1024),
    )(stepped)


def solution(mesh):
    in_specs = (
        P("species", "mode", "space", None),
        P(None, "mode", None, None),
        P(),
        P(),
        P("species"),
        P("species"),
    )
    out_specs = P("species", "mode", "space", None)
    return jax.shard_map(
        functools.partial(per_device, mesh.shape["space"]),
        mesh=mesh,
        in_specs=in_specs,
        out_specs=out_specs,
        check_vma=False,
    )
```

```python
import functools

import jax
import jax.numpy as jnp
import numpy as np
from jax import lax
from jax.experimental import pallas as pl
from jax.experimental.pallas import tpu as pltpu
from jax.sharding import PartitionSpec as P

MESH = pl.DeviceIdType.MESH
F32 = jnp.float32
BF16 = jnp.bfloat16

NVY = 8
NVZ = 8
DEG = 7
NKIND = 2
NY = 256

nu_step = 0.0625
dt_step = 0.05
bound_x = 6.7
bound_y = 4.2
bound_z = 4.2

SPLIT = 4
OWN = 2
ROWS = 256
PER_VX = 4
LANES = 128
HEAD = 208
PACK = 256
PIECE = 64
PAD_J = 128
PAD_N = 32


def packed_table():
    low = [
        (a * NVY + b) * NVZ + c
        for a in range(DEG + 1)
        for b in range(NVY)
        for c in range(NVZ)
        if a + b + c <= DEG
    ]
    table = np.full((PACK, 8), -1, np.int32)
    for start, first in ((0, 0), (HEAD, ROWS)):
        held = [mode for mode in low if first <= mode < first + ROWS]
        row = start
        for slot in range(OWN):
            for mode in held:
                table[row, 0] = slot * ROWS + mode - first
                table[row, 1 + slot] = mode
                row += 1
        assert row <= (HEAD if start == 0 else PACK)
    return table


def dot(left, right):
    return jnp.dot(left, right, preferred_element_type=F32)


def kernel(
    space_count,
    f_in,
    k_in,
    tab_in,
    map_in,
    kind_in,
    th_in,
    rx_in,
    result,
    f_ref,
    out_ref,
    tab_ref,
    lm_ref,
    kind_ref,
    th_ref,
    rx_ref,
    kraw,
    k2,
    low_send,
    full,
    low,
    pmat,
    gsum,
    total,
    gsend,
    grecv,
    pick,
    spread,
    halo_send,
    halo_recv,
    edge_recv,
    ab_send,
    ab_recv,
    copy_sem,
    small_sem,
    s1,
    r1,
    s2,
    r2,
    s3,
    r3,
    hs,
    hr,
    xs,
    xr,
    es,
    er,
):
    q = lax.axis_index("species")
    m = lax.axis_index("mode")
    sx = lax.axis_index("space")

    columns_in = [
        pltpu.make_async_copy(
            f_in.at[slot, :, 0, pl.ds(part * LANES, LANES)],
            f_ref.at[part, slot],
            copy_sem.at[part, slot],
        )
        for part in range(SPLIT)
        for slot in range(OWN)
    ]
    small = [
        pltpu.make_async_copy(tab_in, tab_ref, small_sem.at[0]),
        pltpu.make_async_copy(map_in, lm_ref, small_sem.at[1]),
        pltpu.make_async_copy(kind_in, kind_ref, small_sem.at[2]),
        pltpu.make_async_copy(th_in, th_ref, small_sem.at[3]),
        pltpu.make_async_copy(rx_in, rx_ref, small_sem.at[4]),
    ]
    copy_k = pltpu.make_async_copy(k_in, kraw, small_sem.at[5])
    for item in columns_in + small[:1]:
        item.start()

    barrier = pltpu.get_barrier_semaphore()
    for step in range(1, SPLIT * SPLIT):
        other = lax.rem(q * SPLIT + m + step, SPLIT * SPLIT)
        pl.semaphore_signal(
            barrier,
            inc=1,
            device_id={"species": other // SPLIT, "mode": lax.rem(other, SPLIT)},
            device_id_type=MESH,
        )

    @pl.when(sx > 0)
    def _():
        pl.semaphore_signal(barrier, inc=1, device_id={"space": sx - 1}, device_id_type=MESH)

    @pl.when(sx < space_count - 1)
    def _():
        pl.semaphore_signal(barrier, inc=1, device_id={"space": sx + 1}, device_id_type=MESH)

    for item in small[1:] + [copy_k]:
        item.start()
    for item in columns_in + small[:1]:
        item.wait()

    def load(slot, rows):
        return jnp.concatenate([f_ref[part, slot, rows, :] for part in range(SPLIT)], axis=1)

    def extract(first, count):
        rows = lax.broadcasted_iota(jnp.int32, (count, OWN * ROWS), 1)
        chosen = jnp.where(tab_ref[first : first + count, 0:1] == rows, 1.0, 0.0).astype(BF16)
        for part in range(SPLIT):
            field = f_ref[part].reshape(OWN * ROWS, LANES).astype(BF16)
            low_send[part, first : first + count, :] = dot(chosen, field).astype(BF16)

    @pl.when(m == 0)
    def _():
        extract(0, HEAD)

    @pl.when(m == 1)
    def _():
        extract(HEAD, PACK - HEAD)

    inner = (sx > 0) & (sx < space_count - 1)
    peers = SPLIT * SPLIT - 1

    @pl.when(inner)
    def _():
        pl.semaphore_wait(barrier, peers + 2)

    @pl.when(jnp.logical_not(inner))
    def _():
        pl.semaphore_wait(barrier, peers + min(1, space_count - 1))

    def scatter(part, piece, first, count):
        return pltpu.make_async_remote_copy(
            src_ref=low_send.at[part, pl.ds(first, count)],
            dst_ref=full.at[q, pl.ds(first, count)],
            send_sem=s1,
            recv_sem=r1.at[q],
            device_id={"species": part, "mode": piece},
            device_id_type=MESH,
        )

    head_last = HEAD - 3 * PIECE

    def head_copies(step):
        part = lax.rem(q + step, SPLIT)
        found = []
        for piece in (3, 1, 2, 0):
            if step == 0 and piece == 0:
                continue
            count = PIECE if piece < 3 else head_last
            found.append(scatter(part, piece, piece * PIECE, count))
        return found

    def tail_copies(step):
        return scatter(lax.rem(q + step, SPLIT), 3, HEAD, PACK - HEAD)

    @pl.when(m == 0)
    def _():
        for step in (1, 2, 3, 0):
            for item in head_copies(step):
                item.start()
        full[q, 0:PIECE, :] = low_send[q, 0:PIECE, :]

    @pl.when(m == 1)
    def _():
        for step in (1, 2, 3, 0):
            tail_copies(step).start()

    for slot in range(OWN):
        halo_send[0, slot] = load(slot, slice(0, 64)).astype(BF16)
        halo_send[1, slot] = load(slot, slice(ROWS - 64, ROWS)).astype(BF16)

    def halo(way):
        return pltpu.make_async_remote_copy(
            src_ref=halo_send.at[way],
            dst_ref=halo_recv.at[1 - way],
            send_sem=hs.at[way],
            recv_sem=hr.at[1 - way],
            device_id={"mode": m - 1 if way == 0 else m + 1},
            device_id_type=MESH,
        )

    @pl.when((m == 1) | (m == 3))
    def _():
        halo(0).start()

    @pl.when(m == 2)
    def _():
        halo(1).start()

    for item in small[1:] + [copy_k]:
        item.wait()

    def lay(n, carry):
        k2[n] = jnp.zeros((PAD_J, NKIND * PAD_J), BF16)

        @pl.when(n < kraw.shape[1])
        def _():
            spot = jnp.minimum(n, kraw.shape[1] - 1)
            for kind in range(NKIND):
                k2[n, 0 : kraw.shape[2], kind * PAD_J : kind * PAD_J + kraw.shape[3]] = kraw[
                    kind, spot
                ]

        return carry

    lax.fori_loop(0, PAD_N, lay, 0)

    lanes = lax.broadcasted_iota(jnp.int32, (8, PAD_J), 1)
    low_count = kraw.shape[2]
    block_rows = kraw.shape[1]
    ordered = jnp.concatenate(
        [lm_ref[...], jnp.full((1, PAD_J - low_count), -2, jnp.int32)], axis=1
    )
    ordered = jnp.broadcast_to(ordered, (8, PAD_J))
    by_block = jnp.full((8, PAD_J), -2, jnp.int32)
    for block in range(SPLIT):
        moved = ordered
        if block > 0:
            moved = pltpu.roll(ordered, block * (PAD_N - block_rows), 1)
        inside = (lanes >= block * PAD_N) & (lanes < block * PAD_N + block_rows)
        by_block = jnp.where(inside, moved, by_block)
    for slot in range(OWN):
        same = tab_ref[:, 1 + slot : 2 + slot] == ordered[0:1, :]
        pick[slot * PAD_J : (slot + 1) * PAD_J, :] = jnp.where(same, 1.0, 0.0).T.astype(BF16)
    mode_of = lax.broadcasted_iota(jnp.int32, (ROWS, PAD_J), 0) + m * ROWS
    spread[...] = jnp.where(mode_of == by_block[0:1, :], 1.0, 0.0).astype(BF16)

    def piece_wait(source):
        pltpu.make_async_remote_copy(
            src_ref=low_send.at[0, pl.ds(0, PIECE)],
            dst_ref=full.at[source, pl.ds(0, PIECE)],
            send_sem=s1,
            recv_sem=r1.at[source],
            device_id={"mode": lax.rem(m + 1, SPLIT)},
            device_id_type=MESH,
        ).wait_recv()

    def forward(half, step):
        rows = pl.ds(pl.multiple_of(m * PIECE, PIECE), PIECE)
        return pltpu.make_async_remote_copy(
            src_ref=full.at[pl.ds(half * 2, 2), rows],
            dst_ref=full.at[pl.ds(half * 2, 2), rows],
            send_sem=s2,
            recv_sem=r2.at[half],
            device_id={"mode": lax.rem(m + step, SPLIT)},
            device_id_type=MESH,
        )

    near = q // 2
    halves = (near, 1 - near)
    for half in halves:
        for spot in range(2):
            source = half * 2 + spot

            @pl.when((m > 0) | (source != q))
            def _():
                piece_wait(source)

        for step in (2, 1, 3):
            forward(half, step).start()

    degree_c = lax.broadcasted_iota(jnp.int32, (NVZ, 1), 0)
    sqrt_c = jnp.sqrt(degree_c.astype(F32))
    sqrt_c_up = jnp.where(degree_c == NVZ - 1, 0.0, jnp.sqrt(degree_c.astype(F32) + 1.0))
    planes = SPLIT * LANES // NY

    def own_terms(i, carry):
        slot = i // PER_VX
        a = lax.rem(i, PER_VX)
        scale = nu_step * th_ref[slot]
        relax = dt_step * rx_ref[slot]
        blocks = [
            load(slot, pl.ds(pl.multiple_of(a * 64 + b * NVZ, NVZ), NVZ)) for b in range(NVY)
        ]
        for b in range(NVY):
            here = blocks[b]
            flux_y = jnp.zeros_like(here)
            if b < NVY - 1:
                flux_y = flux_y + float(np.sqrt(np.float32(b + 1))) * blocks[b + 1]
            if b > 0:
                flux_y = flux_y + float(np.sqrt(np.float32(b))) * blocks[b - 1]
            up_y = 0.5 * flux_y - 0.5 * bound_y * here
            down_y = -0.5 * flux_y - 0.5 * bound_y * here
            turned = []
            for plane in range(planes):
                cut = slice(plane * NY, (plane + 1) * NY)
                turned.append(
                    pltpu.roll(up_y[:, cut], NY - 1, 1) + pltpu.roll(down_y[:, cut], 1, 1)
                )
            y_term = jnp.concatenate(turned, axis=1) + bound_y * here
            flux_z = sqrt_c_up * pltpu.roll(here, NVZ - 1, 0) + sqrt_c * pltpu.roll(here, 1, 0)
            wide = planes * NY
            up_z = 0.5 * flux_z - 0.5 * bound_z * here
            down_z = -0.5 * flux_z - 0.5 * bound_z * here
            z_term = (
                pltpu.roll(up_z, wide - NY, 1) + pltpu.roll(down_z, NY, 1) + bound_z * here
            )
            total = degree_c + (b + a + m * PER_VX)
            lost = jnp.where(total > DEG, relax, 0.0)
            value = here - scale * (y_term + z_term + bound_x * here) - lost * here
            rows = pl.ds(pl.multiple_of(a * 64 + b * NVZ, NVZ), NVZ)
            for part in range(SPLIT):
                out_ref[part, slot, rows, :] = value[:, part * LANES : (part + 1) * LANES]
        return carry

    lax.fori_loop(0, OWN * PER_VX, own_terms, 0)

    def degree_roots(a):
        degree = (m * PER_VX + a).astype(F32)
        below = jnp.sqrt(jnp.full((8, 128), degree, F32))[0:1, 0:1]
        above = jnp.sqrt(jnp.full((8, 128), degree + 1.0, F32))[0:1, 0:1]
        return below, above

    def x_parts(a):
        root, root_up = degree_roots(a)

        def part(i, carry):
            slot = i // 4
            r = lax.rem(i, 4) * 16
            here = load(slot, pl.ds(pl.multiple_of(a * 64 + r, 16), 16))
            flux = jnp.zeros_like(here)
            if a < PER_VX - 1:
                flux = flux + root_up * load(slot, pl.ds(pl.multiple_of((a + 1) * 64 + r, 16), 16))
            if a > 0:
                flux = flux + root * load(slot, pl.ds(pl.multiple_of((a - 1) * 64 + r, 16), 16))
            rows = pl.ds(pl.multiple_of(slot * 64 + r, 16), 16)
            ab_send[0, a, rows, :] = (0.5 * flux - 0.5 * bound_x * here).astype(ab_send.dtype)
            ab_send[1, a, rows, :] = (-0.5 * flux - 0.5 * bound_x * here).astype(ab_send.dtype)
            return carry

        lax.fori_loop(0, OWN * 4, part, 0)

    def layer(way):
        return pltpu.make_async_remote_copy(
            src_ref=ab_send.at[way],
            dst_ref=ab_recv.at[way],
            send_sem=xs.at[way],
            recv_sem=xr.at[way],
            device_id={"space": sx - 1 if way == 0 else sx + 1},
            device_id_type=MESH,
        )

    @pl.when(sx == space_count - 1)
    def _():
        ab_recv[0] = jnp.zeros(ab_recv.shape[1:], ab_recv.dtype)
        edge_recv[0] = jnp.zeros(edge_recv.shape[1:], BF16)

    @pl.when(sx == 0)
    def _():
        ab_recv[1] = jnp.zeros(ab_recv.shape[1:], ab_recv.dtype)
        edge_recv[1] = jnp.zeros(edge_recv.shape[1:], BF16)

    for a in range(PER_VX):
        x_parts(a)

    @pl.when(sx > 0)
    def _():
        layer(0).start()

    @pl.when(sx < space_count - 1)
    def _():
        layer(1).start()

    def forward_wait(half):
        others = full.at[pl.ds(half * 2, 2), pl.ds(0, 3 * PIECE)]
        pltpu.make_async_remote_copy(
            src_ref=others,
            dst_ref=others,
            send_sem=s2,
            recv_sem=r2.at[half],
            device_id={"mode": lax.rem(m + 1, SPLIT)},
            device_id_type=MESH,
        ).wait_recv()

    for half in halves:
        forward_wait(half)
        for spot in range(2):
            source = half * 2 + spot
            picked = dot(pick[...], full[source])
            for slot in range(OWN):
                low[source, :, slot * LANES : (slot + 1) * LANES] = picked[
                    slot * PAD_J : (slot + 1) * PAD_J
                ]

    @pl.when(m < 2)
    def _():
        halo(1).start()

    @pl.when(m == 2)
    def _():
        halo(0).start()

    def of_species(r):
        return low[r // OWN, :, (r % OWN) * LANES : (r % OWN + 1) * LANES]

    everyone = of_species(0)
    for r in range(1, SPLIT * OWN):
        everyone = everyone + of_species(r)
    total[...] = everyone

    def partners(pair):
        def one(slot):
            first = jnp.zeros((PAD_J, LANES), F32)
            for r in range(SPLIT * OWN):
                weight = jnp.where(kind_ref[pair * OWN + slot, r] == 0, 1.0, 0.0)
                first = first + weight * of_species(r)
            cut = slice(slot * LANES, (slot + 1) * LANES)
            pmat[pair, 0:PAD_J, cut] = first.astype(BF16)
            pmat[pair, PAD_J:, cut] = (total[...] - first).astype(BF16)

        for slot in range(OWN):
            one(slot)

    def give(pair, target):
        return pltpu.make_async_remote_copy(
            src_ref=gsend.at[pair],
            dst_ref=grecv.at[q, pl.ds(pl.multiple_of(m * PAD_N, PAD_N), PAD_N)],
            send_sem=s3,
            recv_sem=r3.at[q],
            device_id={"species": pair, "mode": target},
            device_id_type=MESH,
        )

    group = 8

    def collide(pair):
        def some(i, carry):
            left = k2[pl.ds(pl.multiple_of(i * group, group), group)]
            product = dot(left.reshape(group * PAD_J, NKIND * PAD_J), pmat[pair])
            own = low[pair]
            gsum[pl.ds(pl.multiple_of(i * group, group), group), :] = jnp.sum(
                product.reshape(group, PAD_J, OWN * LANES) * own[None], axis=1
            )
            return carry

        lax.fori_loop(0, PAD_N // group, some, 0)
        gsend[pair] = gsum[...].astype(BF16)

    for step in (1, 2, 3, 0):
        pair = lax.rem(q + step, SPLIT)
        partners(pair)
        collide(pair)
        for target in range(2):
            if step > 0:
                give(pair, target).start()
            else:

                @pl.when(m != target)
                def _():
                    give(pair, target).start()

                @pl.when(m == target)
                def _():
                    grecv[q, target * PAD_N : (target + 1) * PAD_N, :] = gsend[pair]

    @pl.when(m > 0)
    def _():
        halo(1).wait_recv()

    @pl.when(m == 0)
    def _():
        halo_recv[0] = jnp.zeros(halo_recv.shape[1:], BF16)

    @pl.when(m < SPLIT - 1)
    def _():
        halo(0).wait_recv()

    @pl.when(m == SPLIT - 1)
    def _():
        halo_recv[1] = jnp.zeros(halo_recv.shape[1:], BF16)

    def edges(way):
        return pltpu.make_async_remote_copy(
            src_ref=halo_recv,
            dst_ref=edge_recv.at[way],
            send_sem=es.at[way],
            recv_sem=er.at[way],
            device_id={"space": sx - 1 if way == 0 else sx + 1},
            device_id_type=MESH,
        )

    @pl.when(sx > 0)
    def _():
        edges(0).start()

    @pl.when(sx < space_count - 1)
    def _():
        edges(1).start()

    @pl.when(sx < space_count - 1)
    def _():
        layer(0).wait_recv()
        edges(0).wait_recv()

    @pl.when(sx > 0)
    def _():
        layer(1).wait_recv()
        edges(1).wait_recv()

    for a in range(PER_VX):
        root, root_up = degree_roots(a)

        def add_x(i, carry):
            slot = i // 4
            r = pl.multiple_of(lax.rem(i, 4) * 16, 16)
            rows = pl.ds(pl.multiple_of(slot * 64 + r, 16), 16)
            here = pl.ds(pl.multiple_of(a * 64 + r, 16), 16)
            term = ab_recv[0, a, rows, :] + ab_recv[1, a, rows, :]
            side = {0: 0, PER_VX - 1: 1}.get(a)
            if side is not None:
                up = edge_recv[0, side, slot, pl.ds(r, 16), :].astype(F32)
                down = edge_recv[1, side, slot, pl.ds(r, 16), :].astype(F32)
                term = term + (0.5 * (root_up if side else root)) * (up - down)
            term = (nu_step * th_ref[slot]) * term
            for part in range(SPLIT):
                out_ref[part, slot, here, :] = (
                    out_ref[part, slot, here, :] - term[:, part * LANES : (part + 1) * LANES]
                )
            return carry

        lax.fori_loop(0, OWN * 4, add_x, 0)

    def column_out(part, slot):
        return pltpu.make_async_copy(
            out_ref.at[part, slot],
            result.at[slot, :, 0, pl.ds(pl.multiple_of(part * LANES, LANES), LANES)],
            copy_sem.at[part, slot],
        )

    @pl.when(m >= 2)
    def _():
        for part in range(SPLIT):
            for slot in range(OWN):
                column_out(part, slot).start()

    @pl.when(m < 2)
    def _():
        for back in (1, 2, 3, 0):
            source = lax.rem(q + SPLIT - back, SPLIT)
            came = grecv.at[source, pl.ds(0, (SPLIT if back else SPLIT - 1) * PAD_N)]
            pltpu.make_async_remote_copy(
                src_ref=came,
                dst_ref=came,
                send_sem=s3,
                recv_sem=r3.at[source],
                device_id={"mode": lax.rem(m + 1, SPLIT)},
                device_id_type=MESH,
            ).wait_recv()
            gained = dot(spread[...], grecv[source])
            for slot in range(OWN):
                out_ref[source, slot] = (
                    out_ref[source, slot] + dt_step * gained[:, slot * LANES : (slot + 1) * LANES]
                )
                column_out(source, slot).start()

    def all_sent(rows, sem):
        pltpu.make_async_remote_copy(
            src_ref=rows,
            dst_ref=rows,
            send_sem=sem,
            recv_sem=r1.at[0],
            device_id={"mode": lax.rem(m + 1, SPLIT)},
            device_id_type=MESH,
        ).wait_send()

    @pl.when(m == 0)
    def _():
        all_sent(low_send.at[:, pl.ds(0, HEAD - PIECE // SPLIT)], s1)

    @pl.when(m == 1)
    def _():
        all_sent(low_send.at[:, pl.ds(0, PACK - HEAD)], s1)

    all_sent(full.at[:, pl.ds(0, 3 * PIECE)], s2)

    @pl.when(m > 0)
    def _():
        halo(0).wait_send()

    @pl.when(m < SPLIT - 1)
    def _():
        halo(1).wait_send()

    @pl.when(sx > 0)
    def _():
        layer(0).wait_send()

    @pl.when(sx < space_count - 1)
    def _():
        layer(1).wait_send()

    @pl.when(sx > 0)
    def _():
        edges(0).wait_send()

    @pl.when(sx < space_count - 1)
    def _():
        edges(1).wait_send()

    @pl.when(m < 2)
    def _():
        all_sent(grecv.at[pl.ds(0, 2), pl.ds(0, 7 * PAD_N // 2)], s3)

    @pl.when(m >= 2)
    def _():
        all_sent(grecv.at[pl.ds(0, 2)], s3)

    for part in range(SPLIT):
        for slot in range(OWN):
            column_out(part, slot).wait()


def write_out(source, result, held, sems):
    count = sems.shape[1]
    rows = result.shape[1] // count

    def move(src, dst, way, piece):
        cut = pl.ds(piece * rows, rows)
        return pltpu.make_async_copy(src.at[:, cut], dst.at[:, cut], sems.at[way, piece])

    for piece in range(count):
        move(source, held, 0, piece).start()
    for piece in range(count):
        move(source, held, 0, piece).wait()
        move(held, result, 1, piece).start()
    for piece in range(count):
        move(held, result, 1, piece).wait()


def per_device(space_count, distribution, kernels, pair_kind, low_map, thermal_speed, relax_rate):
    own, rows, layers, cells = distribution.shape
    assert (own, rows, layers, cells) == (OWN, ROWS, 1, SPLIT * LANES)
    kinds, _, low_count, _ = kernels.shape
    table = jnp.asarray(packed_table())
    anywhere = pl.BlockSpec(memory_space=pl.ANY)
    dma = pltpu.SemaphoreType.DMA
    ab_type = F32
    stepped = pl.pallas_call(
        functools.partial(kernel, space_count),
        out_shape=jax.ShapeDtypeStruct(distribution.shape, F32),
        in_specs=[anywhere] * 7,
        out_specs=anywhere,
        scratch_shapes=[
            pltpu.VMEM((SPLIT, own, rows, LANES), F32),
            pltpu.VMEM((SPLIT, own, rows, LANES), F32),
            pltpu.VMEM(table.shape, jnp.int32),
            pltpu.VMEM((1, low_count), jnp.int32),
            pltpu.SMEM(pair_kind.shape, jnp.int32),
            pltpu.SMEM(thermal_speed.shape, F32),
            pltpu.SMEM(relax_rate.shape, F32),
            pltpu.VMEM(kernels.shape, BF16),
            pltpu.VMEM((PAD_N, PAD_J, kinds * PAD_J), BF16),
            pltpu.VMEM((SPLIT, PACK, LANES), BF16),
            pltpu.VMEM((SPLIT, PACK, LANES), BF16),
            pltpu.VMEM((SPLIT, PAD_J, own * LANES), F32),
            pltpu.VMEM((SPLIT, kinds * PAD_J, own * LANES), BF16),
            pltpu.VMEM((PAD_N, own * LANES), F32),
            pltpu.VMEM((PAD_J, LANES), F32),
            pltpu.VMEM((SPLIT, PAD_N, own * LANES), BF16),
            pltpu.VMEM((SPLIT, SPLIT * PAD_N, own * LANES), BF16),
            pltpu.VMEM((own * PAD_J, PACK), BF16),
            pltpu.VMEM((ROWS, PAD_J), BF16),
            pltpu.VMEM((2, own, 64, cells), BF16),
            pltpu.VMEM((2, own, 64, cells), BF16),
            pltpu.VMEM((2, 2, own, 64, cells), BF16),
            pltpu.VMEM((2, PER_VX, own * 64, cells), ab_type),
            pltpu.VMEM((2, PER_VX, own * 64, cells), ab_type),
            dma((SPLIT, OWN)),
            dma((6,)),
            dma,
            dma((SPLIT,)),
            dma,
            dma((2,)),
            dma,
            dma((SPLIT,)),
            dma((2,)),
            dma((2,)),
            dma((2,)),
            dma((2,)),
            dma((2,)),
            dma((2,)),
        ],
        compiler_params=pltpu.CompilerParams(
            collective_id=0, has_side_effects=True, vmem_limit_bytes=60 * 1024 * 1024
        ),
    )(
        distribution,
        kernels,
        table,
        low_map.reshape(1, low_count),
        pair_kind,
        thermal_speed,
        relax_rate,
    )
    return pl.pallas_call(
        write_out,
        out_shape=jax.ShapeDtypeStruct(distribution.shape, F32),
        in_specs=[anywhere],
        out_specs=anywhere,
        scratch_shapes=[pltpu.VMEM(distribution.shape, F32), dma((2, 4))],
        compiler_params=pltpu.CompilerParams(vmem_limit_bytes=60 * 1024 * 1024),
    )(stepped)


def solution(mesh):
    in_specs = (
        P("species", "mode", "space", None),
        P(None, "mode", None, None),
        P(),
        P(),
        P("species"),
        P("species"),
    )
    out_specs = P("species", "mode", "space", None)
    return jax.shard_map(
        functools.partial(per_device, mesh.shape["space"]),
        mesh=mesh,
        in_specs=in_specs,
        out_specs=out_specs,
        check_vma=False,
    )
```

```python
import functools

import jax
import jax.numpy as jnp
import numpy as np
from jax import lax
from jax.experimental import pallas as pl
from jax.experimental.pallas import tpu as pltpu
from jax.sharding import PartitionSpec as P

MESH = pl.DeviceIdType.MESH
F32 = jnp.float32
BF16 = jnp.bfloat16

NVY = 8
NVZ = 8
DEG = 7
NKIND = 2
NY = 256

nu_step = 0.0625
dt_step = 0.05
bound_x = 6.7
bound_y = 4.2
bound_z = 4.2

SPLIT = 4
OWN = 2
ROWS = 256
PER_VX = 4
LANES = 128
HEAD = 208
PACK = 256
PIECE = 64
PAD_J = 128
PAD_N = 32


def packed_table():
    low = [
        (a * NVY + b) * NVZ + c
        for a in range(DEG + 1)
        for b in range(NVY)
        for c in range(NVZ)
        if a + b + c <= DEG
    ]
    table = np.full((PACK, 8), -1, np.int32)
    for start, first in ((0, 0), (HEAD, ROWS)):
        held = [mode for mode in low if first <= mode < first + ROWS]
        row = start
        for slot in range(OWN):
            for mode in held:
                table[row, 0] = slot * ROWS + mode - first
                table[row, 1 + slot] = mode
                row += 1
        assert row <= (HEAD if start == 0 else PACK)
    return table


def dot(left, right):
    return jnp.dot(left, right, preferred_element_type=F32)


def kernel(
    space_count,
    f_in,
    k_in,
    tab_in,
    map_in,
    kind_in,
    th_in,
    rx_in,
    result,
    f_ref,
    out_ref,
    tab_ref,
    lm_ref,
    kind_ref,
    th_ref,
    rx_ref,
    kraw,
    k2,
    low_send,
    full,
    low,
    pmat,
    gsum,
    total,
    gsend,
    grecv,
    pick,
    spread,
    halo_send,
    halo_recv,
    edge_recv,
    ab_send,
    ab_recv,
    copy_sem,
    small_sem,
    s1,
    r1,
    s2,
    r2,
    s3,
    r3,
    hs,
    hr,
    xs,
    xr,
    es,
    er,
):
    q = lax.axis_index("species")
    m = lax.axis_index("mode")
    sx = lax.axis_index("space")

    columns_in = [
        pltpu.make_async_copy(
            f_in.at[slot, :, 0, pl.ds(part * LANES, LANES)],
            f_ref.at[part, slot],
            copy_sem.at[part, slot],
        )
        for part in range(SPLIT)
        for slot in range(OWN)
    ]
    small = [
        pltpu.make_async_copy(tab_in, tab_ref, small_sem.at[0]),
        pltpu.make_async_copy(map_in, lm_ref, small_sem.at[1]),
        pltpu.make_async_copy(kind_in, kind_ref, small_sem.at[2]),
        pltpu.make_async_copy(th_in, th_ref, small_sem.at[3]),
        pltpu.make_async_copy(rx_in, rx_ref, small_sem.at[4]),
    ]
    copy_k = pltpu.make_async_copy(k_in, kraw, small_sem.at[5])
    for item in columns_in + small[:1]:
        item.start()

    barrier = pltpu.get_barrier_semaphore()
    for step in range(1, SPLIT * SPLIT):
        other = lax.rem(q * SPLIT + m + step, SPLIT * SPLIT)
        pl.semaphore_signal(
            barrier,
            inc=1,
            device_id={"species": other // SPLIT, "mode": lax.rem(other, SPLIT)},
            device_id_type=MESH,
        )

    @pl.when(sx > 0)
    def _():
        pl.semaphore_signal(barrier, inc=1, device_id={"space": sx - 1}, device_id_type=MESH)

    @pl.when(sx < space_count - 1)
    def _():
        pl.semaphore_signal(barrier, inc=1, device_id={"space": sx + 1}, device_id_type=MESH)

    for item in small[1:] + [copy_k]:
        item.start()
    for item in columns_in + small[:1]:
        item.wait()

    def load(slot, rows):
        return jnp.concatenate([f_ref[part, slot, rows, :] for part in range(SPLIT)], axis=1)

    def extract(first, count):
        rows = lax.broadcasted_iota(jnp.int32, (count, OWN * ROWS), 1)
        chosen = jnp.where(tab_ref[first : first + count, 0:1] == rows, 1.0, 0.0).astype(BF16)
        for part in range(SPLIT):
            field = f_ref[part].reshape(OWN * ROWS, LANES).astype(BF16)
            low_send[part, first : first + count, :] = dot(chosen, field).astype(BF16)

    @pl.when(m == 0)
    def _():
        extract(0, HEAD)

    @pl.when(m == 1)
    def _():
        extract(HEAD, PACK - HEAD)

    inner = (sx > 0) & (sx < space_count - 1)
    peers = SPLIT * SPLIT - 1

    @pl.when(inner)
    def _():
        pl.semaphore_wait(barrier, peers + 2)

    @pl.when(jnp.logical_not(inner))
    def _():
        pl.semaphore_wait(barrier, peers + min(1, space_count - 1))

    def scatter(part, piece, first, count):
        return pltpu.make_async_remote_copy(
            src_ref=low_send.at[part, pl.ds(first, count)],
            dst_ref=full.at[q, pl.ds(first, count)],
            send_sem=s1,
            recv_sem=r1.at[q],
            device_id={"species": part, "mode": piece},
            device_id_type=MESH,
        )

    head_last = HEAD - 3 * PIECE

    def head_copies(step):
        part = lax.rem(q + step, SPLIT)
        found = []
        for piece in (3, 1, 2, 0):
            if step == 0 and piece == 0:
                continue
            count = PIECE if piece < 3 else head_last
            found.append(scatter(part, piece, piece * PIECE, count))
        return found

    def tail_copies(step):
        return scatter(lax.rem(q + step, SPLIT), 3, HEAD, PACK - HEAD)

    @pl.when(m == 0)
    def _():
        for step in (1, 2, 3, 0):
            for item in head_copies(step):
                item.start()
        full[q, 0:PIECE, :] = low_send[q, 0:PIECE, :]

    @pl.when(m == 1)
    def _():
        for step in (1, 2, 3, 0):
            tail_copies(step).start()

    for slot in range(OWN):
        halo_send[0, slot] = load(slot, slice(0, 64)).astype(BF16)
        halo_send[1, slot] = load(slot, slice(ROWS - 64, ROWS)).astype(BF16)

    def halo(way):
        return pltpu.make_async_remote_copy(
            src_ref=halo_send.at[way],
            dst_ref=halo_recv.at[1 - way],
            send_sem=hs.at[way],
            recv_sem=hr.at[1 - way],
            device_id={"mode": m - 1 if way == 0 else m + 1},
            device_id_type=MESH,
        )

    @pl.when((m == 1) | (m == 3))
    def _():
        halo(0).start()

    @pl.when(m == 2)
    def _():
        halo(1).start()

    for item in small[1:] + [copy_k]:
        item.wait()

    def lay(n, carry):
        k2[n] = jnp.zeros((PAD_J, NKIND * PAD_J), BF16)

        @pl.when(n < kraw.shape[1])
        def _():
            spot = jnp.minimum(n, kraw.shape[1] - 1)
            for kind in range(NKIND):
                k2[n, 0 : kraw.shape[2], kind * PAD_J : kind * PAD_J + kraw.shape[3]] = kraw[
                    kind, spot
                ]

        return carry

    lax.fori_loop(0, PAD_N, lay, 0)

    lanes = lax.broadcasted_iota(jnp.int32, (8, PAD_J), 1)
    low_count = kraw.shape[2]
    block_rows = kraw.shape[1]
    ordered = jnp.concatenate(
        [lm_ref[...], jnp.full((1, PAD_J - low_count), -2, jnp.int32)], axis=1
    )
    ordered = jnp.broadcast_to(ordered, (8, PAD_J))
    by_block = jnp.full((8, PAD_J), -2, jnp.int32)
    for block in range(SPLIT):
        moved = ordered
        if block > 0:
            moved = pltpu.roll(ordered, block * (PAD_N - block_rows), 1)
        inside = (lanes >= block * PAD_N) & (lanes < block * PAD_N + block_rows)
        by_block = jnp.where(inside, moved, by_block)
    for slot in range(OWN):
        same = tab_ref[:, 1 + slot : 2 + slot] == ordered[0:1, :]
        pick[slot * PAD_J : (slot + 1) * PAD_J, :] = jnp.where(same, 1.0, 0.0).T.astype(BF16)
    mode_of = lax.broadcasted_iota(jnp.int32, (ROWS, PAD_J), 0) + m * ROWS
    spread[...] = jnp.where(mode_of == by_block[0:1, :], 1.0, 0.0).astype(BF16)

    def piece_wait(source):
        pltpu.make_async_remote_copy(
            src_ref=low_send.at[0, pl.ds(0, PIECE)],
            dst_ref=full.at[source, pl.ds(0, PIECE)],
            send_sem=s1,
            recv_sem=r1.at[source],
            device_id={"mode": lax.rem(m + 1, SPLIT)},
            device_id_type=MESH,
        ).wait_recv()

    def forward(half, step):
        rows = pl.ds(pl.multiple_of(m * PIECE, PIECE), PIECE)
        return pltpu.make_async_remote_copy(
            src_ref=full.at[pl.ds(half * 2, 2), rows],
            dst_ref=full.at[pl.ds(half * 2, 2), rows],
            send_sem=s2,
            recv_sem=r2.at[half],
            device_id={"mode": lax.rem(m + step, SPLIT)},
            device_id_type=MESH,
        )

    near = q // 2
    halves = (near, 1 - near)
    for half in halves:
        for spot in range(2):
            source = half * 2 + spot

            @pl.when((m > 0) | (source != q))
            def _():
                piece_wait(source)

        for step in (2, 1, 3):
            forward(half, step).start()

    degree_c = lax.broadcasted_iota(jnp.int32, (NVZ, 1), 0)
    sqrt_c = jnp.sqrt(degree_c.astype(F32))
    sqrt_c_up = jnp.where(degree_c == NVZ - 1, 0.0, jnp.sqrt(degree_c.astype(F32) + 1.0))
    planes = SPLIT * LANES // NY

    def own_terms(i, carry):
        slot = i // PER_VX
        a = lax.rem(i, PER_VX)
        scale = nu_step * th_ref[slot]
        relax = dt_step * rx_ref[slot]
        blocks = [
            load(slot, pl.ds(pl.multiple_of(a * 64 + b * NVZ, NVZ), NVZ)) for b in range(NVY)
        ]
        for b in range(NVY):
            here = blocks[b]
            flux_y = jnp.zeros_like(here)
            if b < NVY - 1:
                flux_y = flux_y + float(np.sqrt(np.float32(b + 1))) * blocks[b + 1]
            if b > 0:
                flux_y = flux_y + float(np.sqrt(np.float32(b))) * blocks[b - 1]
            up_y = 0.5 * flux_y - 0.5 * bound_y * here
            down_y = -0.5 * flux_y - 0.5 * bound_y * here
            turned = []
            for plane in range(planes):
                cut = slice(plane * NY, (plane + 1) * NY)
                turned.append(
                    pltpu.roll(up_y[:, cut], NY - 1, 1) + pltpu.roll(down_y[:, cut], 1, 1)
                )
            y_term = jnp.concatenate(turned, axis=1) + bound_y * here
            flux_z = sqrt_c_up * pltpu.roll(here, NVZ - 1, 0) + sqrt_c * pltpu.roll(here, 1, 0)
            wide = planes * NY
            up_z = 0.5 * flux_z - 0.5 * bound_z * here
            down_z = -0.5 * flux_z - 0.5 * bound_z * here
            z_term = (
                pltpu.roll(up_z, wide - NY, 1) + pltpu.roll(down_z, NY, 1) + bound_z * here
            )
            total = degree_c + (b + a + m * PER_VX)
            lost = jnp.where(total > DEG, relax, 0.0)
            value = here - scale * (y_term + z_term + bound_x * here) - lost * here
            rows = pl.ds(pl.multiple_of(a * 64 + b * NVZ, NVZ), NVZ)
            for part in range(SPLIT):
                out_ref[part, slot, rows, :] = value[:, part * LANES : (part + 1) * LANES]
        return carry

    lax.fori_loop(0, OWN * PER_VX, own_terms, 0)

    def degree_roots(a):
        degree = (m * PER_VX + a).astype(F32)
        below = jnp.sqrt(jnp.full((8, 128), degree, F32))[0:1, 0:1]
        above = jnp.sqrt(jnp.full((8, 128), degree + 1.0, F32))[0:1, 0:1]
        return below, above

    def x_parts(a):
        root, root_up = degree_roots(a)

        def part(i, carry):
            slot = i // 4
            r = lax.rem(i, 4) * 16
            here = load(slot, pl.ds(pl.multiple_of(a * 64 + r, 16), 16))
            flux = jnp.zeros_like(here)
            if a < PER_VX - 1:
                flux = flux + root_up * load(slot, pl.ds(pl.multiple_of((a + 1) * 64 + r, 16), 16))
            if a > 0:
                flux = flux + root * load(slot, pl.ds(pl.multiple_of((a - 1) * 64 + r, 16), 16))
            rows = pl.ds(pl.multiple_of(slot * 64 + r, 16), 16)
            ab_send[0, a, rows, :] = (0.5 * flux - 0.5 * bound_x * here).astype(ab_send.dtype)
            ab_send[1, a, rows, :] = (-0.5 * flux - 0.5 * bound_x * here).astype(ab_send.dtype)
            return carry

        lax.fori_loop(0, OWN * 4, part, 0)

    def layer(way):
        return pltpu.make_async_remote_copy(
            src_ref=ab_send.at[way],
            dst_ref=ab_recv.at[way],
            send_sem=xs.at[way],
            recv_sem=xr.at[way],
            device_id={"space": sx - 1 if way == 0 else sx + 1},
            device_id_type=MESH,
        )

    @pl.when(sx == space_count - 1)
    def _():
        ab_recv[0] = jnp.zeros(ab_recv.shape[1:], ab_recv.dtype)
        edge_recv[0] = jnp.zeros(edge_recv.shape[1:], BF16)

    @pl.when(sx == 0)
    def _():
        ab_recv[1] = jnp.zeros(ab_recv.shape[1:], ab_recv.dtype)
        edge_recv[1] = jnp.zeros(edge_recv.shape[1:], BF16)

    for a in range(PER_VX):
        x_parts(a)

    def forward_wait(half):
        others = full.at[pl.ds(half * 2, 2), pl.ds(0, 3 * PIECE)]
        pltpu.make_async_remote_copy(
            src_ref=others,
            dst_ref=others,
            send_sem=s2,
            recv_sem=r2.at[half],
            device_id={"mode": lax.rem(m + 1, SPLIT)},
            device_id_type=MESH,
        ).wait_recv()

    for half in halves:
        forward_wait(half)
        for spot in range(2):
            source = half * 2 + spot
            picked = dot(pick[...], full[source])
            for slot in range(OWN):
                low[source, :, slot * LANES : (slot + 1) * LANES] = picked[
                    slot * PAD_J : (slot + 1) * PAD_J
                ]

    @pl.when(m < 2)
    def _():
        halo(1).start()

    @pl.when(m == 2)
    def _():
        halo(0).start()

    @pl.when(sx > 0)
    def _():
        layer(0).start()

    @pl.when(sx < space_count - 1)
    def _():
        layer(1).start()

    def of_species(r):
        return low[r // OWN, :, (r % OWN) * LANES : (r % OWN + 1) * LANES]

    everyone = of_species(0)
    for r in range(1, SPLIT * OWN):
        everyone = everyone + of_species(r)
    total[...] = everyone

    def partners(pair):
        def one(slot):
            first = jnp.zeros((PAD_J, LANES), F32)
            for r in range(SPLIT * OWN):
                weight = jnp.where(kind_ref[pair * OWN + slot, r] == 0, 1.0, 0.0)
                first = first + weight * of_species(r)
            cut = slice(slot * LANES, (slot + 1) * LANES)
            pmat[pair, 0:PAD_J, cut] = first.astype(BF16)
            pmat[pair, PAD_J:, cut] = (total[...] - first).astype(BF16)

        for slot in range(OWN):
            one(slot)

    def give(pair, target):
        return pltpu.make_async_remote_copy(
            src_ref=gsend.at[pair],
            dst_ref=grecv.at[q, pl.ds(pl.multiple_of(m * PAD_N, PAD_N), PAD_N)],
            send_sem=s3,
            recv_sem=r3.at[q],
            device_id={"species": pair, "mode": target},
            device_id_type=MESH,
        )

    group = 8

    def collide(pair):
        def some(i, carry):
            left = k2[pl.ds(pl.multiple_of(i * group, group), group)]
            product = dot(left.reshape(group * PAD_J, NKIND * PAD_J), pmat[pair])
            own = low[pair]
            gsum[pl.ds(pl.multiple_of(i * group, group), group), :] = jnp.sum(
                product.reshape(group, PAD_J, OWN * LANES) * own[None], axis=1
            )
            return carry

        lax.fori_loop(0, PAD_N // group, some, 0)
        gsend[pair] = gsum[...].astype(BF16)

    for step in (1, 2, 3, 0):
        pair = lax.rem(q + step, SPLIT)
        partners(pair)
        collide(pair)
        for target in range(2):
            if step > 0:
                give(pair, target).start()
            else:

                @pl.when(m != target)
                def _():
                    give(pair, target).start()

                @pl.when(m == target)
                def _():
                    grecv[q, target * PAD_N : (target + 1) * PAD_N, :] = gsend[pair]

    @pl.when(m > 0)
    def _():
        halo(1).wait_recv()

    @pl.when(m == 0)
    def _():
        halo_recv[0] = jnp.zeros(halo_recv.shape[1:], BF16)

    @pl.when(m < SPLIT - 1)
    def _():
        halo(0).wait_recv()

    @pl.when(m == SPLIT - 1)
    def _():
        halo_recv[1] = jnp.zeros(halo_recv.shape[1:], BF16)

    def edges(way):
        return pltpu.make_async_remote_copy(
            src_ref=halo_recv,
            dst_ref=edge_recv.at[way],
            send_sem=es.at[way],
            recv_sem=er.at[way],
            device_id={"space": sx - 1 if way == 0 else sx + 1},
            device_id_type=MESH,
        )

    @pl.when(sx > 0)
    def _():
        edges(0).start()

    @pl.when(sx < space_count - 1)
    def _():
        edges(1).start()

    @pl.when(sx < space_count - 1)
    def _():
        layer(0).wait_recv()
        edges(0).wait_recv()

    @pl.when(sx > 0)
    def _():
        layer(1).wait_recv()
        edges(1).wait_recv()

    for a in range(PER_VX):
        root, root_up = degree_roots(a)

        def add_x(i, carry):
            slot = i // 4
            r = pl.multiple_of(lax.rem(i, 4) * 16, 16)
            rows = pl.ds(pl.multiple_of(slot * 64 + r, 16), 16)
            here = pl.ds(pl.multiple_of(a * 64 + r, 16), 16)
            term = ab_recv[0, a, rows, :] + ab_recv[1, a, rows, :]
            side = {0: 0, PER_VX - 1: 1}.get(a)
            if side is not None:
                up = edge_recv[0, side, slot, pl.ds(r, 16), :].astype(F32)
                down = edge_recv[1, side, slot, pl.ds(r, 16), :].astype(F32)
                term = term + (0.5 * (root_up if side else root)) * (up - down)
            term = (nu_step * th_ref[slot]) * term
            for part in range(SPLIT):
                out_ref[part, slot, here, :] = (
                    out_ref[part, slot, here, :] - term[:, part * LANES : (part + 1) * LANES]
                )
            return carry

        lax.fori_loop(0, OWN * 4, add_x, 0)

    def column_out(part, slot):
        return pltpu.make_async_copy(
            out_ref.at[part, slot],
            result.at[slot, :, 0, pl.ds(pl.multiple_of(part * LANES, LANES), LANES)],
            copy_sem.at[part, slot],
        )

    @pl.when(m >= 2)
    def _():
        for part in range(SPLIT):
            for slot in range(OWN):
                column_out(part, slot).start()

    @pl.when(m < 2)
    def _():
        for back in (1, 2, 3, 0):
            source = lax.rem(q + SPLIT - back, SPLIT)
            came = grecv.at[source, pl.ds(0, (SPLIT if back else SPLIT - 1) * PAD_N)]
            pltpu.make_async_remote_copy(
                src_ref=came,
                dst_ref=came,
                send_sem=s3,
                recv_sem=r3.at[source],
                device_id={"mode": lax.rem(m + 1, SPLIT)},
                device_id_type=MESH,
            ).wait_recv()
            gained = dot(spread[...], grecv[source])
            for slot in range(OWN):
                out_ref[source, slot] = (
                    out_ref[source, slot] + dt_step * gained[:, slot * LANES : (slot + 1) * LANES]
                )
                column_out(source, slot).start()

    def all_sent(rows, sem):
        pltpu.make_async_remote_copy(
            src_ref=rows,
            dst_ref=rows,
            send_sem=sem,
            recv_sem=r1.at[0],
            device_id={"mode": lax.rem(m + 1, SPLIT)},
            device_id_type=MESH,
        ).wait_send()

    @pl.when(m == 0)
    def _():
        all_sent(low_send.at[:, pl.ds(0, HEAD - PIECE // SPLIT)], s1)

    @pl.when(m == 1)
    def _():
        all_sent(low_send.at[:, pl.ds(0, PACK - HEAD)], s1)

    all_sent(full.at[:, pl.ds(0, 3 * PIECE)], s2)

    @pl.when(m > 0)
    def _():
        halo(0).wait_send()

    @pl.when(m < SPLIT - 1)
    def _():
        halo(1).wait_send()

    @pl.when(sx > 0)
    def _():
        layer(0).wait_send()

    @pl.when(sx < space_count - 1)
    def _():
        layer(1).wait_send()

    @pl.when(sx > 0)
    def _():
        edges(0).wait_send()

    @pl.when(sx < space_count - 1)
    def _():
        edges(1).wait_send()

    @pl.when(m < 2)
    def _():
        all_sent(grecv.at[pl.ds(0, 2), pl.ds(0, 7 * PAD_N // 2)], s3)

    @pl.when(m >= 2)
    def _():
        all_sent(grecv.at[pl.ds(0, 2)], s3)

    for part in range(SPLIT):
        for slot in range(OWN):
            column_out(part, slot).wait()


def write_out(source, result, held, sems):
    count = sems.shape[1]
    rows = result.shape[1] // count

    def move(src, dst, way, piece):
        cut = pl.ds(piece * rows, rows)
        return pltpu.make_async_copy(src.at[:, cut], dst.at[:, cut], sems.at[way, piece])

    for piece in range(count):
        move(source, held, 0, piece).start()
    for piece in range(count):
        move(source, held, 0, piece).wait()
        move(held, result, 1, piece).start()
    for piece in range(count):
        move(held, result, 1, piece).wait()


def per_device(space_count, distribution, kernels, pair_kind, low_map, thermal_speed, relax_rate):
    own, rows, layers, cells = distribution.shape
    assert (own, rows, layers, cells) == (OWN, ROWS, 1, SPLIT * LANES)
    kinds, _, low_count, _ = kernels.shape
    table = jnp.asarray(packed_table())
    anywhere = pl.BlockSpec(memory_space=pl.ANY)
    dma = pltpu.SemaphoreType.DMA
    ab_type = F32
    stepped = pl.pallas_call(
        functools.partial(kernel, space_count),
        out_shape=jax.ShapeDtypeStruct(distribution.shape, F32),
        in_specs=[anywhere] * 7,
        out_specs=anywhere,
        scratch_shapes=[
            pltpu.VMEM((SPLIT, own, rows, LANES), F32),
            pltpu.VMEM((SPLIT, own, rows, LANES), F32),
            pltpu.VMEM(table.shape, jnp.int32),
            pltpu.VMEM((1, low_count), jnp.int32),
            pltpu.SMEM(pair_kind.shape, jnp.int32),
            pltpu.SMEM(thermal_speed.shape, F32),
            pltpu.SMEM(relax_rate.shape, F32),
            pltpu.VMEM(kernels.shape, BF16),
            pltpu.VMEM((PAD_N, PAD_J, kinds * PAD_J), BF16),
            pltpu.VMEM((SPLIT, PACK, LANES), BF16),
            pltpu.VMEM((SPLIT, PACK, LANES), BF16),
            pltpu.VMEM((SPLIT, PAD_J, own * LANES), F32),
            pltpu.VMEM((SPLIT, kinds * PAD_J, own * LANES), BF16),
            pltpu.VMEM((PAD_N, own * LANES), F32),
            pltpu.VMEM((PAD_J, LANES), F32),
            pltpu.VMEM((SPLIT, PAD_N, own * LANES), BF16),
            pltpu.VMEM((SPLIT, SPLIT * PAD_N, own * LANES), BF16),
            pltpu.VMEM((own * PAD_J, PACK), BF16),
            pltpu.VMEM((ROWS, PAD_J), BF16),
            pltpu.VMEM((2, own, 64, cells), BF16),
            pltpu.VMEM((2, own, 64, cells), BF16),
            pltpu.VMEM((2, 2, own, 64, cells), BF16),
            pltpu.VMEM((2, PER_VX, own * 64, cells), ab_type),
            pltpu.VMEM((2, PER_VX, own * 64, cells), ab_type),
            dma((SPLIT, OWN)),
            dma((6,)),
            dma,
            dma((SPLIT,)),
            dma,
            dma((2,)),
            dma,
            dma((SPLIT,)),
            dma((2,)),
            dma((2,)),
            dma((2,)),
            dma((2,)),
            dma((2,)),
            dma((2,)),
        ],
        compiler_params=pltpu.CompilerParams(
            collective_id=0, has_side_effects=True, vmem_limit_bytes=60 * 1024 * 1024
        ),
    )(
        distribution,
        kernels,
        table,
        low_map.reshape(1, low_count),
        pair_kind,
        thermal_speed,
        relax_rate,
    )
    return pl.pallas_call(
        write_out,
        out_shape=jax.ShapeDtypeStruct(distribution.shape, F32),
        in_specs=[anywhere],
        out_specs=anywhere,
        scratch_shapes=[pltpu.VMEM(distribution.shape, F32), dma((2, 4))],
        compiler_params=pltpu.CompilerParams(vmem_limit_bytes=60 * 1024 * 1024),
    )(stepped)


def solution(mesh):
    in_specs = (
        P("species", "mode", "space", None),
        P(None, "mode", None, None),
        P(),
        P(),
        P("species"),
        P("species"),
    )
    out_specs = P("species", "mode", "space", None)
    return jax.shard_map(
        functools.partial(per_device, mesh.shape["space"]),
        mesh=mesh,
        in_specs=in_specs,
        out_specs=out_specs,
        check_vma=False,
    )
```
